32 devices in a mesh: seq: 4 (over z), head: 4 (over y, x), rep: 2 (over core).
Axes of the slice: x: 2, y: 2, z: 4, core: 2. Of those that a mesh axis runs over, the one named last changes fastest.
Arguments:
- queries: bfloat16 [64, 64, 128], P(('seq', 'head', 'rep'))
- prefix_keys: bfloat16 [16384, 4, 128], P(('seq', 'rep'), 'head')
- prefix_values: bfloat16 [16384, 4, 128], P(('seq', 'rep'), 'head'), may hold values from -6 to 6
- suffix_keys: bfloat16 [64, 2048, 4, 128], P(('seq', 'head', 'rep')), may hold values from -8.375 to 8.375
- suffix_values: bfloat16 [64, 2048, 4, 128], P(('seq', 'head', 'rep')), may hold values from -6 to 6
- suffix_lengths: int32 [64], P(('seq', 'head', 'rep')), may hold values from 256 to 2048, as said below
- slot_map: int32 [64], P(('seq', 'head', 'rep')), may hold values from 0 to 63, as said below
Outputs:
- attention: float32 [64, 64, 128], P(('seq', 'head', 'rep'))
- log_total: float32 [64, 64], P(('seq', 'head', 'rep'))
The draws below stay inside these ranges and needn't reach their ends.
Inputs may be any that keep to these rules, and one draw needn't show every extreme that they name: `suffix_lengths`: every request has at least 256 live suffix positions, and some request has exactly 2048. slot_map is a permutation of the slots that keeps each aligned block of 2 requests in the block of 2 slots with the same indices.
All inputs are finite; a program needn't handle non-finite values.
Results may differ from the reference program's by a relative error of at most 0.00099.
Values may be sent and summed in bfloat16 or wider, within the bound.
No kernel may reach another device: no remote copies, remote signals or barrier semaphores. Data moves between devices by JAX's collectives and lax.ppermute only.
A program may use at most 64 MiB of HBM per device.

```python
import jax
import jax.numpy as jnp
from jax import lax

QH = 64
KVH = 4
HD = 128
REQ_DEV = 2
PRE_DEV = 2048
SUF = 2048
REQUESTS = 64
PREFIX = 16384
N_SEQ = 4
N_REP = 2


def draw_queries(key, part):
    key = jax.random.fold_in(key, 11)
    result = jnp.clip(2.5 * jax.random.normal(key, (REQUESTS, QH, HD), jnp.float32), -8.0, 8.0)
    return result.astype(jnp.bfloat16)


def draw_prefix_keys(key, part):
    key = jax.random.fold_in(key, 12)
    result = jnp.clip(jax.random.normal(key, (PREFIX, KVH, HD), jnp.float32), -6.0, 6.0)
    return result.astype(jnp.bfloat16)


def draw_suffix_lengths(key, part):
    key = jax.random.fold_in(key, 13)
    lengths = jax.random.randint(key, (REQUESTS,), SUF // 8, SUF + 1)
    chosen = jax.random.randint(jax.random.fold_in(key, 1), (), 0, REQUESTS)
    return jnp.where(jnp.arange(REQUESTS) == chosen, SUF, lengths).astype(jnp.int32)


def draw_slot_map(key, part):
    key = jax.random.fold_in(key, 14)
    block_count = REQUESTS // REQ_DEV
    block_keys = jax.random.split(key, block_count)

    def permute_block(block_key):
        return jax.random.permutation(block_key, REQ_DEV)
    perms = jax.vmap(permute_block)(block_keys)
    slots = perms + jnp.arange(block_count)[:, None] * REQ_DEV
    return slots.reshape(-1).astype(jnp.int32)


def levels(own_key, dims, pieces, low, top_value):
    level, own = 1.0, jax.random.fold_in(own_key, 6)
    for dim, shards_of in pieces:
        heights = jnp.exp(jax.random.uniform(jax.random.fold_in(own, dim), (shards_of,), jnp.float32, low / len(pieces), top_value / len(pieces)))
        level = level * jnp.repeat(heights, dims[dim] // shards_of).reshape([-1 if axis == dim else 1 for axis in range(len(dims))])
    return level


def bell_draw(key, dims, deviation, most, cuts=(), kind=jnp.bfloat16):
    entries = jax.random.normal(key, dims, jnp.float32) * deviation
    if len(cuts) > 0:
        entries = levels(key, dims, cuts, -0.22, 0.18) * entries
    return jnp.clip(entries, min=-most, max=most).astype(kind)


def setup_inputs(seed: int = 0) -> dict:
    seeds = jax.random.split(jax.random.key(seed), 8)
    queries = draw_queries(jax.random.fold_in(seeds[7], 71), 0)
    prefix_keys = draw_prefix_keys(jax.random.fold_in(seeds[7], 71), 0)
    prefix_values = bell_draw(seeds[2], (PREFIX, KVH, HD), 1.0, 6.0, ((0, 8), (1, 4)))
    suffix_keys = bell_draw(seeds[3], (REQUESTS, SUF, KVH, HD), 1.4, 8.375, ((0, 32),))
    suffix_values = bell_draw(seeds[4], (REQUESTS, SUF, KVH, HD), 1.0, 6.0, ((0, 32),))
    suffix_lengths = draw_suffix_lengths(jax.random.fold_in(seeds[7], 71), 0)
    slot_map = draw_slot_map(jax.random.fold_in(seeds[7], 71), 0)
    return {"queries": queries, "prefix_keys": prefix_keys, "prefix_values": prefix_values, "suffix_keys": suffix_keys, "suffix_values": suffix_values, "suffix_lengths": suffix_lengths, "slot_map": slot_map}


def suffix_partial(query_row, slot_index, live_count, suffix_keys, suffix_values, score_scale):
    keys_row = lax.dynamic_index_in_dim(suffix_keys, slot_index, 0, keepdims=False).astype(jnp.float32)
    values_row = lax.dynamic_index_in_dim(suffix_values, slot_index, 0, keepdims=False).astype(jnp.float32)
    scores = jnp.einsum("ghd,sgd->ghs", query_row, keys_row, precision=lax.Precision.HIGHEST) * score_scale
    live_mask = jnp.arange(SUF, dtype=jnp.int32)[None, None, :] < live_count
    scores = jnp.where(live_mask, scores, -1e30)
    row_max = jnp.max(scores, axis=-1)
    exp_terms = jnp.where(live_mask, jnp.exp(scores - row_max[..., None]), 0.0)
    row_total = jnp.sum(exp_terms, axis=-1)
    weights = exp_terms.astype(jnp.bfloat16).astype(jnp.float32)
    mixed = jnp.einsum("ghs,sgd->ghd", weights, values_row, precision=lax.Precision.HIGHEST) / row_total[..., None]
    return mixed, row_max + jnp.log(row_total)


def reference(queries, prefix_keys, prefix_values, suffix_keys, suffix_values, suffix_lengths, slot_map):
    group_size = QH // KVH
    score_scale = HD ** -0.5
    grouped = queries.astype(jnp.float32).reshape(REQUESTS, KVH, group_size, HD)

    def one_request(items):
        return suffix_partial(items[0], items[1], items[2], suffix_keys, suffix_values, score_scale)

    suf_mixed, suf_log = lax.map(one_request, (grouped, slot_map, suffix_lengths))

    def one_block(carry, block_index):
        run_max, run_total, run_acc = carry
        begin = block_index * PRE_DEV
        keys_blk = lax.dynamic_slice_in_dim(prefix_keys, begin, PRE_DEV, 0).astype(jnp.float32)
        values_blk = lax.dynamic_slice_in_dim(prefix_values, begin, PRE_DEV, 0).astype(jnp.float32)
        mixed_list = []
        log_list = []
        for head_kv in range(KVH):
            rows = grouped[:, head_kv].reshape(REQUESTS * group_size, HD)
            scores = jnp.dot(rows, keys_blk[:, head_kv].T, precision=lax.Precision.HIGHEST) * score_scale
            row_max = jnp.max(scores, axis=1, keepdims=True)
            exp_terms = jnp.exp(scores - row_max)
            row_total = jnp.sum(exp_terms, axis=1, keepdims=True)
            weights = exp_terms.astype(jnp.bfloat16).astype(jnp.float32)
            mixed = jnp.dot(weights, values_blk[:, head_kv], precision=lax.Precision.HIGHEST) / row_total
            mixed_list.append(mixed.reshape(REQUESTS, group_size, HD))
            log_list.append((row_max + jnp.log(row_total)).reshape(REQUESTS, group_size))
        block_mixed = jnp.stack(mixed_list, axis=1)
        block_log = jnp.stack(log_list, axis=1)
        new_max = jnp.maximum(run_max, block_log)
        fold_old = jnp.exp(run_max - new_max)
        fold_new = jnp.exp(block_log - new_max)
        run_total = run_total * fold_old + fold_new
        run_acc = run_acc * fold_old[..., None] + fold_new[..., None] * block_mixed
        return (new_max, run_total, run_acc), None

    start_carry = (suf_log, jnp.ones_like(suf_log), suf_mixed)
    block_ids = jnp.arange(N_SEQ * N_REP, dtype=jnp.int32)
    (run_max, run_total, run_acc), _ = lax.scan(one_block, start_carry, block_ids)
    attention = (run_acc / run_total[..., None]).reshape(REQUESTS, QH, HD)
    log_total = (run_max + jnp.log(run_total)).reshape(REQUESTS, QH)
    return attention, log_total
```

```python
import functools
import math

import jax
import jax.numpy as jnp
from jax import lax
from jax.experimental import pallas as pl
from jax.experimental.pallas import tpu as pltpu
from jax.sharding import PartitionSpec as P

ROW_TILE = 128
STEP_ROWS = 512
SUF_CHUNK = 1024
LOG_ROWS = 8
NT = (((1,), (1,)), ((), ()))
VMEM_BYTES = 48 * 1024 * 1024


def suffix_kernel(
    slot_ref, length_ref, q_ref, k_ref, v_ref, mixed_ref, log_ref, score_ref, *, kv_count, score_scale
):
    heads, width = q_ref.shape[1], q_ref.shape[2]
    rows = k_ref.shape[1]
    limit = length_ref[pl.program_id(0)] * kv_count
    query = q_ref[0]
    lane = lax.broadcasted_iota(jnp.int32, (heads, SUF_CHUNK), 1)
    group = lax.broadcasted_iota(jnp.int32, (heads, SUF_CHUNK), 0) // (heads // kv_count)
    own_head = (lane % kv_count) == group
    peak = jnp.full((heads, SUF_CHUNK), -1e30, jnp.float32)
    for begin in range(0, rows, SUF_CHUNK):
        part = lax.dot_general(
            query, k_ref[0, begin : begin + SUF_CHUNK], NT, preferred_element_type=jnp.float32
        )
        part = jnp.where(own_head & (lane < limit - begin), part, -1e30)
        score_ref[:, begin : begin + SUF_CHUNK] = part
        peak = jnp.maximum(peak, part)
    row_max = jnp.max(peak, axis=1, keepdims=True)
    sums = jnp.zeros((heads, SUF_CHUNK), jnp.float32)
    acc = jnp.zeros((heads, width), jnp.float32)
    for begin in range(0, rows, SUF_CHUNK):
        terms = jnp.exp((score_ref[:, begin : begin + SUF_CHUNK] - row_max) * score_scale)
        sums = sums + terms
        acc = acc + jnp.dot(
            terms.astype(jnp.bfloat16),
            v_ref[0, begin : begin + SUF_CHUNK],
            preferred_element_type=jnp.float32,
        )
    total = jnp.sum(sums, axis=1, keepdims=True)
    mixed_ref[0] = acc / total
    log_ref[0] = jnp.broadcast_to(row_max * score_scale + jnp.log(total), (heads, width))


def suffix_partials(queries, keys, values, lengths, slots, score_scale):
    count, heads, width = queries.shape
    kv_count = keys.shape[2]
    rows = keys.shape[1] * kv_count
    keys = keys.reshape(count, rows, width)
    values = values.reshape(count, rows, width)

    def by_slot(i, slot_ref, length_ref):
        return (lax.rem(slot_ref[i], count), 0, 0)

    def by_request(i, slot_ref, length_ref):
        return (i, 0, 0)

    return pl.pallas_call(
        functools.partial(suffix_kernel, kv_count=kv_count, score_scale=score_scale),
        grid_spec=pltpu.PrefetchScalarGridSpec(
            num_scalar_prefetch=2,
            grid=(count,),
            in_specs=[
                pl.BlockSpec((1, heads, width), by_request),
                pl.BlockSpec((1, rows, width), by_slot),
                pl.BlockSpec((1, rows, width), by_slot),
            ],
            out_specs=[
                pl.BlockSpec((1, heads, width), by_request),
                pl.BlockSpec((1, heads, width), by_request),
            ],
            scratch_shapes=[pltpu.VMEM((heads, rows), jnp.float32)],
        ),
        out_shape=[jax.ShapeDtypeStruct((count, heads, width), jnp.float32)] * 2,
        compiler_params=pltpu.CompilerParams(vmem_limit_bytes=VMEM_BYTES),
        cost_estimate=pl.CostEstimate(
            flops=4 * count * heads * rows * width,
            bytes_accessed=4 * count * rows * width,
            transcendentals=count * heads * rows,
        ),
        name="suffix_attention",
    )(slots, lengths, queries, keys, values)


def prefix_kernel(q_ref, k0_ref, v0_ref, k1_ref, v1_ref, out_ref, score_ref, *, per_dest, score_scale):
    width = q_ref.shape[1]
    tiles = q_ref.shape[0] // ROW_TILE
    dests = ROW_TILE // per_dest
    keys, values = (k0_ref, k1_ref), (v0_ref, v1_ref)
    units = [(tile, block) for tile in range(tiles) for block in range(2)]
    lane = lax.broadcasted_iota(jnp.int32, (per_dest, width), 1)
    row = lax.broadcasted_iota(jnp.int32, (per_dest, width), 0)
    diagonal = lane == row

    def score(unit, slot):
        tile, block = unit
        score_ref[slot] = lax.dot_general(
            q_ref[tile * ROW_TILE : (tile + 1) * ROW_TILE],
            keys[block][...],
            NT,
            preferred_element_type=jnp.float32,
        )

    score(units[0], 0)
    held = None
    for step, (tile, block) in enumerate(units):
        if step + 1 < len(units):
            score(units[step + 1], (step + 1) % 2)
        scores = score_ref[step % 2]
        row_max = jnp.max(scores, axis=1, keepdims=True)
        terms = jnp.exp((scores - row_max) * score_scale)
        total = jnp.sum(terms, axis=1, keepdims=True)
        acc = jnp.dot(
            terms.astype(jnp.bfloat16), values[block][...], preferred_element_type=jnp.float32
        )
        if block == 0:
            held = (row_max, total, acc)
            continue
        max0, total0, acc0 = held
        top = jnp.maximum(max0, row_max)
        weight0 = jnp.exp((max0 - top) * score_scale)
        weight1 = jnp.exp((row_max - top) * score_scale)
        joined = weight0 * total0 + weight1 * total
        mixed = (weight0 * acc0 + weight1 * acc) / joined
        logs = jnp.broadcast_to(top * score_scale + jnp.log(joined), (ROW_TILE, width))
        for k in range(dests):
            rows = slice(k * per_dest, (k + 1) * per_dest)
            dest = tile * dests + k
            out_ref[dest, :per_dest] = mixed[rows]
            line = jnp.sum(jnp.where(diagonal, logs[rows], 0.0), axis=0, keepdims=True)
            out_ref[dest, per_dest:] = jnp.broadcast_to(line, (LOG_ROWS, width))


def prefix_partials(rows_q, keys, values, far_keys, far_values, per_dest, score_scale):
    rows, width = rows_q.shape
    length = keys.shape[0]
    step_rows = min(STEP_ROWS, rows)
    dests = step_rows // per_dest

    def whole(i):
        return (0, 0)

    return pl.pallas_call(
        functools.partial(prefix_kernel, per_dest=per_dest, score_scale=score_scale),
        grid=(rows // step_rows,),
        in_specs=[pl.BlockSpec((step_rows, width), lambda i: (i, 0))]
        + [pl.BlockSpec((length, width), whole)] * 4,
        out_specs=pl.BlockSpec((dests, per_dest + LOG_ROWS, width), lambda i: (i, 0, 0)),
        out_shape=jax.ShapeDtypeStruct((rows // per_dest, per_dest + LOG_ROWS, width), jnp.float32),
        scratch_shapes=[pltpu.VMEM((2, ROW_TILE, length), jnp.float32)],
        compiler_params=pltpu.CompilerParams(vmem_limit_bytes=VMEM_BYTES),
        cost_estimate=pl.CostEstimate(
            flops=8 * rows * length * width,
            bytes_accessed=8 * length * width + 6 * rows * width,
            transcendentals=2 * rows * length,
        ),
        name="prefix_attention",
    )(rows_q, keys, values, far_keys, far_values)


def join_kernel(got_ref, suf_ref, suf_log_ref, out_ref, log_ref, *, kv_count):
    count, heads, width = out_ref.shape
    group = heads // kv_count
    per_dest = count * group
    parts = got_ref.shape[0] // kv_count
    lane = lax.broadcasted_iota(jnp.int32, (per_dest, width), 1)
    row = lax.broadcasted_iota(jnp.int32, (per_dest, width), 0)
    diagonal = lane == row
    lines = [jnp.zeros((1, width), jnp.float32) for _ in range(count)]
    for g in range(kv_count):
        heads_of = slice(g * group, (g + 1) * group)
        suf_log = jnp.concatenate([suf_log_ref[r, heads_of] for r in range(count)], axis=0)
        suf_mixed = jnp.concatenate([suf_ref[r, heads_of] for r in range(count)], axis=0)
        logs = []
        top = suf_log
        for s in range(parts):
            line = got_ref[s * kv_count + g, per_dest : per_dest + 1]
            column = jnp.sum(jnp.where(diagonal, line, 0.0), axis=1, keepdims=True)
            logs.append(jnp.broadcast_to(column, (per_dest, width)))
            top = jnp.maximum(top, logs[-1])
        weight = jnp.exp(suf_log - top)
        acc = weight * suf_mixed
        total = weight
        for s in range(parts):
            weight = jnp.exp(logs[s] - top)
            acc = acc + weight * got_ref[s * kv_count + g, :per_dest]
            total = total + weight
        acc = acc / total
        logged = top + jnp.log(total)
        for r in range(count):
            rows = slice(r * group, (r + 1) * group)
            out_ref[r, heads_of] = acc[rows]
            place = lane[:group] == row[:group] + g * group
            lines[r] = lines[r] + jnp.sum(jnp.where(place, logged[rows], 0.0), axis=0, keepdims=True)
    for r in range(count):
        log_ref[r : r + 1] = lines[r][:, :heads]


def per_device(
    queries, prefix_keys, prefix_values, suffix_keys, suffix_values, suffix_lengths, slot_map
):
    count, heads, width = queries.shape
    kv_count = suffix_keys.shape[2]
    group = heads // kv_count
    score_scale = 1.0 / math.sqrt(width)
    keys = prefix_keys[:, 0, :]
    values = prefix_values[:, 0, :]
    swap = [(i, lax.axis_size("rep") - 1 - i) for i in range(lax.axis_size("rep"))]
    far_keys = lax.ppermute(keys, "rep", swap)
    far_values = lax.ppermute(values, "rep", swap)
    by_group = queries.reshape(count, kv_count, group, width).transpose(1, 0, 2, 3)
    sent = jnp.broadcast_to(
        by_group[None], (lax.axis_size("seq"), kv_count, count, group, width)
    ).reshape(-1, count * group, width)
    got_q = lax.all_to_all(sent, ("seq", "head"), split_axis=0, concat_axis=0, tiled=True)
    suf_mixed, suf_log = suffix_partials(
        queries, suffix_keys, suffix_values, suffix_lengths, slot_map, score_scale
    )
    partials = prefix_partials(
        got_q.reshape(-1, width), keys, values, far_keys, far_values, count * group, score_scale
    )
    got = lax.all_to_all(partials, ("seq", "head"), split_axis=0, concat_axis=0, tiled=True)
    return pl.pallas_call(
        functools.partial(join_kernel, kv_count=kv_count),
        in_specs=[pl.BlockSpec(memory_space=pltpu.VMEM)] * 3,
        out_specs=[pl.BlockSpec(memory_space=pltpu.VMEM)] * 2,
        out_shape=[
            jax.ShapeDtypeStruct((count, heads, width), jnp.float32),
            jax.ShapeDtypeStruct((count, heads), jnp.float32),
        ],
        compiler_params=pltpu.CompilerParams(vmem_limit_bytes=VMEM_BYTES),
        name="join_partials",
    )(got, suf_mixed, suf_log)


def solution(mesh):
    by_request = P(("seq", "head", "rep"))
    by_block = P(("seq", "rep"), "head", None)
    placed = (by_request, by_block, by_block, by_request, by_request, by_request, by_request)
    return jax.shard_map(
        per_device,
        mesh=mesh,
        in_specs=placed,
        out_specs=(by_request, by_request),
        check_vma=False,
    )
```

```python
import functools
import math

import jax
import jax.numpy as jnp
from jax import lax
from jax.experimental import pallas as pl
from jax.experimental.pallas import tpu as pltpu
from jax.sharding import PartitionSpec as P

ROW_TILE = 128
CALL_PIECES = 16
SUF_CHUNK = 1024
SUF_COPIES = 4
LOG_ROWS = 8
NT = (((1,), (1,)), ((), ()))
PREFIX_VMEM = 14 * 1024 * 1024
SUFFIX_VMEM = 58 * 1024 * 1024
SMALL_VMEM = 8 * 1024 * 1024
IN_VMEM = pl.BlockSpec(memory_space=pltpu.VMEM)
IN_SMEM = pl.BlockSpec(memory_space=pltpu.SMEM)
IN_HBM = pl.BlockSpec(memory_space=pltpu.HBM)


def split_kernel(q_ref, *piece_refs):
    count = q_ref.shape[0]
    group = q_ref.shape[1] // len(piece_refs)
    own = lax.axis_index("head")
    for d, piece_ref in enumerate(piece_refs):
        begin = pl.multiple_of((own ^ d) * group, group)
        for r in range(count):
            piece_ref[r * group : (r + 1) * group] = q_ref[r, pl.ds(begin, group)]


def split_queries(queries, kv_count):
    count, heads, width = queries.shape
    piece = jax.ShapeDtypeStruct((count * heads // kv_count, width), queries.dtype)
    return pl.pallas_call(
        split_kernel,
        in_specs=[IN_VMEM],
        out_specs=[IN_VMEM] * kv_count,
        out_shape=[piece] * kv_count,
        compiler_params=pltpu.CompilerParams(vmem_limit_bytes=SMALL_VMEM),
        name="split_queries",
    )(queries)


def suffix_kernel(
    slot_ref, length_ref, q_ref, k_hbm, v_hbm, mixed_ref, log_ref, k_buf, v_buf, score_ref, sems, *, kv_count, score_scale
):
    count, heads, width = q_ref.shape
    rows = k_hbm.shape[1]
    copy_rows = rows // SUF_COPIES
    copies = {}
    for r in range(count):
        slot = lax.rem(slot_ref[r], count)
        for which, (source, target) in enumerate(((k_hbm, k_buf), (v_hbm, v_buf))):
            for c in range(SUF_COPIES):
                part = pl.ds(c * copy_rows, copy_rows)
                copies[r, which, c] = pltpu.make_async_copy(
                    source.at[slot, part], target.at[r, part], sems.at[r, which, c]
                )
                copies[r, which, c].start()
    lane = lax.broadcasted_iota(jnp.int32, (heads, SUF_CHUNK), 1)
    group = lax.broadcasted_iota(jnp.int32, (heads, SUF_CHUNK), 0) // (heads // kv_count)
    own_head = (lane % kv_count) == group
    for r in range(count):
        limit = length_ref[r] * kv_count
        query = q_ref[r]
        peak = jnp.full((heads, SUF_CHUNK), -1e30, jnp.float32)
        for begin in range(0, rows, SUF_CHUNK):
            if begin % copy_rows == 0:
                copies[r, 0, begin // copy_rows].wait()
            part = lax.dot_general(
                query, k_buf[r, begin : begin + SUF_CHUNK], NT, preferred_element_type=jnp.float32
            )
            part = jnp.where(own_head & (lane < limit - begin), part, -1e30)
            score_ref[:, begin : begin + SUF_CHUNK] = part
            peak = jnp.maximum(peak, part)
        row_max = jnp.max(peak, axis=1, keepdims=True)
        sums = jnp.zeros((heads, SUF_CHUNK), jnp.float32)
        acc = jnp.zeros((heads, width), jnp.float32)
        for begin in range(0, rows, SUF_CHUNK):
            if begin % copy_rows == 0:
                copies[r, 1, begin // copy_rows].wait()
            terms = jnp.exp((score_ref[:, begin : begin + SUF_CHUNK] - row_max) * score_scale)
            sums = sums + terms
            acc = acc + jnp.dot(
                terms.astype(jnp.bfloat16),
                v_buf[r, begin : begin + SUF_CHUNK],
                preferred_element_type=jnp.float32,
            )
        total = jnp.sum(sums, axis=1, keepdims=True)
        mixed_ref[r] = acc / total
        log_ref[r] = jnp.broadcast_to(row_max * score_scale + jnp.log(total), (heads, width))


def suffix_partials(queries, keys, values, lengths, slots, score_scale):
    count, heads, width = queries.shape
    kv_count = keys.shape[2]
    rows = keys.shape[1] * kv_count
    return pl.pallas_call(
        functools.partial(suffix_kernel, kv_count=kv_count, score_scale=score_scale),
        in_specs=[IN_SMEM, IN_SMEM, IN_VMEM, IN_HBM, IN_HBM],
        out_specs=[IN_VMEM, IN_VMEM],
        out_shape=[jax.ShapeDtypeStruct((count, heads, width), jnp.float32)] * 2,
        scratch_shapes=[
            pltpu.VMEM((count, rows, width), keys.dtype),
            pltpu.VMEM((count, rows, width), values.dtype),
            pltpu.VMEM((heads, rows), jnp.float32),
            pltpu.SemaphoreType.DMA((count, 2, SUF_COPIES)),
        ],
        compiler_params=pltpu.CompilerParams(vmem_limit_bytes=SUFFIX_VMEM),
        cost_estimate=pl.CostEstimate(
            flops=4 * count * heads * rows * width,
            bytes_accessed=4 * count * rows * width,
            transcendentals=count * heads * rows,
        ),
        name="suffix_attention",
    )(slots, lengths, queries, keys.reshape(count, rows, width), values.reshape(count, rows, width))


def prefix_kernel(*refs, pieces, score_scale):
    q_refs, (k0_ref, v0_ref, k1_ref, v1_ref) = refs[:pieces], refs[pieces : pieces + 4]
    out_refs, score_ref = refs[pieces + 4 : -1], refs[-1]
    per_dest, width = q_refs[0].shape
    per_tile = ROW_TILE // per_dest
    keys, values = (k0_ref, k1_ref), (v0_ref, v1_ref)
    units = [(tile, block) for tile in range(pieces // per_tile) for block in range(2)]
    lane = lax.broadcasted_iota(jnp.int32, (per_dest, width), 1)
    row = lax.broadcasted_iota(jnp.int32, (per_dest, width), 0)
    diagonal = lane == row

    def score(unit, slot):
        tile, block = unit
        query = jnp.concatenate(
            [q_refs[tile * per_tile + k][...] for k in range(per_tile)], axis=0
        )
        score_ref[slot] = lax.dot_general(
            query, keys[block][...], NT, preferred_element_type=jnp.float32
        )

    score(units[0], 0)
    held = None
    for step, (tile, block) in enumerate(units):
        if step + 1 < len(units):
            score(units[step + 1], (step + 1) % 2)
        scores = score_ref[step % 2]
        row_max = jnp.max(scores, axis=1, keepdims=True)
        terms = jnp.exp((scores - row_max) * score_scale)
        total = jnp.sum(terms, axis=1, keepdims=True)
        acc = jnp.dot(
            terms.astype(jnp.bfloat16), values[block][...], preferred_element_type=jnp.float32
        )
        if block == 0:
            held = (row_max, total, acc)
            continue
        max0, total0, acc0 = held
        top = jnp.maximum(max0, row_max)
        weight0 = jnp.exp((max0 - top) * score_scale)
        weight1 = jnp.exp((row_max - top) * score_scale)
        joined = weight0 * total0 + weight1 * total
        mixed = (weight0 * acc0 + weight1 * acc) / joined
        logs = jnp.broadcast_to(top * score_scale + jnp.log(joined), (ROW_TILE, width))
        for k in range(per_tile):
            rows = slice(k * per_dest, (k + 1) * per_dest)
            out_ref = out_refs[tile * per_tile + k]
            out_ref[:per_dest] = mixed[rows]
            line = jnp.sum(jnp.where(diagonal, logs[rows], 0.0), axis=0, keepdims=True)
            out_ref[per_dest:] = jnp.broadcast_to(line, (LOG_ROWS, width))


def prefix_partials(pieces_q, keys, values, far_keys, far_values, score_scale):
    pieces = len(pieces_q)
    per_dest, width = pieces_q[0].shape
    length = keys.shape[0]
    rows = pieces * per_dest
    piece = jax.ShapeDtypeStruct((per_dest + LOG_ROWS, width), jnp.float32)
    return pl.pallas_call(
        functools.partial(prefix_kernel, pieces=pieces, score_scale=score_scale),
        in_specs=[IN_VMEM] * (pieces + 4),
        out_specs=[IN_VMEM] * pieces,
        out_shape=[piece] * pieces,
        scratch_shapes=[pltpu.VMEM((2, ROW_TILE, length), jnp.float32)],
        compiler_params=pltpu.CompilerParams(vmem_limit_bytes=PREFIX_VMEM),
        cost_estimate=pl.CostEstimate(
            flops=8 * rows * length * width,
            bytes_accessed=8 * length * width + 6 * rows * width,
            transcendentals=2 * rows * length,
        ),
        name="prefix_attention",
    )(*pieces_q, keys, values, far_keys, far_values)


def join_kernel(*refs, kv_count):
    got_refs = refs[:-4]
    suf_ref, suf_log_ref, out_ref, log_ref = refs[-4:]
    count, heads, width = out_ref.shape
    group = heads // kv_count
    per_dest = count * group
    parts = len(got_refs) // kv_count
    own = lax.axis_index("head")
    lane = lax.broadcasted_iota(jnp.int32, (per_dest, width), 1)
    row = lax.broadcasted_iota(jnp.int32, (per_dest, width), 0)
    diagonal = lane == row
    lines = [jnp.zeros((1, width), jnp.float32) for _ in range(count)]
    for d in range(kv_count):
        begin = pl.multiple_of((own ^ d) * group, group)
        heads_of = pl.ds(begin, group)
        suf_log = jnp.concatenate([suf_log_ref[r, heads_of] for r in range(count)], axis=0)
        suf_mixed = jnp.concatenate([suf_ref[r, heads_of] for r in range(count)], axis=0)
        logs = []
        top = suf_log
        for s in range(parts):
            line = got_refs[s * kv_count + d][per_dest : per_dest + 1]
            column = jnp.sum(jnp.where(diagonal, line, 0.0), axis=1, keepdims=True)
            logs.append(jnp.broadcast_to(column, (per_dest, width)))
            top = jnp.maximum(top, logs[-1])
        weight = jnp.exp(suf_log - top)
        acc = weight * suf_mixed
        total = weight
        for s in range(parts):
            weight = jnp.exp(logs[s] - top)
            acc = acc + weight * got_refs[s * kv_count + d][:per_dest]
            total = total + weight
        acc = acc / total
        logged = top + jnp.log(total)
        for r in range(count):
            rows = slice(r * group, (r + 1) * group)
            out_ref[r, heads_of] = acc[rows]
            place = lane[:group] == row[:group] + begin
            lines[r] = lines[r] + jnp.sum(jnp.where(place, logged[rows], 0.0), axis=0, keepdims=True)
    for r in range(count):
        log_ref[r : r + 1] = lines[r][:, :heads]


def join_partials(got, suf_mixed, suf_log, kv_count):
    count, heads, width = suf_mixed.shape
    return pl.pallas_call(
        functools.partial(join_kernel, kv_count=kv_count),
        in_specs=[IN_VMEM] * (len(got) + 2),
        out_specs=[IN_VMEM] * 2,
        out_shape=[
            jax.ShapeDtypeStruct((count, heads, width), jnp.float32),
            jax.ShapeDtypeStruct((count, heads), jnp.float32),
        ],
        compiler_params=pltpu.CompilerParams(vmem_limit_bytes=SMALL_VMEM),
        name="join_partials",
    )(*got, suf_mixed, suf_log)


def per_device(
    queries, prefix_keys, prefix_values, suffix_keys, suffix_values, suffix_lengths, slot_map
):
    width = queries.shape[2]
    kv_count = suffix_keys.shape[2]
    score_scale = 1.0 / math.sqrt(width)
    seq_devices, head_devices = lax.axis_size("seq"), lax.axis_size("head")
    offsets = [(s, h) for s in range(seq_devices) for h in range(head_devices)]

    def cross(array, offset):
        if offset == (0, 0):
            return array
        step = offset[0] * head_devices + offset[1]
        pairs = [(i, i ^ step) for i in range(seq_devices * head_devices)]
        return lax.ppermute(array, ("seq", "head"), pairs)

    sent = split_queries(queries, kv_count)
    got_q = [cross(sent[h], (s, h)) for s, h in offsets]
    keys = prefix_keys[:, 0, :]
    values = prefix_values[:, 0, :]
    far_keys = lax.ppermute(keys, "rep", [(0, 1), (1, 0)])
    far_values = lax.ppermute(values, "rep", [(0, 1), (1, 0)])
    suf_mixed, suf_log = suffix_partials(
        queries, suffix_keys, suffix_values, suffix_lengths, slot_map, score_scale
    )
    got = []
    for begin in range(0, len(offsets), CALL_PIECES):
        some = slice(begin, begin + CALL_PIECES)
        partials = prefix_partials(got_q[some], keys, values, far_keys, far_values, score_scale)
        got += [cross(part, offset) for part, offset in zip(partials, offsets[some])]
    return join_partials(got, suf_mixed, suf_log, kv_count)


def solution(mesh):
    by_request = P(("seq", "head", "rep"))
    by_block = P(("seq", "rep"), "head", None)
    placed = (by_request, by_block, by_block, by_request, by_request, by_request, by_request)
    return jax.shard_map(
        per_device,
        mesh=mesh,
        in_specs=placed,
        out_specs=(by_request, by_request),
        check_vma=False,
    )
```

```python
import functools
import math

import jax
import jax.numpy as jnp
from jax import lax
from jax.experimental import pallas as pl
from jax.experimental.pallas import tpu as pltpu
from jax.sharding import PartitionSpec as P

ROW_TILE = 128
STEP_ROWS = 512
SUF_CHUNK = 1024
SUF_COPIES = 4
IN_FLIGHT = 4
LOG_ROWS = 8
NT = (((1,), (1,)), ((), ()))
PREFIX_VMEM = 14 * 1024 * 1024
SUFFIX_VMEM = 20 * 1024 * 1024
SMALL_VMEM = 8 * 1024 * 1024
IN_VMEM = pl.BlockSpec(memory_space=pltpu.VMEM)
IN_SMEM = pl.BlockSpec(memory_space=pltpu.SMEM)
IN_HBM = pl.BlockSpec(memory_space=pltpu.HBM)


def in_hbm(array):
    return pltpu.with_memory_space_constraint(array, pltpu.HBM)


def suffix_kernel(*refs, request, carried, kv_count, score_scale):
    slot_ref, length_ref, q_ref, k_hbm, v_hbm = refs[:5]
    carried_refs = refs[5 : 5 + carried]
    mixed_ref, log_ref = refs[5 + carried : 7 + carried]
    brought_refs = refs[7 + carried : 7 + 2 * carried]
    k_buf, v_buf, score_ref, sems, carry_sems = refs[7 + 2 * carried :]
    count, heads, width = q_ref.shape
    rows = k_hbm.shape[1]
    copy_rows = rows // SUF_COPIES
    slot = lax.rem(slot_ref[request], count)
    copies = []
    for which, (source, target) in enumerate(((k_hbm, k_buf), (v_hbm, v_buf))):
        for c in range(SUF_COPIES):
            part = pl.ds(c * copy_rows, copy_rows)
            copies.append(
                pltpu.make_async_copy(source.at[slot, part], target.at[part], sems.at[which, c])
            )
    carries = [
        pltpu.make_async_copy(source, target, carry_sems.at[i])
        for i, (source, target) in enumerate(zip(carried_refs, brought_refs))
    ]
    for copy in copies[:IN_FLIGHT]:
        copy.start()

    def arrive(i):
        copies[i].wait()
        if i + IN_FLIGHT < len(copies):
            copies[i + IN_FLIGHT].start()
        elif i + IN_FLIGHT - len(copies) < carried:
            carries[i + IN_FLIGHT - len(copies)].start()

    lane = lax.broadcasted_iota(jnp.int32, (heads, SUF_CHUNK), 1)
    group = lax.broadcasted_iota(jnp.int32, (heads, SUF_CHUNK), 0) // (heads // kv_count)
    own_head = (lane % kv_count) == group
    limit = length_ref[request] * kv_count
    query = q_ref[request]
    peak = jnp.full((heads, SUF_CHUNK), -1e30, jnp.float32)
    for begin in range(0, rows, SUF_CHUNK):
        if begin % copy_rows == 0:
            arrive(begin // copy_rows)
        part = lax.dot_general(
            query, k_buf[begin : begin + SUF_CHUNK], NT, preferred_element_type=jnp.float32
        )
        part = jnp.where(own_head & (lane < limit - begin), part, -1e30)
        score_ref[:, begin : begin + SUF_CHUNK] = part
        peak = jnp.maximum(peak, part)
    row_max = jnp.max(peak, axis=1, keepdims=True)
    sums = jnp.zeros((heads, SUF_CHUNK), jnp.float32)
    acc = jnp.zeros((heads, width), jnp.float32)
    for begin in range(0, rows, SUF_CHUNK):
        if begin % copy_rows == 0:
            arrive(SUF_COPIES + begin // copy_rows)
        terms = jnp.exp((score_ref[:, begin : begin + SUF_CHUNK] - row_max) * score_scale)
        sums = sums + terms
        acc = acc + jnp.dot(
            terms.astype(jnp.bfloat16),
            v_buf[begin : begin + SUF_CHUNK],
            preferred_element_type=jnp.float32,
        )
    total = jnp.sum(sums, axis=1, keepdims=True)
    mixed_ref[...] = acc / total
    log_ref[...] = jnp.broadcast_to(row_max * score_scale + jnp.log(total), (heads, width))
    for carry in carries:
        carry.wait()


def suffix_partials(request, queries, keys, values, lengths, slots, carried, score_scale):
    count, heads, width = queries.shape
    kv_count = keys.shape[2]
    rows = keys.shape[1] * kv_count
    return pl.pallas_call(
        functools.partial(
            suffix_kernel,
            request=request,
            carried=len(carried),
            kv_count=kv_count,
            score_scale=score_scale,
        ),
        in_specs=[IN_SMEM, IN_SMEM, IN_VMEM] + [IN_HBM] * (2 + len(carried)),
        out_specs=[IN_VMEM] * (2 + len(carried)),
        out_shape=[pltpu.VMEM((heads, width), jnp.float32)] * 2
        + [pltpu.VMEM(array.shape, array.dtype) for array in carried],
        scratch_shapes=[
            pltpu.VMEM((rows, width), keys.dtype),
            pltpu.VMEM((rows, width), values.dtype),
            pltpu.VMEM((heads, rows), jnp.float32),
            pltpu.SemaphoreType.DMA((2, SUF_COPIES)),
            pltpu.SemaphoreType.DMA((max(1, len(carried)),)),
        ],
        compiler_params=pltpu.CompilerParams(vmem_limit_bytes=SUFFIX_VMEM),
        cost_estimate=pl.CostEstimate(
            flops=4 * heads * rows * width,
            bytes_accessed=4 * rows * width,
            transcendentals=heads * rows,
        ),
        name=f"suffix_attention_{request}",
    )(
        slots,
        lengths,
        queries,
        in_hbm(keys.reshape(count, rows, width)),
        in_hbm(values.reshape(count, rows, width)),
        *map(in_hbm, carried),
    )


def prefix_kernel(
    q_ref, k0_ref, v0_ref, k1_ref, v1_ref, out_ref, score_ref, *, per_dest, score_scale
):
    width = q_ref.shape[1]
    tiles = q_ref.shape[0] // ROW_TILE
    dests = ROW_TILE // per_dest
    keys, values = (k0_ref, k1_ref), (v0_ref, v1_ref)
    units = [(tile, block) for tile in range(tiles) for block in range(2)]
    lane = lax.broadcasted_iota(jnp.int32, (per_dest, width), 1)
    row = lax.broadcasted_iota(jnp.int32, (per_dest, width), 0)
    diagonal = lane == row

    def score(unit, slot):
        tile, block = unit
        score_ref[slot] = lax.dot_general(
            q_ref[tile * ROW_TILE : (tile + 1) * ROW_TILE],
            keys[block][...],
            NT,
            preferred_element_type=jnp.float32,
        )

    score(units[0], 0)
    held = None
    for step, (tile, block) in enumerate(units):
        if step + 1 < len(units):
            score(units[step + 1], (step + 1) % 2)
        scores = score_ref[step % 2]
        row_max = jnp.max(scores, axis=1, keepdims=True)
        terms = jnp.exp((scores - row_max) * score_scale)
        total = jnp.sum(terms, axis=1, keepdims=True)
        acc = jnp.dot(
            terms.astype(jnp.bfloat16), values[block][...], preferred_element_type=jnp.float32
        )
        if block == 0:
            held = (row_max, total, acc)
            continue
        max0, total0, acc0 = held
        top = jnp.maximum(max0, row_max)
        weight0 = jnp.exp((max0 - top) * score_scale)
        weight1 = jnp.exp((row_max - top) * score_scale)
        joined = weight0 * total0 + weight1 * total
        mixed = (weight0 * acc0 + weight1 * acc) / joined
        logs = jnp.broadcast_to(top * score_scale + jnp.log(joined), (ROW_TILE, width))
        for k in range(dests):
            rows = slice(k * per_dest, (k + 1) * per_dest)
            dest = tile * dests + k
            out_ref[dest, :per_dest] = mixed[rows]
            line = jnp.sum(jnp.where(diagonal, logs[rows], 0.0), axis=0, keepdims=True)
            out_ref[dest, per_dest:] = jnp.broadcast_to(line, (LOG_ROWS, width))


def prefix_partials(rows_q, keys, values, far_keys, far_values, per_dest, score_scale):
    rows, width = rows_q.shape
    length = keys.shape[0]
    step_rows = min(STEP_ROWS, rows)
    blocked = {}
    if step_rows == rows:
        blocked["in_specs"] = [IN_VMEM] * 5
        blocked["out_specs"] = IN_VMEM
    else:
        blocked["grid"] = (rows // step_rows,)
        blocked["in_specs"] = [pl.BlockSpec((step_rows, width), lambda i: (i, 0))]
        blocked["in_specs"] += [pl.BlockSpec((length, width), lambda i: (0, 0))] * 4
        blocked["out_specs"] = pl.BlockSpec(
            (step_rows // per_dest, per_dest + LOG_ROWS, width), lambda i: (i, 0, 0)
        )
    return pl.pallas_call(
        functools.partial(prefix_kernel, per_dest=per_dest, score_scale=score_scale),
        **blocked,
        out_shape=jax.ShapeDtypeStruct((rows // per_dest, per_dest + LOG_ROWS, width), jnp.float32),
        scratch_shapes=[pltpu.VMEM((2, ROW_TILE, length), jnp.float32)],
        compiler_params=pltpu.CompilerParams(vmem_limit_bytes=PREFIX_VMEM),
        cost_estimate=pl.CostEstimate(
            flops=8 * rows * length * width,
            bytes_accessed=8 * length * width + 6 * rows * width,
            transcendentals=2 * rows * length,
        ),
        name="prefix_attention",
    )(rows_q, keys, values, far_keys, far_values)


def join_kernel(got_ref, *refs, kv_count):
    suffix_refs, (out_ref, log_ref) = refs[:-2], refs[-2:]
    count, heads, width = out_ref.shape
    group = heads // kv_count
    per_dest = count * group
    parts = got_ref.shape[0] // kv_count
    lane = lax.broadcasted_iota(jnp.int32, (per_dest, width), 1)
    row = lax.broadcasted_iota(jnp.int32, (per_dest, width), 0)
    diagonal = lane == row
    lines = [jnp.zeros((1, width), jnp.float32) for _ in range(count)]
    for g in range(kv_count):
        heads_of = slice(g * group, (g + 1) * group)
        suf_mixed = jnp.concatenate([suffix_refs[2 * r][heads_of] for r in range(count)], axis=0)
        suf_log = jnp.concatenate([suffix_refs[2 * r + 1][heads_of] for r in range(count)], axis=0)
        logs = []
        top = suf_log
        for s in range(parts):
            line = got_ref[s * kv_count + g, per_dest : per_dest + 1]
            column = jnp.sum(jnp.where(diagonal, line, 0.0), axis=1, keepdims=True)
            logs.append(jnp.broadcast_to(column, (per_dest, width)))
            top = jnp.maximum(top, logs[-1])
        weight = jnp.exp(suf_log - top)
        acc = weight * suf_mixed
        total = weight
        for s in range(parts):
            weight = jnp.exp(logs[s] - top)
            acc = acc + weight * got_ref[s * kv_count + g, :per_dest]
            total = total + weight
        acc = acc / total
        logged = top + jnp.log(total)
        for r in range(count):
            rows = slice(r * group, (r + 1) * group)
            out_ref[r, heads_of] = acc[rows]
            place = lane[:group] == row[:group] + g * group
            lines[r] = lines[r] + jnp.sum(jnp.where(place, logged[rows], 0.0), axis=0, keepdims=True)
    for r in range(count):
        log_ref[r : r + 1] = lines[r][:, :heads]


def join_partials(got, suffix_parts, kv_count):
    heads, width = suffix_parts[0].shape
    count = len(suffix_parts) // 2
    return pl.pallas_call(
        functools.partial(join_kernel, kv_count=kv_count),
        in_specs=[IN_VMEM] * (1 + len(suffix_parts)),
        out_specs=[IN_VMEM] * 2,
        out_shape=[
            jax.ShapeDtypeStruct((count, heads, width), jnp.float32),
            jax.ShapeDtypeStruct((count, heads), jnp.float32),
        ],
        compiler_params=pltpu.CompilerParams(vmem_limit_bytes=SMALL_VMEM),
        name="join_partials",
    )(got, *suffix_parts)


def per_device(
    queries, prefix_keys, prefix_values, suffix_keys, suffix_values, suffix_lengths, slot_map
):
    count, heads, width = queries.shape
    kv_count = suffix_keys.shape[2]
    group = heads // kv_count
    score_scale = 1.0 / math.sqrt(width)
    by_group = queries.reshape(count, kv_count, group, width).transpose(1, 0, 2, 3)
    sent = jnp.broadcast_to(
        by_group[None], (lax.axis_size("seq"), kv_count, count, group, width)
    ).reshape(-1, count * group, width)
    got_q = lax.all_to_all(sent, ("seq", "head"), split_axis=0, concat_axis=0, tiled=True)
    keys = prefix_keys[:, 0, :]
    values = prefix_values[:, 0, :]
    far_keys = lax.ppermute(keys, "rep", [(0, 1), (1, 0)])
    far_values = lax.ppermute(values, "rep", [(0, 1), (1, 0)])
    suffix_parts = []
    for request in range(count):
        carried = (keys, values) if request == 0 else ()
        mixed, log, *brought = suffix_partials(
            request, queries, suffix_keys, suffix_values, suffix_lengths, slot_map, carried, score_scale
        )
        suffix_parts += [mixed, log]
        if brought:
            keys, values = brought
    partials = prefix_partials(
        got_q.reshape(-1, width), keys, values, far_keys, far_values, count * group, score_scale
    )
    got = lax.all_to_all(partials, ("seq", "head"), split_axis=0, concat_axis=0, tiled=True)
    return join_partials(got, suffix_parts, kv_count)


def solution(mesh):
    by_request = P(("seq", "head", "rep"))
    by_block = P(("seq", "rep"), "head", None)
    placed = (by_request, by_block, by_block, by_request, by_request, by_request, by_request)
    return jax.shard_map(
        per_device,
        mesh=mesh,
        in_specs=placed,
        out_specs=(by_request, by_request),
        check_vma=False,
    )
```

```python
import functools
import math

import jax
import jax.numpy as jnp
from jax import lax
from jax.experimental import pallas as pl
from jax.experimental.pallas import tpu as pltpu
from jax.sharding import PartitionSpec as P

ROW_TILE = 128
STEP_ROWS = 512
SUF_COPIES = 4
IN_FLIGHT = 4
LANES = 128
LOG_ROWS = 8
VALUE_BITS = 15
LOG_BITS = 30
LEAST = 1e-25
PEAK_LEAST = 1e-33
NT = (((1,), (1,)), ((), ()))
PREFIX_VMEM = 14 * 1024 * 1024
SUFFIX_VMEM = 20 * 1024 * 1024
SMALL_VMEM = 8 * 1024 * 1024
IN_VMEM = pl.BlockSpec(memory_space=pltpu.VMEM)
IN_HBM = pl.BlockSpec(memory_space=pltpu.HBM)


def in_hbm(array):
    return pltpu.with_memory_space_constraint(array, pltpu.HBM)


def layout_kernel(q_hbm, sent_hbm, buf, in_sems, out_sems):
    groups, rows, width = buf.shape
    count = q_hbm.shape[0]
    group = rows // count
    repeats = sent_hbm.shape[0] // groups
    reads = [
        pltpu.make_async_copy(
            q_hbm.at[r, pl.ds(g * group, group)], buf.at[g, pl.ds(r * group, group)], in_sems.at[g, r]
        )
        for g in range(groups)
        for r in range(count)
    ]
    for read in reads:
        read.start()
    for read in reads:
        read.wait()
    writes = [
        pltpu.make_async_copy(buf, sent_hbm.at[pl.ds(s * groups, groups)], out_sems.at[s])
        for s in range(repeats)
    ]
    for write in writes:
        write.start()
    for write in writes:
        write.wait()


def layout_queries(queries, groups, repeats):
    count, heads, width = queries.shape
    rows = count * heads // groups
    return pl.pallas_call(
        layout_kernel,
        in_specs=[IN_HBM],
        out_specs=IN_HBM,
        out_shape=pltpu.HBM((repeats * groups, rows, width), queries.dtype),
        scratch_shapes=[
            pltpu.VMEM((groups, rows, width), queries.dtype),
            pltpu.SemaphoreType.DMA((groups, count)),
            pltpu.SemaphoreType.DMA((repeats,)),
        ],
        compiler_params=pltpu.CompilerParams(vmem_limit_bytes=SMALL_VMEM),
        name="layout_queries",
    )(in_hbm(queries))


def suffix_kernel(*refs, place, carried, kv_count, score_scale):
    slot_hbm, length_hbm, q_hbm, k_hbm, v_hbm = refs[:5]
    refs = refs[5:]
    count, heads, width = q_hbm.shape
    carried_refs, refs = refs[:carried], refs[carried:]
    last = place == count - 1
    earlier, refs = (refs[: 2 * place], refs[2 * place :]) if last else ((), refs)
    mixed_ref, log_ref = refs[:2]
    brought_refs, refs = refs[2 : 2 + carried], refs[2 + carried :]
    slot_ref, length_ref, q_ref, k_buf, v_buf, score_ref, sems, small_sems = refs
    rows = k_hbm.shape[1]
    copy_rows = rows // SUF_COPIES
    copies = []
    for which, (source, target) in enumerate(((k_hbm, k_buf), (v_hbm, v_buf))):
        for c in range(SUF_COPIES):
            part = pl.ds(c * copy_rows, copy_rows)
            copies.append(
                pltpu.make_async_copy(source.at[place, part], target.at[part], sems.at[which, c])
            )
    small = [
        pltpu.make_async_copy(source, target, small_sems.at[i])
        for i, (source, target) in enumerate(
            [(slot_hbm, slot_ref), (length_hbm, length_ref), (q_hbm, q_ref)]
            + list(zip(carried_refs, brought_refs))
        )
    ]
    carries = small[3:]
    for copy in small[:3] + copies[:IN_FLIGHT]:
        copy.start()

    def arrive(i):
        copies[i].wait()
        if i + IN_FLIGHT < len(copies):
            copies[i + IN_FLIGHT].start()
        elif i + IN_FLIGHT - len(copies) < carried:
            carries[i + IN_FLIGHT - len(copies)].start()

    for copy in small[:3]:
        copy.wait()

    def request_of(slot):
        found = jnp.int32(0)
        for r in range(1, count):
            found = jnp.where(lax.rem(slot_ref[r], count) == slot, r, found)
        return found

    request = request_of(place)
    limit = length_ref[request] * kv_count
    query = q_ref[request]
    lane = lax.broadcasted_iota(jnp.int32, (heads, LANES), 1)
    group = lax.broadcasted_iota(jnp.int32, (heads, LANES), 0) // (heads // kv_count)
    lane = jnp.where((lane % kv_count) == group, lane, rows)
    peak = jnp.full((heads, LANES), -1e30, jnp.float32)
    for c in range(SUF_COPIES):
        arrive(c)
        part = lax.dot_general(
            query, k_buf[c * copy_rows : (c + 1) * copy_rows], NT, preferred_element_type=jnp.float32
        )
        for begin in range(0, copy_rows, LANES):
            at = c * copy_rows + begin
            tile = jnp.where(lane < limit - at, part[:, begin : begin + LANES], -1e30)
            score_ref[:, at : at + LANES] = tile
            peak = jnp.maximum(peak, tile)
    row_max = jnp.max(peak, axis=1, keepdims=True)
    sums = jnp.zeros((heads, LANES), jnp.float32)
    acc = jnp.zeros((heads, width), jnp.float32)
    for c in range(SUF_COPIES):
        arrive(SUF_COPIES + c)
        part = slice(c * copy_rows, (c + 1) * copy_rows)
        terms = jnp.exp((score_ref[:, part] - row_max) * score_scale)
        for begin in range(0, copy_rows, LANES):
            sums = sums + terms[:, begin : begin + LANES]
        acc = acc + jnp.dot(
            terms.astype(jnp.bfloat16), v_buf[part], preferred_element_type=jnp.float32
        )
    total = jnp.sum(sums, axis=1, keepdims=True)
    mixed = acc / total
    log = jnp.broadcast_to(row_max * score_scale + jnp.log(total), (heads, width))
    for carry in carries:
        carry.wait()
    if not last:
        mixed_ref[...] = mixed
        log_ref[...] = log
        return
    mixed_ref[request] = mixed
    log_ref[request] = log
    for slot in range(place):
        mixed_ref[request_of(slot)] = earlier[2 * slot][...]
        log_ref[request_of(slot)] = earlier[2 * slot + 1][...]


def suffix_partials(place, queries, keys, values, lengths, slots, carried, earlier, score_scale):
    count, heads, width = queries.shape
    kv_count = keys.shape[2]
    rows = keys.shape[1] * kv_count
    result = (count, heads, width) if place == count - 1 else (heads, width)
    operands = (
        slots,
        lengths,
        queries,
        keys.reshape(count, rows, width),
        values.reshape(count, rows, width),
        *carried,
    )
    return pl.pallas_call(
        functools.partial(
            suffix_kernel,
            place=place,
            carried=len(carried),
            kv_count=kv_count,
            score_scale=score_scale,
        ),
        in_specs=[IN_HBM] * len(operands) + [IN_VMEM] * len(earlier),
        out_specs=[IN_VMEM] * (2 + len(carried)),
        out_shape=[pltpu.VMEM(result, jnp.float32)] * 2
        + [pltpu.VMEM(array.shape, array.dtype) for array in carried],
        scratch_shapes=[
            pltpu.SMEM((count,), jnp.int32),
            pltpu.SMEM((count,), jnp.int32),
            pltpu.VMEM((count, heads, width), queries.dtype),
            pltpu.VMEM((rows, width), keys.dtype),
            pltpu.VMEM((rows, width), values.dtype),
            pltpu.VMEM((heads, rows), jnp.float32),
            pltpu.SemaphoreType.DMA((2, SUF_COPIES)),
            pltpu.SemaphoreType.DMA((3 + len(carried),)),
        ],
        compiler_params=pltpu.CompilerParams(vmem_limit_bytes=SUFFIX_VMEM),
        cost_estimate=pl.CostEstimate(
            flops=4 * heads * rows * width,
            bytes_accessed=4 * rows * width,
            transcendentals=heads * rows,
        ),
        name=f"suffix_attention_{place}",
    )(*map(in_hbm, operands), *earlier)


def exponent(size, least):
    return jnp.floor(jnp.log2(jnp.maximum(size, least))) + 1.0


def prefix_kernel(
    q_ref, k0_ref, v0_ref, k1_ref, v1_ref, out_ref, score_ref, *, per_dest, score_scale
):
    width = q_ref.shape[1]
    tiles = q_ref.shape[0] // ROW_TILE
    dests = ROW_TILE // per_dest
    keys, values = (k0_ref, k1_ref), (v0_ref, v1_ref)
    units = [(tile, block) for tile in range(tiles) for block in range(2)]
    lane = lax.broadcasted_iota(jnp.int32, (per_dest, width), 1)
    row = lax.broadcasted_iota(jnp.int32, (per_dest, width), 0)
    diagonal = lane == row

    def score(unit, slot):
        tile, block = unit
        score_ref[slot] = lax.dot_general(
            q_ref[tile * ROW_TILE : (tile + 1) * ROW_TILE],
            keys[block][...],
            NT,
            preferred_element_type=jnp.float32,
        )

    score(units[0], 0)
    held = None
    for step, (tile, block) in enumerate(units):
        if step + 1 < len(units):
            score(units[step + 1], (step + 1) % 2)
        scores = score_ref[step % 2]
        row_max = jnp.max(scores, axis=1, keepdims=True)
        terms = jnp.exp((scores - row_max) * score_scale)
        total = jnp.sum(terms, axis=1, keepdims=True)
        acc = jnp.dot(
            terms.astype(jnp.bfloat16), values[block][...], preferred_element_type=jnp.float32
        )
        if block == 0:
            held = (row_max, total, acc)
            continue
        max0, total0, acc0 = held
        top = jnp.maximum(max0, row_max)
        weight0 = jnp.exp((max0 - top) * score_scale)
        weight1 = jnp.exp((row_max - top) * score_scale)
        joined = weight0 * total0 + weight1 * total
        mixed = (weight0 * acc0 + weight1 * acc) / joined
        logs = jnp.broadcast_to(top * score_scale + jnp.log(joined), (ROW_TILE, width))
        peak = jnp.max(jnp.abs(mixed), axis=1, keepdims=True)
        coded = jnp.round(mixed * jnp.exp2(VALUE_BITS - exponent(peak, PEAK_LEAST)))
        most = 2.0**VALUE_BITS - 1
        coded = jnp.clip(coded, -most, most).astype(jnp.int32)
        peaks = jnp.broadcast_to(peak, (ROW_TILE, width))
        half = per_dest // 2
        for k in range(dests):
            rows = slice(k * per_dest, (k + 1) * per_dest)
            dest = tile * dests + k
            high, low = coded[k * per_dest : k * per_dest + half], coded[k * per_dest + half : rows.stop]
            out_ref[dest, :half] = (high << 16) | (low & 0xFFFF)
            log_line = jnp.sum(jnp.where(diagonal, logs[rows], 0.0), axis=0, keepdims=True)
            peak_line = jnp.sum(jnp.where(diagonal, peaks[rows], 0.0), axis=0, keepdims=True)
            log_power = exponent(jnp.abs(log_line), LEAST)
            lines = jnp.concatenate(
                [
                    jnp.round(log_line * jnp.exp2(LOG_BITS - log_power)),
                    log_power,
                    exponent(peak_line, PEAK_LEAST),
                    jnp.zeros((LOG_ROWS - 3, width), jnp.float32),
                ],
                axis=0,
            )
            out_ref[dest, half:] = lines.astype(jnp.int32)


def prefix_partials(rows_q, keys, values, far_keys, far_values, per_dest, score_scale):
    rows, width = rows_q.shape
    length = keys.shape[0]
    step_rows = min(STEP_ROWS, rows)
    blocked = {}
    if step_rows == rows:
        blocked["in_specs"] = [IN_VMEM] * 5
        blocked["out_specs"] = IN_VMEM
    else:
        blocked["grid"] = (rows // step_rows,)
        blocked["in_specs"] = [pl.BlockSpec((step_rows, width), lambda i: (i, 0))]
        blocked["in_specs"] += [pl.BlockSpec((length, width), lambda i: (0, 0))] * 4
        blocked["out_specs"] = pl.BlockSpec(
            (step_rows // per_dest, per_dest // 2 + LOG_ROWS, width), lambda i: (i, 0, 0)
        )
    return pl.pallas_call(
        functools.partial(prefix_kernel, per_dest=per_dest, score_scale=score_scale),
        **blocked,
        out_shape=jax.ShapeDtypeStruct(
            (rows // per_dest, per_dest // 2 + LOG_ROWS, width), jnp.int32
        ),
        scratch_shapes=[pltpu.VMEM((2, ROW_TILE, length), jnp.float32)],
        compiler_params=pltpu.CompilerParams(vmem_limit_bytes=PREFIX_VMEM),
        cost_estimate=pl.CostEstimate(
            flops=8 * rows * length * width,
            bytes_accessed=8 * length * width + 6 * rows * width,
            transcendentals=2 * rows * length,
        ),
        name="prefix_attention",
    )(rows_q, keys, values, far_keys, far_values)


def join_kernel(got_ref, suf_ref, suf_log_ref, out_ref, log_ref, *, kv_count):
    count, heads, width = out_ref.shape
    group = heads // kv_count
    per_dest = count * group
    half = per_dest // 2
    parts = got_ref.shape[0] // kv_count
    lane = lax.broadcasted_iota(jnp.int32, (per_dest, width), 1)
    row = lax.broadcasted_iota(jnp.int32, (per_dest, width), 0)
    diagonal = lane == row

    def column(line):
        return jnp.sum(jnp.where(diagonal, line, 0.0), axis=1, keepdims=True)

    lines = [jnp.zeros((1, width), jnp.float32) for _ in range(count)]
    for g in range(kv_count):
        heads_of = slice(g * group, (g + 1) * group)
        suf_mixed = jnp.concatenate([suf_ref[r, heads_of] for r in range(count)], axis=0)
        suf_log = jnp.concatenate([suf_log_ref[r, heads_of] for r in range(count)], axis=0)
        logs, scales = [], []
        top = suf_log
        for s in range(parts):
            tail = got_ref[s * kv_count + g, half:].astype(jnp.float32)
            log_line = tail[0:1] * jnp.exp2(tail[1:2] - LOG_BITS)
            logs.append(jnp.broadcast_to(column(log_line), (per_dest, width)))
            scales.append(column(jnp.exp2(tail[2:3] - VALUE_BITS)))
            top = jnp.maximum(top, logs[-1])
        weight = jnp.exp(suf_log - top)
        acc = weight * suf_mixed
        total = weight
        for s in range(parts):
            words = got_ref[s * kv_count + g, :half]
            coded = jnp.concatenate([words >> 16, (words << 16) >> 16], axis=0)
            weight = jnp.exp(logs[s] - top)
            acc = acc + (weight * scales[s]) * coded.astype(jnp.float32)
            total = total + weight
        acc = acc / total
        logged = top + jnp.log(total)
        for r in range(count):
            rows = slice(r * group, (r + 1) * group)
            out_ref[r, heads_of] = acc[rows]
            place = lane[:group] == row[:group] + g * group
            lines[r] = lines[r] + jnp.sum(jnp.where(place, logged[rows], 0.0), axis=0, keepdims=True)
    for r in range(count):
        log_ref[r : r + 1] = lines[r][:, :heads]


def join_partials(got, suf_mixed, suf_log, kv_count):
    count, heads, width = suf_mixed.shape
    return pl.pallas_call(
        functools.partial(join_kernel, kv_count=kv_count),
        in_specs=[IN_VMEM] * 3,
        out_specs=[IN_VMEM] * 2,
        out_shape=[
            jax.ShapeDtypeStruct((count, heads, width), jnp.float32),
            jax.ShapeDtypeStruct((count, heads), jnp.float32),
        ],
        compiler_params=pltpu.CompilerParams(vmem_limit_bytes=SMALL_VMEM),
        name="join_partials",
    )(got, suf_mixed, suf_log)


def per_device(
    queries, prefix_keys, prefix_values, suffix_keys, suffix_values, suffix_lengths, slot_map
):
    count, heads, width = queries.shape
    kv_count = suffix_keys.shape[2]
    per_dest = count * heads // kv_count
    score_scale = 1.0 / math.sqrt(width)
    sent = layout_queries(queries, kv_count, lax.axis_size("seq"))
    got_q = lax.all_to_all(sent, ("seq", "head"), split_axis=0, concat_axis=0, tiled=True)
    keys = prefix_keys[:, 0, :]
    values = prefix_values[:, 0, :]
    far_keys = lax.ppermute(keys, "rep", [(0, 1), (1, 0)])
    far_values = lax.ppermute(values, "rep", [(0, 1), (1, 0)])
    earlier = []
    for place in range(count):
        first, last = place == 0, place == count - 1
        mixed, log, *brought = suffix_partials(
            place,
            queries,
            suffix_keys,
            suffix_values,
            suffix_lengths,
            slot_map,
            (keys, values) if first else (),
            earlier if last else (),
            score_scale,
        )
        earlier += [mixed, log]
        if first:
            near_keys, near_values = brought
    partials = prefix_partials(
        got_q.reshape(-1, width), near_keys, near_values, far_keys, far_values, per_dest, score_scale
    )
    got = lax.all_to_all(partials, ("seq", "head"), split_axis=0, concat_axis=0, tiled=True)
    return join_partials(got, mixed, log, kv_count)


def solution(mesh):
    by_request = P(("seq", "head", "rep"))
    by_block = P(("seq", "rep"), "head", None)
    placed = (by_request, by_block, by_block, by_request, by_request, by_request, by_request)
    return jax.shard_map(
        per_device,
        mesh=mesh,
        in_specs=placed,
        out_specs=(by_request, by_request),
        check_vma=False,
    )
```

```python
import functools
import math

import jax
import jax.numpy as jnp
from jax import lax
from jax.experimental import pallas as pl
from jax.experimental.pallas import tpu as pltpu
from jax.sharding import PartitionSpec as P

ROW_TILE = 256
STEP_ROWS = 512
SUF_COPIES = 4
IN_FLIGHT = 4
LANES = 128
LOG_ROWS = 8
VALUE_BITS = 15
LOG_BITS = 30
LOG2E = math.log2(math.e)
LEAST = 1e-25
PEAK_LEAST = 1e-33
NT = (((1,), (1,)), ((), ()))
PREFIX_VMEM = 24 * 1024 * 1024
SUFFIX_VMEM = 20 * 1024 * 1024
SMALL_VMEM = 8 * 1024 * 1024
IN_VMEM = pl.BlockSpec(memory_space=pltpu.VMEM)
IN_HBM = pl.BlockSpec(memory_space=pltpu.HBM)


def in_hbm(array):
    return pltpu.with_memory_space_constraint(array, pltpu.HBM)


def layout_kernel(q_hbm, sent_hbm, sems):
    count, groups, group, _ = q_hbm.shape
    repeats = sent_hbm.shape[0] // groups
    copies = [
        pltpu.make_async_copy(
            q_hbm.at[r],
            sent_hbm.at[pl.ds(s * groups, groups), pl.ds(r * group, group)],
            sems.at[s, r],
        )
        for s in range(repeats)
        for r in range(count)
    ]
    for copy in copies:
        copy.start()
    for copy in copies:
        copy.wait()


def layout_queries(queries, groups, repeats):
    count, heads, width = queries.shape
    group = heads // groups
    return pl.pallas_call(
        layout_kernel,
        in_specs=[IN_HBM],
        out_specs=IN_HBM,
        out_shape=pltpu.HBM((repeats * groups, count * group, width), queries.dtype),
        scratch_shapes=[pltpu.SemaphoreType.DMA((repeats, count))],
        compiler_params=pltpu.CompilerParams(vmem_limit_bytes=SMALL_VMEM),
        name="layout_queries",
    )(in_hbm(queries.reshape(count, groups, group, width)))


def suffix_kernel(*refs, place, carried, kv_count, score_scale):
    slot_hbm, length_hbm, q_hbm, k_hbm, v_hbm = refs[:5]
    refs = refs[5:]
    count, heads, width = q_hbm.shape
    carried_refs, refs = refs[:carried], refs[carried:]
    last = place == count - 1
    earlier, refs = (refs[: 2 * place], refs[2 * place :]) if last else ((), refs)
    mixed_ref, log_ref = refs[:2]
    brought_refs, refs = refs[2 : 2 + carried], refs[2 + carried :]
    slot_ref, length_ref, q_ref, k_buf, v_buf, score_ref, sems, small_sems = refs
    rows = k_hbm.shape[1]
    copy_rows = rows // SUF_COPIES
    copies = []
    for which, (source, target) in enumerate(((k_hbm, k_buf), (v_hbm, v_buf))):
        for c in range(SUF_COPIES):
            part = pl.ds(c * copy_rows, copy_rows)
            copies.append(
                pltpu.make_async_copy(source.at[place, part], target.at[part], sems.at[which, c])
            )
    small = [
        pltpu.make_async_copy(source, target, small_sems.at[i])
        for i, (source, target) in enumerate(
            [(slot_hbm, slot_ref), (length_hbm, length_ref), (q_hbm, q_ref)]
            + list(zip(carried_refs, brought_refs))
        )
    ]
    carries = small[3:]
    for copy in small[:3] + copies[:IN_FLIGHT]:
        copy.start()

    def arrive(i):
        copies[i].wait()
        if i + IN_FLIGHT < len(copies):
            copies[i + IN_FLIGHT].start()
        elif i + IN_FLIGHT - len(copies) < carried:
            carries[i + IN_FLIGHT - len(copies)].start()

    for copy in small[:3]:
        copy.wait()

    def request_of(slot):
        found = jnp.int32(0)
        for r in range(1, count):
            found = jnp.where(lax.rem(slot_ref[r], count) == slot, r, found)
        return found

    request = request_of(place)
    limit = length_ref[request] * kv_count
    query = q_ref[request]
    lane = lax.broadcasted_iota(jnp.int32, (heads, LANES), 1)
    group = lax.broadcasted_iota(jnp.int32, (heads, LANES), 0) // (heads // kv_count)
    lane = jnp.where((lane % kv_count) == group, lane, rows)
    peak = jnp.full((heads, LANES), -1e30, jnp.float32)
    for c in range(SUF_COPIES):
        arrive(c)
        part = lax.dot_general(
            query, k_buf[c * copy_rows : (c + 1) * copy_rows], NT, preferred_element_type=jnp.float32
        )
        for begin in range(0, copy_rows, LANES):
            at = c * copy_rows + begin
            tile = jnp.where(lane < limit - at, part[:, begin : begin + LANES], -1e30)
            score_ref[:, at : at + LANES] = tile
            peak = jnp.maximum(peak, tile)
    row_max = jnp.max(peak, axis=1, keepdims=True)
    sums = jnp.zeros((heads, LANES), jnp.float32)
    acc = jnp.zeros((heads, width), jnp.float32)
    for c in range(SUF_COPIES):
        arrive(SUF_COPIES + c)
        part = slice(c * copy_rows, (c + 1) * copy_rows)
        terms = jnp.exp2((score_ref[:, part] - row_max) * (score_scale * LOG2E))
        for begin in range(0, copy_rows, LANES):
            sums = sums + terms[:, begin : begin + LANES]
        acc = acc + jnp.dot(
            terms.astype(jnp.bfloat16), v_buf[part], preferred_element_type=jnp.float32
        )
    total = jnp.sum(sums, axis=1, keepdims=True)
    mixed = acc / total
    log = jnp.broadcast_to(row_max * score_scale + jnp.log(total), (heads, width))
    for carry in carries:
        carry.wait()
    if not last:
        mixed_ref[...] = mixed
        log_ref[...] = log
        return
    mixed_ref[request] = mixed
    log_ref[request] = log
    for slot in range(place):
        mixed_ref[request_of(slot)] = earlier[2 * slot][...]
        log_ref[request_of(slot)] = earlier[2 * slot + 1][...]


def suffix_partials(place, queries, keys, values, lengths, slots, carried, earlier, score_scale):
    count, heads, width = queries.shape
    kv_count = keys.shape[2]
    rows = keys.shape[1] * kv_count
    result = (count, heads, width) if place == count - 1 else (heads, width)
    operands = (
        slots,
        lengths,
        queries,
        keys.reshape(count, rows, width),
        values.reshape(count, rows, width),
        *carried,
    )
    return pl.pallas_call(
        functools.partial(
            suffix_kernel,
            place=place,
            carried=len(carried),
            kv_count=kv_count,
            score_scale=score_scale,
        ),
        in_specs=[IN_HBM] * len(operands) + [IN_VMEM] * len(earlier),
        out_specs=[IN_VMEM] * (2 + len(carried)),
        out_shape=[pltpu.VMEM(result, jnp.float32)] * 2
        + [pltpu.VMEM(array.shape, array.dtype) for array in carried],
        scratch_shapes=[
            pltpu.SMEM((count,), jnp.int32),
            pltpu.SMEM((count,), jnp.int32),
            pltpu.VMEM((count, heads, width), queries.dtype),
            pltpu.VMEM((rows, width), keys.dtype),
            pltpu.VMEM((rows, width), values.dtype),
            pltpu.VMEM((heads, rows), jnp.float32),
            pltpu.SemaphoreType.DMA((2, SUF_COPIES)),
            pltpu.SemaphoreType.DMA((3 + len(carried),)),
        ],
        compiler_params=pltpu.CompilerParams(vmem_limit_bytes=SUFFIX_VMEM),
        cost_estimate=pl.CostEstimate(
            flops=4 * heads * rows * width,
            bytes_accessed=4 * rows * width,
            transcendentals=heads * rows,
        ),
        name=f"suffix_attention_{place}",
    )(*map(in_hbm, operands), *earlier)


def exponent(size, least):
    return jnp.floor(jnp.log2(jnp.maximum(size, least))) + 1.0


def prefix_kernel(
    q_ref, k0_ref, v0_ref, k1_ref, v1_ref, out_hbm, out_ref, score_ref, sems, *, per_dest, score_scale
):
    width = q_ref.shape[1]
    tiles = q_ref.shape[0] // ROW_TILE
    dests = ROW_TILE // per_dest
    keys, values = (k0_ref, k1_ref), (v0_ref, v1_ref)
    units = [(tile, block) for tile in range(tiles) for block in range(2)]
    first_dest = 0 if out_hbm.shape == out_ref.shape else pl.program_id(0) * (tiles * dests)
    copies = []
    lane = lax.broadcasted_iota(jnp.int32, (per_dest, width), 1)
    row = lax.broadcasted_iota(jnp.int32, (per_dest, width), 0)
    diagonal = lane == row

    def score(unit, slot):
        tile, block = unit
        score_ref[slot] = lax.dot_general(
            q_ref[tile * ROW_TILE : (tile + 1) * ROW_TILE],
            keys[block][...],
            NT,
            preferred_element_type=jnp.float32,
        )

    score(units[0], 0)
    held = None
    for step, (tile, block) in enumerate(units):
        if step + 1 < len(units):
            score(units[step + 1], (step + 1) % 2)
        scores = score_ref[step % 2]
        row_max = jnp.max(scores, axis=1, keepdims=True)
        terms = jnp.exp2((scores - row_max) * (score_scale * LOG2E))
        total = jnp.sum(terms, axis=1, keepdims=True)
        acc = jnp.dot(
            terms.astype(jnp.bfloat16), values[block][...], preferred_element_type=jnp.float32
        )
        if block == 0:
            held = (row_max, total, acc)
            continue
        max0, total0, acc0 = held
        top = jnp.maximum(max0, row_max)
        weight0 = jnp.exp((max0 - top) * score_scale)
        weight1 = jnp.exp((row_max - top) * score_scale)
        joined = weight0 * total0 + weight1 * total
        mixed = (weight0 * acc0 + weight1 * acc) / joined
        logs = jnp.broadcast_to(top * score_scale + jnp.log(joined), (ROW_TILE, width))
        peak = jnp.max(jnp.abs(mixed), axis=1, keepdims=True)
        coded = jnp.round(mixed * jnp.exp2(VALUE_BITS - exponent(peak, PEAK_LEAST)))
        most = 2.0**VALUE_BITS - 1
        coded = jnp.clip(coded, -most, most).astype(jnp.int32)
        peaks = jnp.broadcast_to(peak, (ROW_TILE, width))
        half = per_dest // 2
        for k in range(dests):
            rows = slice(k * per_dest, (k + 1) * per_dest)
            dest = tile * dests + k
            high, low = coded[k * per_dest : k * per_dest + half], coded[k * per_dest + half : rows.stop]
            out_ref[dest, :half] = (high << 16) | (low & 0xFFFF)
            log_line = jnp.sum(jnp.where(diagonal, logs[rows], 0.0), axis=0, keepdims=True)
            peak_line = jnp.sum(jnp.where(diagonal, peaks[rows], 0.0), axis=0, keepdims=True)
            log_power = exponent(jnp.abs(log_line), LEAST)
            lines = jnp.concatenate(
                [
                    jnp.round(log_line * jnp.exp2(LOG_BITS - log_power)),
                    log_power,
                    exponent(peak_line, PEAK_LEAST),
                    jnp.zeros((LOG_ROWS - 3, width), jnp.float32),
                ],
                axis=0,
            )
            out_ref[dest, half:] = lines.astype(jnp.int32)
        ready = pl.ds(tile * dests, dests)
        copies.append(
            pltpu.make_async_copy(
                out_ref.at[ready],
                out_hbm.at[pl.ds(first_dest + tile * dests, dests)],
                sems.at[tile],
            )
        )
        copies[-1].start()
    for copy in copies:
        copy.wait()


def prefix_partials(rows_q, keys, values, far_keys, far_values, per_dest, score_scale):
    rows, width = rows_q.shape
    length = keys.shape[0]
    step_rows = min(STEP_ROWS, rows)
    dests = step_rows // per_dest
    out_rows = per_dest // 2 + LOG_ROWS
    blocked = {"in_specs": [IN_VMEM] * 5}
    if step_rows < rows:
        blocked["grid"] = (rows // step_rows,)
        blocked["in_specs"] = [pl.BlockSpec((step_rows, width), lambda i: (i, 0))]
        blocked["in_specs"] += [pl.BlockSpec((length, width), lambda i: (0, 0))] * 4
    return pl.pallas_call(
        functools.partial(prefix_kernel, per_dest=per_dest, score_scale=score_scale),
        **blocked,
        out_specs=IN_HBM,
        out_shape=pltpu.HBM((rows // per_dest, out_rows, width), jnp.int32),
        scratch_shapes=[
            pltpu.VMEM((dests, out_rows, width), jnp.int32),
            pltpu.VMEM((2, ROW_TILE, length), jnp.float32),
            pltpu.SemaphoreType.DMA((step_rows // ROW_TILE,)),
        ],
        compiler_params=pltpu.CompilerParams(vmem_limit_bytes=PREFIX_VMEM),
        cost_estimate=pl.CostEstimate(
            flops=8 * rows * length * width,
            bytes_accessed=8 * length * width + 6 * rows * width,
            transcendentals=2 * rows * length,
        ),
        name="prefix_attention",
    )(rows_q, keys, values, far_keys, far_values)


def join_kernel(got_ref, suf_ref, suf_log_ref, out_ref, log_ref, *, kv_count):
    count, heads, width = out_ref.shape
    group = heads // kv_count
    per_dest = count * group
    half = per_dest // 2
    parts = got_ref.shape[0] // kv_count
    lane = lax.broadcasted_iota(jnp.int32, (per_dest, width), 1)
    row = lax.broadcasted_iota(jnp.int32, (per_dest, width), 0)
    diagonal = lane == row

    def column(line):
        return jnp.sum(jnp.where(diagonal, line, 0.0), axis=1, keepdims=True)

    lines = [jnp.zeros((1, width), jnp.float32) for _ in range(count)]
    for g in range(kv_count):
        heads_of = slice(g * group, (g + 1) * group)
        suf_mixed = jnp.concatenate([suf_ref[r, heads_of] for r in range(count)], axis=0)
        suf_log = jnp.concatenate([suf_log_ref[r, heads_of] for r in range(count)], axis=0)
        logs, scales = [], []
        top = suf_log
        for s in range(parts):
            tail = got_ref[s * kv_count + g, half:].astype(jnp.float32)
            log_line = tail[0:1] * jnp.exp2(tail[1:2] - LOG_BITS)
            logs.append(jnp.broadcast_to(column(log_line), (per_dest, width)))
            scales.append(column(jnp.exp2(tail[2:3] - VALUE_BITS)))
            top = jnp.maximum(top, logs[-1])
        weight = jnp.exp(suf_log - top)
        acc = weight * suf_mixed
        total = weight
        for s in range(parts):
            words = got_ref[s * kv_count + g, :half]
            coded = jnp.concatenate([words >> 16, (words << 16) >> 16], axis=0)
            weight = jnp.exp(logs[s] - top)
            acc = acc + (weight * scales[s]) * coded.astype(jnp.float32)
            total = total + weight
        acc = acc / total
        logged = top + jnp.log(total)
        for r in range(count):
            rows = slice(r * group, (r + 1) * group)
            out_ref[r, heads_of] = acc[rows]
            place = lane[:group] == row[:group] + g * group
            lines[r] = lines[r] + jnp.sum(jnp.where(place, logged[rows], 0.0), axis=0, keepdims=True)
    for r in range(count):
        log_ref[r : r + 1] = lines[r][:, :heads]


def join_partials(got, suf_mixed, suf_log, kv_count):
    count, heads, width = suf_mixed.shape
    return pl.pallas_call(
        functools.partial(join_kernel, kv_count=kv_count),
        in_specs=[IN_VMEM] * 3,
        out_specs=[IN_VMEM] * 2,
        out_shape=[
            jax.ShapeDtypeStruct((count, heads, width), jnp.float32),
            jax.ShapeDtypeStruct((count, heads), jnp.float32),
        ],
        compiler_params=pltpu.CompilerParams(vmem_limit_bytes=SMALL_VMEM),
        name="join_partials",
    )(got, suf_mixed, suf_log)


def per_device(
    queries, prefix_keys, prefix_values, suffix_keys, suffix_values, suffix_lengths, slot_map
):
    count, heads, width = queries.shape
    kv_count = suffix_keys.shape[2]
    per_dest = count * heads // kv_count
    score_scale = 1.0 / math.sqrt(width)
    sent = layout_queries(queries, kv_count, lax.axis_size("seq"))
    got_q = lax.all_to_all(sent, ("seq", "head"), split_axis=0, concat_axis=0, tiled=True)
    keys = prefix_keys[:, 0, :]
    values = prefix_values[:, 0, :]
    far_keys = lax.ppermute(keys, "rep", [(0, 1), (1, 0)])
    far_values = lax.ppermute(values, "rep", [(0, 1), (1, 0)])
    earlier = []
    for place in range(count):
        first, last = place == 0, place == count - 1
        mixed, log, *brought = suffix_partials(
            place,
            queries,
            suffix_keys,
            suffix_values,
            suffix_lengths,
            slot_map,
            (keys, values) if first else (),
            earlier if last else (),
            score_scale,
        )
        earlier += [mixed, log]
        if first:
            near_keys, near_values = brought
    partials = prefix_partials(
        got_q.reshape(-1, width), near_keys, near_values, far_keys, far_values, per_dest, score_scale
    )
    got = lax.all_to_all(partials, ("seq", "head"), split_axis=0, concat_axis=0, tiled=True)
    return join_partials(got, mixed, log, kv_count)


def solution(mesh):
    by_request = P(("seq", "head", "rep"))
    by_block = P(("seq", "rep"), "head", None)
    placed = (by_request, by_block, by_block, by_request, by_request, by_request, by_request)
    return jax.shard_map(
        per_device,
        mesh=mesh,
        in_specs=placed,
        out_specs=(by_request, by_request),
        check_vma=False,
    )
```

```python
import functools
import math

import jax
import jax.numpy as jnp
from jax import lax
from jax.experimental import pallas as pl
from jax.experimental.pallas import tpu as pltpu
from jax.sharding import PartitionSpec as P

ROW_TILE = 128
STEP_ROWS = 512
SUF_COPIES = 4
IN_FLIGHT = 4
LANES = 128
LOG_ROWS = 8
VALUE_BITS = 15
LOG_BITS = 30
LOG2E = math.log2(math.e)
LEAST = 1e-25
PEAK_LEAST = 1e-33
NT = (((1,), (1,)), ((), ()))
PREFIX_VMEM = 14 * 1024 * 1024
SUFFIX_VMEM = 20 * 1024 * 1024
SMALL_VMEM = 8 * 1024 * 1024
IN_VMEM = pl.BlockSpec(memory_space=pltpu.VMEM)
IN_HBM = pl.BlockSpec(memory_space=pltpu.HBM)


def in_hbm(array):
    return pltpu.with_memory_space_constraint(array, pltpu.HBM)


def layout_kernel(*refs, carried):
    q_hbm, carried_refs, refs = refs[0], refs[1 : 1 + carried], refs[1 + carried :]
    sent_hbm, brought_refs = refs[0], refs[1 : 1 + carried]
    buf, in_sems, out_sems, carry_sems = refs[1 + carried :]
    groups, rows, _ = buf.shape
    count = q_hbm.shape[0]
    group = rows // count
    repeats = sent_hbm.shape[0] // groups
    reads = [
        pltpu.make_async_copy(
            q_hbm.at[r, pl.ds(g * group, group)], buf.at[g, pl.ds(r * group, group)], in_sems.at[g, r]
        )
        for g in range(groups)
        for r in range(count)
    ]
    carries = [
        pltpu.make_async_copy(source, target, carry_sems.at[i])
        for i, (source, target) in enumerate(zip(carried_refs, brought_refs))
    ]
    for copy in reads + carries:
        copy.start()
    for read in reads:
        read.wait()
    writes = [
        pltpu.make_async_copy(buf, sent_hbm.at[pl.ds(s * groups, groups)], out_sems.at[s])
        for s in range(repeats)
    ]
    for write in writes:
        write.start()
    for copy in writes + carries:
        copy.wait()


def layout_queries(queries, groups, repeats, carried):
    count, heads, width = queries.shape
    rows = count * heads // groups
    return pl.pallas_call(
        functools.partial(layout_kernel, carried=len(carried)),
        in_specs=[IN_HBM] * (1 + len(carried)),
        out_specs=[IN_HBM] + [IN_VMEM] * len(carried),
        out_shape=[pltpu.HBM((repeats * groups, rows, width), queries.dtype)]
        + [pltpu.VMEM(array.shape, array.dtype) for array in carried],
        scratch_shapes=[
            pltpu.VMEM((groups, rows, width), queries.dtype),
            pltpu.SemaphoreType.DMA((groups, count)),
            pltpu.SemaphoreType.DMA((repeats,)),
            pltpu.SemaphoreType.DMA((len(carried),)),
        ],
        compiler_params=pltpu.CompilerParams(vmem_limit_bytes=SMALL_VMEM),
        name="layout_queries",
    )(in_hbm(queries), *map(in_hbm, carried))


def suffix_kernel(*refs, place, kv_count, score_scale):
    slot_hbm, length_hbm, q_hbm, k_hbm, v_hbm = refs[:5]
    refs = refs[5:]
    count, heads, width = q_hbm.shape
    last = place == count - 1
    earlier, refs = (refs[: 2 * place], refs[2 * place :]) if last else ((), refs)
    mixed_ref, log_ref = refs[:2]
    slot_ref, length_ref, q_ref, k_buf, v_buf, score_ref, sems, small_sems = refs[2:]
    rows = k_hbm.shape[1]
    copy_rows = rows // SUF_COPIES
    copies = []
    for which, (source, target) in enumerate(((k_hbm, k_buf), (v_hbm, v_buf))):
        for c in range(SUF_COPIES):
            part = pl.ds(c * copy_rows, copy_rows)
            copies.append(
                pltpu.make_async_copy(source.at[place, part], target.at[part], sems.at[which, c])
            )
    small = [
        pltpu.make_async_copy(source, target, small_sems.at[i])
        for i, (source, target) in enumerate(
            [(slot_hbm, slot_ref), (length_hbm, length_ref), (q_hbm, q_ref)]
        )
    ]
    for copy in small + copies[:IN_FLIGHT]:
        copy.start()

    def arrive(i):
        copies[i].wait()
        if i + IN_FLIGHT < len(copies):
            copies[i + IN_FLIGHT].start()

    for copy in small:
        copy.wait()

    def request_of(slot):
        found = jnp.int32(0)
        for r in range(1, count):
            found = jnp.where(lax.rem(slot_ref[r], count) == slot, r, found)
        return found

    request = request_of(place)
    limit = length_ref[request] * kv_count
    query = q_ref[request]
    lane = lax.broadcasted_iota(jnp.int32, (heads, LANES), 1)
    group = lax.broadcasted_iota(jnp.int32, (heads, LANES), 0) // (heads // kv_count)
    lane = jnp.where((lane % kv_count) == group, lane, rows)
    peak = jnp.full((heads, LANES), -1e30, jnp.float32)
    for c in range(SUF_COPIES):
        arrive(c)
        part = lax.dot_general(
            query, k_buf[c * copy_rows : (c + 1) * copy_rows], NT, preferred_element_type=jnp.float32
        )
        for begin in range(0, copy_rows, LANES):
            at = c * copy_rows + begin
            tile = jnp.where(lane < limit - at, part[:, begin : begin + LANES], -1e30)
            score_ref[:, at : at + LANES] = tile
            peak = jnp.maximum(peak, tile)
    row_max = jnp.max(peak, axis=1, keepdims=True)
    sums = jnp.zeros((heads, LANES), jnp.float32)
    acc = jnp.zeros((heads, width), jnp.float32)
    for c in range(SUF_COPIES):
        arrive(SUF_COPIES + c)
        part = slice(c * copy_rows, (c + 1) * copy_rows)
        terms = jnp.exp2((score_ref[:, part] - row_max) * (score_scale * LOG2E))
        for begin in range(0, copy_rows, LANES):
            sums = sums + terms[:, begin : begin + LANES]
        acc = acc + jnp.dot(
            terms.astype(jnp.bfloat16), v_buf[part], preferred_element_type=jnp.float32
        )
    total = jnp.sum(sums, axis=1, keepdims=True)
    mixed = acc / total
    log = jnp.broadcast_to(row_max * score_scale + jnp.log(total), (heads, width))
    if not last:
        mixed_ref[...] = mixed
        log_ref[...] = log
        return
    mixed_ref[request] = mixed
    log_ref[request] = log
    for slot in range(place):
        mixed_ref[request_of(slot)] = earlier[2 * slot][...]
        log_ref[request_of(slot)] = earlier[2 * slot + 1][...]


def suffix_partials(place, queries, keys, values, lengths, slots, earlier, score_scale):
    count, heads, width = queries.shape
    kv_count = keys.shape[2]
    rows = keys.shape[1] * kv_count
    result = (count, heads, width) if place == count - 1 else (heads, width)
    operands = (
        slots,
        lengths,
        queries,
        keys.reshape(count, rows, width),
        values.reshape(count, rows, width),
    )
    return pl.pallas_call(
        functools.partial(
            suffix_kernel,
            place=place,
            kv_count=kv_count,
            score_scale=score_scale,
        ),
        in_specs=[IN_HBM] * len(operands) + [IN_VMEM] * len(earlier),
        out_specs=[IN_VMEM] * 2,
        out_shape=[pltpu.VMEM(result, jnp.float32)] * 2,
        scratch_shapes=[
            pltpu.SMEM((count,), jnp.int32),
            pltpu.SMEM((count,), jnp.int32),
            pltpu.VMEM((count, heads, width), queries.dtype),
            pltpu.VMEM((rows, width), keys.dtype),
            pltpu.VMEM((rows, width), values.dtype),
            pltpu.VMEM((heads, rows), jnp.float32),
            pltpu.SemaphoreType.DMA((2, SUF_COPIES)),
            pltpu.SemaphoreType.DMA((3,)),
        ],
        compiler_params=pltpu.CompilerParams(vmem_limit_bytes=SUFFIX_VMEM),
        cost_estimate=pl.CostEstimate(
            flops=4 * heads * rows * width,
            bytes_accessed=4 * rows * width,
            transcendentals=heads * rows,
        ),
        name=f"suffix_attention_{place}",
    )(*map(in_hbm, operands), *earlier)


def exponent(size, least):
    return jnp.floor(jnp.log2(jnp.maximum(size, least))) + 1.0


def prefix_kernel(
    q_ref, k0_ref, v0_ref, k1_ref, v1_ref, _, out_hbm, out_ref, score_ref, sems, *, per_dest, score_scale
):
    width = q_ref.shape[1]
    tiles = q_ref.shape[0] // ROW_TILE
    dests = ROW_TILE // per_dest
    keys, values = (k0_ref, k1_ref), (v0_ref, v1_ref)
    units = [(tile, block) for tile in range(tiles) for block in range(2)]
    first_dest = 0 if out_hbm.shape == out_ref.shape else pl.program_id(0) * (tiles * dests)
    copies = []
    lane = lax.broadcasted_iota(jnp.int32, (per_dest, width), 1)
    row = lax.broadcasted_iota(jnp.int32, (per_dest, width), 0)
    diagonal = lane == row

    def score(unit, slot):
        tile, block = unit
        score_ref[slot] = lax.dot_general(
            q_ref[tile * ROW_TILE : (tile + 1) * ROW_TILE],
            keys[block][...],
            NT,
            preferred_element_type=jnp.float32,
        )

    score(units[0], 0)
    held = None
    for step, (tile, block) in enumerate(units):
        if step + 1 < len(units):
            score(units[step + 1], (step + 1) % 2)
        scores = score_ref[step % 2]
        row_max = jnp.max(scores, axis=1, keepdims=True)
        terms = jnp.exp2((scores - row_max) * (score_scale * LOG2E))
        total = jnp.sum(terms, axis=1, keepdims=True)
        acc = jnp.dot(
            terms.astype(jnp.bfloat16), values[block][...], preferred_element_type=jnp.float32
        )
        if block == 0:
            held = (row_max, total, acc)
            continue
        max0, total0, acc0 = held
        top = jnp.maximum(max0, row_max)
        weight0 = jnp.exp((max0 - top) * score_scale)
        weight1 = jnp.exp((row_max - top) * score_scale)
        joined = weight0 * total0 + weight1 * total
        mixed = (weight0 * acc0 + weight1 * acc) / joined
        logs = jnp.broadcast_to(top * score_scale + jnp.log(joined), (ROW_TILE, width))
        peak = jnp.max(jnp.abs(mixed), axis=1, keepdims=True)
        coded = jnp.round(mixed * jnp.exp2(VALUE_BITS - exponent(peak, PEAK_LEAST)))
        most = 2.0**VALUE_BITS - 1
        coded = jnp.clip(coded, -most, most).astype(jnp.int32)
        peaks = jnp.broadcast_to(peak, (ROW_TILE, width))
        half = per_dest // 2
        for k in range(dests):
            rows = slice(k * per_dest, (k + 1) * per_dest)
            dest = tile * dests + k
            high, low = coded[k * per_dest : k * per_dest + half], coded[k * per_dest + half : rows.stop]
            out_ref[dest, :half] = (high << 16) | (low & 0xFFFF)
            log_line = jnp.sum(jnp.where(diagonal, logs[rows], 0.0), axis=0, keepdims=True)
            peak_line = jnp.sum(jnp.where(diagonal, peaks[rows], 0.0), axis=0, keepdims=True)
            log_power = exponent(jnp.abs(log_line), LEAST)
            lines = jnp.concatenate(
                [
                    jnp.round(log_line * jnp.exp2(LOG_BITS - log_power)),
                    log_power,
                    exponent(peak_line, PEAK_LEAST),
                    jnp.zeros((LOG_ROWS - 3, width), jnp.float32),
                ],
                axis=0,
            )
            out_ref[dest, half:] = lines.astype(jnp.int32)
        ready = pl.ds(tile * dests, dests)
        copies.append(
            pltpu.make_async_copy(
                out_ref.at[ready],
                out_hbm.at[pl.ds(first_dest + tile * dests, dests)],
                sems.at[tile],
            )
        )
        copies[-1].start()
    for copy in copies:
        copy.wait()


def prefix_partials(rows_q, keys, values, far_keys, far_values, after, per_dest, score_scale):
    rows, width = rows_q.shape
    length = keys.shape[0]
    step_rows = min(STEP_ROWS, rows)
    dests = step_rows // per_dest
    out_rows = per_dest // 2 + LOG_ROWS
    blocked = {"in_specs": [IN_VMEM] * 5}
    if step_rows < rows:
        blocked["grid"] = (rows // step_rows,)
        blocked["in_specs"] = [pl.BlockSpec((step_rows, width), lambda i: (i, 0))]
        blocked["in_specs"] += [pl.BlockSpec((length, width), lambda i: (0, 0))] * 4
    blocked["in_specs"] += [pl.BlockSpec(memory_space=pl.ANY)]
    return pl.pallas_call(
        functools.partial(prefix_kernel, per_dest=per_dest, score_scale=score_scale),
        **blocked,
        out_specs=IN_HBM,
        out_shape=pltpu.HBM((rows // per_dest, out_rows, width), jnp.int32),
        scratch_shapes=[
            pltpu.VMEM((dests, out_rows, width), jnp.int32),
            pltpu.VMEM((2, ROW_TILE, length), jnp.float32),
            pltpu.SemaphoreType.DMA((step_rows // ROW_TILE,)),
        ],
        compiler_params=pltpu.CompilerParams(vmem_limit_bytes=PREFIX_VMEM),
        cost_estimate=pl.CostEstimate(
            flops=8 * rows * length * width,
            bytes_accessed=8 * length * width + 6 * rows * width,
            transcendentals=2 * rows * length,
        ),
        name="prefix_attention",
    )(rows_q, keys, values, far_keys, far_values, after)


def join_kernel(got_ref, suf_ref, suf_log_ref, out_ref, log_ref, *, kv_count):
    count, heads, width = out_ref.shape
    group = heads // kv_count
    per_dest = count * group
    half = per_dest // 2
    parts = got_ref.shape[0] // kv_count
    lane = lax.broadcasted_iota(jnp.int32, (per_dest, width), 1)
    row = lax.broadcasted_iota(jnp.int32, (per_dest, width), 0)
    diagonal = lane == row

    def column(line):
        return jnp.sum(jnp.where(diagonal, line, 0.0), axis=1, keepdims=True)

    lines = [jnp.zeros((1, width), jnp.float32) for _ in range(count)]
    for g in range(kv_count):
        heads_of = slice(g * group, (g + 1) * group)
        suf_mixed = jnp.concatenate([suf_ref[r, heads_of] for r in range(count)], axis=0)
        suf_log = jnp.concatenate([suf_log_ref[r, heads_of] for r in range(count)], axis=0)
        logs, scales = [], []
        top = suf_log
        for s in range(parts):
            tail = got_ref[s * kv_count + g, half:].astype(jnp.float32)
            log_line = tail[0:1] * jnp.exp2(tail[1:2] - LOG_BITS)
            logs.append(jnp.broadcast_to(column(log_line), (per_dest, width)))
            scales.append(column(jnp.exp2(tail[2:3] - VALUE_BITS)))
            top = jnp.maximum(top, logs[-1])
        weight = jnp.exp(suf_log - top)
        acc = weight * suf_mixed
        total = weight
        for s in range(parts):
            words = got_ref[s * kv_count + g, :half]
            coded = jnp.concatenate([words >> 16, (words << 16) >> 16], axis=0)
            weight = jnp.exp(logs[s] - top)
            acc = acc + (weight * scales[s]) * coded.astype(jnp.float32)
            total = total + weight
        acc = acc / total
        logged = top + jnp.log(total)
        for r in range(count):
            rows = slice(r * group, (r + 1) * group)
            out_ref[r, heads_of] = acc[rows]
            place = lane[:group] == row[:group] + g * group
            lines[r] = lines[r] + jnp.sum(jnp.where(place, logged[rows], 0.0), axis=0, keepdims=True)
    for r in range(count):
        log_ref[r : r + 1] = lines[r][:, :heads]


def join_partials(got, suf_mixed, suf_log, kv_count):
    count, heads, width = suf_mixed.shape
    return pl.pallas_call(
        functools.partial(join_kernel, kv_count=kv_count),
        in_specs=[IN_VMEM] * 3,
        out_specs=[IN_VMEM] * 2,
        out_shape=[
            jax.ShapeDtypeStruct((count, heads, width), jnp.float32),
            jax.ShapeDtypeStruct((count, heads), jnp.float32),
        ],
        compiler_params=pltpu.CompilerParams(vmem_limit_bytes=SMALL_VMEM),
        name="join_partials",
    )(got, suf_mixed, suf_log)


def per_device(
    queries, prefix_keys, prefix_values, suffix_keys, suffix_values, suffix_lengths, slot_map
):
    count, heads, width = queries.shape
    kv_count = suffix_keys.shape[2]
    per_dest = count * heads // kv_count
    score_scale = 1.0 / math.sqrt(width)
    sent, near_keys, near_values = layout_queries(
        queries, kv_count, lax.axis_size("seq"), (prefix_keys[:, 0, :], prefix_values[:, 0, :])
    )
    got_q = lax.all_to_all(sent, ("seq", "head"), split_axis=0, concat_axis=0, tiled=True)
    far_keys = lax.ppermute(near_keys, "rep", [(0, 1), (1, 0)])
    far_values = lax.ppermute(near_values, "rep", [(0, 1), (1, 0)])
    earlier = []
    for place in range(count):
        mixed, log = suffix_partials(
            place,
            queries,
            suffix_keys,
            suffix_values,
            suffix_lengths,
            slot_map,
            earlier if place == count - 1 else (),
            score_scale,
        )
        earlier += [mixed, log]
    partials = prefix_partials(
        got_q.reshape(-1, width),
        near_keys,
        near_values,
        far_keys,
        far_values,
        earlier[0],
        per_dest,
        score_scale,
    )
    got = lax.all_to_all(partials, ("seq", "head"), split_axis=0, concat_axis=0, tiled=True)
    return join_partials(got, mixed, log, kv_count)


def solution(mesh):
    by_request = P(("seq", "head", "rep"))
    by_block = P(("seq", "rep"), "head", None)
    placed = (by_request, by_block, by_block, by_request, by_request, by_request, by_request)
    return jax.shard_map(
        per_device,
        mesh=mesh,
        in_specs=placed,
        out_specs=(by_request, by_request),
        check_vma=False,
    )
```

```python
import functools
import math

import jax
import jax.numpy as jnp
from jax import lax
from jax.experimental import pallas as pl
from jax.experimental.pallas import tpu as pltpu
from jax.sharding import PartitionSpec as P

ROW_TILE = 128
STEP_ROWS = 512
SUF_COPIES = 4
IN_FLIGHT = 4
LANES = 128
LOG_ROWS = 8
VALUE_BITS = 15
LOG_BITS = 30
LOG2E = math.log2(math.e)
LEAST = 1e-25
PEAK_LEAST = 1e-33
NT = (((1,), (1,)), ((), ()))
PREFIX_VMEM = 14 * 1024 * 1024
SUFFIX_VMEM = 20 * 1024 * 1024
SMALL_VMEM = 8 * 1024 * 1024
IN_VMEM = pl.BlockSpec(memory_space=pltpu.VMEM)
IN_HBM = pl.BlockSpec(memory_space=pltpu.HBM)


def in_hbm(array):
    return pltpu.with_memory_space_constraint(array, pltpu.HBM)


def layout_kernel(*refs, carried):
    q_hbm, carried_refs, refs = refs[0], refs[1 : 1 + carried], refs[1 + carried :]
    sent_hbm, brought_refs = refs[0], refs[1 : 1 + carried]
    buf, in_sems, out_sems, carry_sems = refs[1 + carried :]
    groups, rows, _ = buf.shape
    count = q_hbm.shape[0]
    group = rows // count
    repeats = sent_hbm.shape[0] // groups
    reads = [
        pltpu.make_async_copy(
            q_hbm.at[r, pl.ds(g * group, group)], buf.at[g, pl.ds(r * group, group)], in_sems.at[g, r]
        )
        for g in range(groups)
        for r in range(count)
    ]
    carries = [
        pltpu.make_async_copy(source, target, carry_sems.at[i])
        for i, (source, target) in enumerate(zip(carried_refs, brought_refs))
    ]
    for copy in reads + carries:
        copy.start()
    for read in reads:
        read.wait()
    writes = [
        pltpu.make_async_copy(buf, sent_hbm.at[pl.ds(s * groups, groups)], out_sems.at[s])
        for s in range(repeats)
    ]
    for write in writes:
        write.start()
    for copy in writes + carries:
        copy.wait()


def layout_queries(queries, groups, repeats, carried):
    count, heads, width = queries.shape
    rows = count * heads // groups
    return pl.pallas_call(
        functools.partial(layout_kernel, carried=len(carried)),
        in_specs=[IN_HBM] * (1 + len(carried)),
        out_specs=[IN_HBM] + [IN_VMEM] * len(carried),
        out_shape=[pltpu.HBM((repeats * groups, rows, width), queries.dtype)]
        + [pltpu.VMEM(array.shape, array.dtype) for array in carried],
        scratch_shapes=[
            pltpu.VMEM((groups, rows, width), queries.dtype),
            pltpu.SemaphoreType.DMA((groups, count)),
            pltpu.SemaphoreType.DMA((repeats,)),
            pltpu.SemaphoreType.DMA((len(carried),)),
        ],
        compiler_params=pltpu.CompilerParams(vmem_limit_bytes=SMALL_VMEM),
        name="layout_queries",
    )(in_hbm(queries), *map(in_hbm, carried))


def suffix_kernel(*refs, place, kv_count, score_scale):
    slot_hbm, length_hbm, q_hbm, k_hbm, v_hbm = refs[:5]
    refs = refs[5:]
    count, heads, width = q_hbm.shape
    last = place == count - 1
    earlier, refs = (refs[: 2 * place], refs[2 * place :]) if last else ((), refs)
    mixed_ref, log_ref = refs[:2]
    slot_ref, length_ref, q_ref, k_buf, v_buf, score_ref, sems, small_sems = refs[2:]
    rows = k_hbm.shape[1]
    copy_rows = rows // SUF_COPIES
    copies = []
    for which, (source, target) in enumerate(((k_hbm, k_buf), (v_hbm, v_buf))):
        for c in range(SUF_COPIES):
            part = pl.ds(c * copy_rows, copy_rows)
            copies.append(
                pltpu.make_async_copy(source.at[place, part], target.at[part], sems.at[which, c])
            )
    small = [
        pltpu.make_async_copy(source, target, small_sems.at[i])
        for i, (source, target) in enumerate(
            [(slot_hbm, slot_ref), (length_hbm, length_ref), (q_hbm, q_ref)]
        )
    ]
    for copy in small + copies[:IN_FLIGHT]:
        copy.start()

    def arrive(i):
        copies[i].wait()
        if i + IN_FLIGHT < len(copies):
            copies[i + IN_FLIGHT].start()

    for copy in small:
        copy.wait()

    def request_of(slot):
        found = jnp.int32(0)
        for r in range(1, count):
            found = jnp.where(lax.rem(slot_ref[r], count) == slot, r, found)
        return found

    request = request_of(place)
    limit = length_ref[request] * kv_count
    query = q_ref[request]
    lane = lax.broadcasted_iota(jnp.int32, (heads, LANES), 1)
    group = lax.broadcasted_iota(jnp.int32, (heads, LANES), 0) // (heads // kv_count)
    lane = jnp.where((lane % kv_count) == group, lane, rows)
    peak = jnp.full((heads, LANES), -1e30, jnp.float32)
    for c in range(SUF_COPIES):
        arrive(c)
        part = lax.dot_general(
            query, k_buf[c * copy_rows : (c + 1) * copy_rows], NT, preferred_element_type=jnp.float32
        )
        for begin in range(0, copy_rows, LANES):
            at = c * copy_rows + begin
            tile = jnp.where(lane < limit - at, part[:, begin : begin + LANES], -1e30)
            score_ref[:, at : at + LANES] = tile
            peak = jnp.maximum(peak, tile)
    row_max = jnp.max(peak, axis=1, keepdims=True)
    sums = jnp.zeros((heads, LANES), jnp.float32)
    acc = jnp.zeros((heads, width), jnp.float32)
    for c in range(SUF_COPIES):
        arrive(SUF_COPIES + c)
        part = slice(c * copy_rows, (c + 1) * copy_rows)
        terms = jnp.exp2((score_ref[:, part] - row_max) * (score_scale * LOG2E))
        for begin in range(0, copy_rows, LANES):
            sums = sums + terms[:, begin : begin + LANES]
        acc = acc + jnp.dot(
            terms.astype(jnp.bfloat16), v_buf[part], preferred_element_type=jnp.float32
        )
    total = jnp.sum(sums, axis=1, keepdims=True)
    mixed = acc / total
    log = jnp.broadcast_to(row_max * score_scale + jnp.log(total), (heads, width))
    if not last:
        mixed_ref[...] = mixed
        log_ref[...] = log
        return
    mixed_ref[request] = mixed
    log_ref[request] = log
    for slot in range(place):
        mixed_ref[request_of(slot)] = earlier[2 * slot][...]
        log_ref[request_of(slot)] = earlier[2 * slot + 1][...]


def suffix_partials(place, queries, keys, values, lengths, slots, earlier, score_scale):
    count, heads, width = queries.shape
    kv_count = keys.shape[2]
    rows = keys.shape[1] * kv_count
    result = (count, heads, width) if place == count - 1 else (heads, width)
    operands = (
        slots,
        lengths,
        queries,
        keys.reshape(count, rows, width),
        values.reshape(count, rows, width),
    )
    return pl.pallas_call(
        functools.partial(
            suffix_kernel,
            place=place,
            kv_count=kv_count,
            score_scale=score_scale,
        ),
        in_specs=[IN_HBM] * len(operands) + [IN_VMEM] * len(earlier),
        out_specs=[IN_VMEM] * 2,
        out_shape=[pltpu.VMEM(result, jnp.float32)] * 2,
        scratch_shapes=[
            pltpu.SMEM((count,), jnp.int32),
            pltpu.SMEM((count,), jnp.int32),
            pltpu.VMEM((count, heads, width), queries.dtype),
            pltpu.VMEM((rows, width), keys.dtype),
            pltpu.VMEM((rows, width), values.dtype),
            pltpu.VMEM((heads, rows), jnp.float32),
            pltpu.SemaphoreType.DMA((2, SUF_COPIES)),
            pltpu.SemaphoreType.DMA((3,)),
        ],
        compiler_params=pltpu.CompilerParams(vmem_limit_bytes=SUFFIX_VMEM),
        cost_estimate=pl.CostEstimate(
            flops=4 * heads * rows * width,
            bytes_accessed=4 * rows * width,
            transcendentals=heads * rows,
        ),
        name=f"suffix_attention_{place}",
    )(*map(in_hbm, operands), *earlier)


def exponent(size, least):
    return jnp.floor(jnp.log2(jnp.maximum(size, least))) + 1.0


def prefix_kernel(
    q_ref, k0_ref, v0_ref, k1_ref, v1_ref, _, out_hbm, out_ref, score_ref, sems, *, per_dest, score_scale
):
    width = q_ref.shape[1]
    tiles = q_ref.shape[0] // ROW_TILE
    dests = ROW_TILE // per_dest
    keys, values = (k0_ref, k1_ref), (v0_ref, v1_ref)
    units = [(tile, block) for tile in range(tiles) for block in range(2)]
    first_dest = 0 if out_hbm.shape == out_ref.shape else pl.program_id(0) * (tiles * dests)
    copies = []
    lane = lax.broadcasted_iota(jnp.int32, (per_dest, width), 1)
    row = lax.broadcasted_iota(jnp.int32, (per_dest, width), 0)
    diagonal = lane == row

    def score(unit, slot):
        tile, block = unit
        score_ref[slot] = lax.dot_general(
            q_ref[tile * ROW_TILE : (tile + 1) * ROW_TILE],
            keys[block][...],
            NT,
            preferred_element_type=jnp.float32,
        )

    score(units[0], 0)
    held = None
    for step, (tile, block) in enumerate(units):
        if step + 1 < len(units):
            score(units[step + 1], (step + 1) % 2)
        scores = score_ref[step % 2]
        row_max = jnp.max(scores, axis=1, keepdims=True)
        terms = jnp.exp2((scores - row_max) * (score_scale * LOG2E))
        total = jnp.sum(terms, axis=1, keepdims=True)
        acc = jnp.dot(
            terms.astype(jnp.bfloat16), values[block][...], preferred_element_type=jnp.float32
        )
        if block == 0:
            held = (row_max, total, acc)
            continue
        max0, total0, acc0 = held
        top = jnp.maximum(max0, row_max)
        weight0 = jnp.exp((max0 - top) * score_scale)
        weight1 = jnp.exp((row_max - top) * score_scale)
        joined = weight0 * total0 + weight1 * total
        mixed = (weight0 * acc0 + weight1 * acc) / joined
        logs = jnp.broadcast_to(top * score_scale + jnp.log(joined), (ROW_TILE, width))
        peak = jnp.max(jnp.abs(mixed), axis=1, keepdims=True)
        coded = jnp.round(mixed * jnp.exp2(VALUE_BITS - exponent(peak, PEAK_LEAST)))
        most = 2.0**VALUE_BITS - 1
        coded = jnp.clip(coded, -most, most).astype(jnp.int32)
        peaks = jnp.broadcast_to(peak, (ROW_TILE, width))
        half = per_dest // 2
        for k in range(dests):
            rows = slice(k * per_dest, (k + 1) * per_dest)
            dest = tile * dests + k
            high, low = coded[k * per_dest : k * per_dest + half], coded[k * per_dest + half : rows.stop]
            out_ref[dest, :half] = (high << 16) | (low & 0xFFFF)
            log_line = jnp.sum(jnp.where(diagonal, logs[rows], 0.0), axis=0, keepdims=True)
            peak_line = jnp.sum(jnp.where(diagonal, peaks[rows], 0.0), axis=0, keepdims=True)
            log_power = exponent(jnp.abs(log_line), LEAST)
            lines = jnp.concatenate(
                [
                    jnp.round(log_line * jnp.exp2(LOG_BITS - log_power)),
                    log_power,
                    exponent(peak_line, PEAK_LEAST),
                    jnp.zeros((LOG_ROWS - 3, width), jnp.float32),
                ],
                axis=0,
            )
            out_ref[dest, half:] = lines.astype(jnp.int32)
        ready = pl.ds(tile * dests, dests)
        copies.append(
            pltpu.make_async_copy(
                out_ref.at[ready],
                out_hbm.at[pl.ds(first_dest + tile * dests, dests)],
                sems.at[tile],
            )
        )
        copies[-1].start()
    for copy in copies:
        copy.wait()


def prefix_partials(rows_q, keys, values, far_keys, far_values, after, per_dest, score_scale):
    rows, width = rows_q.shape
    length = keys.shape[0]
    step_rows = min(STEP_ROWS, rows)
    dests = step_rows // per_dest
    out_rows = per_dest // 2 + LOG_ROWS
    blocked = {"in_specs": [IN_VMEM] * 5}
    if step_rows < rows:
        blocked["grid"] = (rows // step_rows,)
        blocked["in_specs"] = [pl.BlockSpec((step_rows, width), lambda i: (i, 0))]
        blocked["in_specs"] += [pl.BlockSpec((length, width), lambda i: (0, 0))] * 4
    blocked["in_specs"] += [pl.BlockSpec(memory_space=pl.ANY)]
    return pl.pallas_call(
        functools.partial(prefix_kernel, per_dest=per_dest, score_scale=score_scale),
        **blocked,
        out_specs=IN_HBM,
        out_shape=pltpu.HBM((rows // per_dest, out_rows, width), jnp.int32),
        scratch_shapes=[
            pltpu.VMEM((dests, out_rows, width), jnp.int32),
            pltpu.VMEM((2, ROW_TILE, length), jnp.float32),
            pltpu.SemaphoreType.DMA((step_rows // ROW_TILE,)),
        ],
        compiler_params=pltpu.CompilerParams(vmem_limit_bytes=PREFIX_VMEM),
        cost_estimate=pl.CostEstimate(
            flops=8 * rows * length * width,
            bytes_accessed=8 * length * width + 6 * rows * width,
            transcendentals=2 * rows * length,
        ),
        name="prefix_attention",
    )(rows_q, keys, values, far_keys, far_values, after)


def join_kernel(got_ref, suf_ref, suf_log_ref, out_ref, log_ref, *, kv_count):
    count, heads, width = out_ref.shape
    group = heads // kv_count
    per_dest = count * group
    half = per_dest // 2
    parts = got_ref.shape[0] // kv_count
    lane = lax.broadcasted_iota(jnp.int32, (per_dest, width), 1)
    row = lax.broadcasted_iota(jnp.int32, (per_dest, width), 0)
    diagonal = lane == row

    def column(line):
        return jnp.sum(jnp.where(diagonal, line, 0.0), axis=1, keepdims=True)

    lines = [jnp.zeros((1, width), jnp.float32) for _ in range(count)]
    for g in range(kv_count):
        heads_of = slice(g * group, (g + 1) * group)
        suf_mixed = jnp.concatenate([suf_ref[r, heads_of] for r in range(count)], axis=0)
        suf_log = jnp.concatenate([suf_log_ref[r, heads_of] for r in range(count)], axis=0)
        logs, scales = [], []
        top = suf_log
        for s in range(parts):
            tail = got_ref[s * kv_count + g, half:].astype(jnp.float32)
            log_line = tail[0:1] * jnp.exp2(tail[1:2] - LOG_BITS)
            logs.append(jnp.broadcast_to(column(log_line), (per_dest, width)))
            scales.append(column(jnp.exp2(tail[2:3] - VALUE_BITS)))
            top = jnp.maximum(top, logs[-1])
        weight = jnp.exp(suf_log - top)
        acc = weight * suf_mixed
        total = weight
        for s in range(parts):
            words = got_ref[s * kv_count + g, :half]
            coded = jnp.concatenate([words >> 16, (words << 16) >> 16], axis=0)
            weight = jnp.exp(logs[s] - top)
            acc = acc + (weight * scales[s]) * coded.astype(jnp.float32)
            total = total + weight
        acc = acc / total
        logged = top + jnp.log(total)
        for r in range(count):
            rows = slice(r * group, (r + 1) * group)
            out_ref[r, heads_of] = acc[rows]
            place = lane[:group] == row[:group] + g * group
            lines[r] = lines[r] + jnp.sum(jnp.where(place, logged[rows], 0.0), axis=0, keepdims=True)
    for r in range(count):
        log_ref[r : r + 1] = lines[r][:, :heads]


def join_partials(got, suf_mixed, suf_log, kv_count):
    count, heads, width = suf_mixed.shape
    return pl.pallas_call(
        functools.partial(join_kernel, kv_count=kv_count),
        in_specs=[IN_VMEM] * 3,
        out_specs=[IN_VMEM] * 2,
        out_shape=[
            jax.ShapeDtypeStruct((count, heads, width), jnp.float32),
            jax.ShapeDtypeStruct((count, heads), jnp.float32),
        ],
        compiler_params=pltpu.CompilerParams(vmem_limit_bytes=SMALL_VMEM),
        name="join_partials",
    )(got, suf_mixed, suf_log)


def exchange(pieces):
    seq, head, rep = lax.axis_size("seq"), lax.axis_size("head"), lax.axis_size("rep")
    order = seq_order(seq)
    groups = [
        [(s * head + h) * rep + r for s in order for h in range(head)] for r in range(rep)
    ]
    return lax.all_to_all(
        pieces,
        ("seq", "head", "rep"),
        split_axis=0,
        concat_axis=0,
        axis_index_groups=groups,
        tiled=True,
    )


def seq_order(count):
    middle = count // 2
    return [middle] + [s for s in range(count) if s != middle]


def per_device(
    queries, prefix_keys, prefix_values, suffix_keys, suffix_values, suffix_lengths, slot_map
):
    count, heads, width = queries.shape
    kv_count = suffix_keys.shape[2]
    per_dest = count * heads // kv_count
    score_scale = 1.0 / math.sqrt(width)
    sent, near_keys, near_values = layout_queries(
        queries, kv_count, lax.axis_size("seq"), (prefix_keys[:, 0, :], prefix_values[:, 0, :])
    )
    got_q = exchange(sent)
    far_keys = lax.ppermute(near_keys, "rep", [(0, 1), (1, 0)])
    far_values = lax.ppermute(near_values, "rep", [(0, 1), (1, 0)])
    earlier = []
    for place in range(count):
        mixed, log = suffix_partials(
            place,
            queries,
            suffix_keys,
            suffix_values,
            suffix_lengths,
            slot_map,
            earlier if place == count - 1 else (),
            score_scale,
        )
        earlier += [mixed, log]
    partials = prefix_partials(
        got_q.reshape(-1, width),
        near_keys,
        near_values,
        far_keys,
        far_values,
        earlier[0],
        per_dest,
        score_scale,
    )
    got = exchange(partials)
    return join_partials(got, mixed, log, kv_count)


def solution(mesh):
    by_request = P(("seq", "head", "rep"))
    by_block = P(("seq", "rep"), "head", None)
    placed = (by_request, by_block, by_block, by_request, by_request, by_request, by_request)
    return jax.shard_map(
        per_device,
        mesh=mesh,
        in_specs=placed,
        out_specs=(by_request, by_request),
        check_vma=False,
    )
```

```python
import functools
import math

import jax
import jax.numpy as jnp
from jax import lax
from jax.experimental import pallas as pl
from jax.experimental.pallas import tpu as pltpu
from jax.sharding import PartitionSpec as P

ROW_TILE = 128
STEP_ROWS = 512
SUF_COPIES = 4
IN_FLIGHT = 4
LANES = 128
LOG_ROWS = 8
VALUE_BITS = 15
LOG_BITS = 30
LOG2E = math.log2(math.e)
LEAST = 1e-25
PEAK_LEAST = 1e-33
NT = (((1,), (1,)), ((), ()))
PREFIX_VMEM = 14 * 1024 * 1024
SUFFIX_VMEM = 20 * 1024 * 1024
SMALL_VMEM = 8 * 1024 * 1024
IN_VMEM = pl.BlockSpec(memory_space=pltpu.VMEM)
IN_HBM = pl.BlockSpec(memory_space=pltpu.HBM)


def in_hbm(array):
    return pltpu.with_memory_space_constraint(array, pltpu.HBM)


def layout_kernel(*refs, carried):
    q_hbm, carried_refs, refs = refs[0], refs[1 : 1 + carried], refs[1 + carried :]
    sent_hbm, brought_refs = refs[0], refs[1 : 1 + carried]
    buf, in_sems, out_sems, carry_sems = refs[1 + carried :]
    groups, rows, _ = buf.shape
    count = q_hbm.shape[0]
    group = rows // count
    repeats = sent_hbm.shape[0] // groups
    reads = [
        pltpu.make_async_copy(
            q_hbm.at[r, pl.ds(g * group, group)],
            buf.at[groups - 1 - g, pl.ds(r * group, group)],
            in_sems.at[g, r],
        )
        for g in range(groups)
        for r in range(count)
    ]
    carries = [
        pltpu.make_async_copy(source, target, carry_sems.at[i])
        for i, (source, target) in enumerate(zip(carried_refs, brought_refs))
    ]
    for copy in reads + carries:
        copy.start()
    for read in reads:
        read.wait()
    writes = [
        pltpu.make_async_copy(buf, sent_hbm.at[pl.ds(s * groups, groups)], out_sems.at[s])
        for s in range(repeats)
    ]
    for write in writes:
        write.start()
    for copy in writes + carries:
        copy.wait()


def layout_queries(queries, groups, repeats, carried):
    count, heads, width = queries.shape
    rows = count * heads // groups
    return pl.pallas_call(
        functools.partial(layout_kernel, carried=len(carried)),
        in_specs=[IN_HBM] * (1 + len(carried)),
        out_specs=[IN_HBM] + [IN_VMEM] * len(carried),
        out_shape=[pltpu.HBM((repeats * groups, rows, width), queries.dtype)]
        + [pltpu.VMEM(array.shape, array.dtype) for array in carried],
        scratch_shapes=[
            pltpu.VMEM((groups, rows, width), queries.dtype),
            pltpu.SemaphoreType.DMA((groups, count)),
            pltpu.SemaphoreType.DMA((repeats,)),
            pltpu.SemaphoreType.DMA((len(carried),)),
        ],
        compiler_params=pltpu.CompilerParams(vmem_limit_bytes=SMALL_VMEM),
        name="layout_queries",
    )(in_hbm(queries), *map(in_hbm, carried))


def suffix_kernel(*refs, place, kv_count, score_scale):
    slot_hbm, length_hbm, q_hbm, k_hbm, v_hbm = refs[:5]
    refs = refs[5:]
    count, heads, width = q_hbm.shape
    last = place == count - 1
    earlier, refs = (refs[: 2 * place], refs[2 * place :]) if last else ((), refs)
    mixed_ref, log_ref = refs[:2]
    slot_ref, length_ref, q_ref, k_buf, v_buf, score_ref, sems, small_sems = refs[2:]
    rows = k_hbm.shape[1]
    copy_rows = rows // SUF_COPIES
    copies = []
    for which, (source, target) in enumerate(((k_hbm, k_buf), (v_hbm, v_buf))):
        for c in range(SUF_COPIES):
            part = pl.ds(c * copy_rows, copy_rows)
            copies.append(
                pltpu.make_async_copy(source.at[place, part], target.at[part], sems.at[which, c])
            )
    small = [
        pltpu.make_async_copy(source, target, small_sems.at[i])
        for i, (source, target) in enumerate(
            [(slot_hbm, slot_ref), (length_hbm, length_ref), (q_hbm, q_ref)]
        )
    ]
    for copy in small + copies[:IN_FLIGHT]:
        copy.start()

    def arrive(i):
        copies[i].wait()
        if i + IN_FLIGHT < len(copies):
            copies[i + IN_FLIGHT].start()

    for copy in small:
        copy.wait()

    def request_of(slot):
        found = jnp.int32(0)
        for r in range(1, count):
            found = jnp.where(lax.rem(slot_ref[r], count) == slot, r, found)
        return found

    request = request_of(place)
    limit = length_ref[request] * kv_count
    query = q_ref[request]
    lane = lax.broadcasted_iota(jnp.int32, (heads, LANES), 1)
    group = lax.broadcasted_iota(jnp.int32, (heads, LANES), 0) // (heads // kv_count)
    lane = jnp.where((lane % kv_count) == group, lane, rows)
    peak = jnp.full((heads, LANES), -1e30, jnp.float32)
    for c in range(SUF_COPIES):
        arrive(c)
        part = lax.dot_general(
            query, k_buf[c * copy_rows : (c + 1) * copy_rows], NT, preferred_element_type=jnp.float32
        )
        for begin in range(0, copy_rows, LANES):
            at = c * copy_rows + begin
            tile = jnp.where(lane < limit - at, part[:, begin : begin + LANES], -1e30)
            score_ref[:, at : at + LANES] = tile
            peak = jnp.maximum(peak, tile)
    row_max = jnp.max(peak, axis=1, keepdims=True)
    sums = jnp.zeros((heads, LANES), jnp.float32)
    acc = jnp.zeros((heads, width), jnp.float32)
    for c in range(SUF_COPIES):
        arrive(SUF_COPIES + c)
        part = slice(c * copy_rows, (c + 1) * copy_rows)
        terms = jnp.exp2((score_ref[:, part] - row_max) * (score_scale * LOG2E))
        for begin in range(0, copy_rows, LANES):
            sums = sums + terms[:, begin : begin + LANES]
        acc = acc + jnp.dot(
            terms.astype(jnp.bfloat16), v_buf[part], preferred_element_type=jnp.float32
        )
    total = jnp.sum(sums, axis=1, keepdims=True)
    mixed = acc / total
    log = jnp.broadcast_to(row_max * score_scale + jnp.log(total), (heads, width))
    if not last:
        mixed_ref[...] = mixed
        log_ref[...] = log
        return
    mixed_ref[request] = mixed
    log_ref[request] = log
    for slot in range(place):
        mixed_ref[request_of(slot)] = earlier[2 * slot][...]
        log_ref[request_of(slot)] = earlier[2 * slot + 1][...]


def suffix_partials(place, queries, keys, values, lengths, slots, earlier, score_scale):
    count, heads, width = queries.shape
    kv_count = keys.shape[2]
    rows = keys.shape[1] * kv_count
    result = (count, heads, width) if place == count - 1 else (heads, width)
    operands = (
        slots,
        lengths,
        queries,
        keys.reshape(count, rows, width),
        values.reshape(count, rows, width),
    )
    return pl.pallas_call(
        functools.partial(
            suffix_kernel,
            place=place,
            kv_count=kv_count,
            score_scale=score_scale,
        ),
        in_specs=[IN_HBM] * len(operands) + [IN_VMEM] * len(earlier),
        out_specs=[IN_VMEM] * 2,
        out_shape=[pltpu.VMEM(result, jnp.float32)] * 2,
        scratch_shapes=[
            pltpu.SMEM((count,), jnp.int32),
            pltpu.SMEM((count,), jnp.int32),
            pltpu.VMEM((count, heads, width), queries.dtype),
            pltpu.VMEM((rows, width), keys.dtype),
            pltpu.VMEM((rows, width), values.dtype),
            pltpu.VMEM((heads, rows), jnp.float32),
            pltpu.SemaphoreType.DMA((2, SUF_COPIES)),
            pltpu.SemaphoreType.DMA((3,)),
        ],
        compiler_params=pltpu.CompilerParams(vmem_limit_bytes=SUFFIX_VMEM),
        cost_estimate=pl.CostEstimate(
            flops=4 * heads * rows * width,
            bytes_accessed=4 * rows * width * (16 if place == 0 else 1),
            transcendentals=heads * rows,
        ),
        name=f"suffix_attention_{place}",
    )(*map(in_hbm, operands), *earlier)


def exponent(size, least):
    return jnp.floor(jnp.log2(jnp.maximum(size, least))) + 1.0


def prefix_kernel(
    q_ref, k0_ref, v0_ref, k1_ref, v1_ref, _, out_hbm, out_ref, score_ref, sems, *, per_dest, turn, score_scale
):
    width = q_ref.shape[1]
    tiles = q_ref.shape[0] // ROW_TILE
    dests = ROW_TILE // per_dest
    keys, values = (k0_ref, k1_ref), (v0_ref, v1_ref)
    units = [(tile, block) for tile in range(tiles) for block in range(2)]
    places = out_hbm.shape[0] // dests
    first_place = turn + (0 if out_hbm.shape == out_ref.shape else pl.program_id(0) * tiles)
    copies = []
    lane = lax.broadcasted_iota(jnp.int32, (per_dest, width), 1)
    row = lax.broadcasted_iota(jnp.int32, (per_dest, width), 0)
    diagonal = lane == row

    def score(unit, slot):
        tile, block = unit
        score_ref[slot] = lax.dot_general(
            q_ref[tile * ROW_TILE : (tile + 1) * ROW_TILE],
            keys[block][...],
            NT,
            preferred_element_type=jnp.float32,
        )

    score(units[0], 0)
    held = None
    for step, (tile, block) in enumerate(units):
        if step + 1 < len(units):
            score(units[step + 1], (step + 1) % 2)
        scores = score_ref[step % 2]
        row_max = jnp.max(scores, axis=1, keepdims=True)
        terms = jnp.exp2((scores - row_max) * (score_scale * LOG2E))
        total = jnp.sum(terms, axis=1, keepdims=True)
        acc = jnp.dot(
            terms.astype(jnp.bfloat16), values[block][...], preferred_element_type=jnp.float32
        )
        if block == 0:
            held = (row_max, total, acc)
            continue
        max0, total0, acc0 = held
        top = jnp.maximum(max0, row_max)
        weight0 = jnp.exp((max0 - top) * score_scale)
        weight1 = jnp.exp((row_max - top) * score_scale)
        joined = weight0 * total0 + weight1 * total
        mixed = (weight0 * acc0 + weight1 * acc) / joined
        logs = jnp.broadcast_to(top * score_scale + jnp.log(joined), (ROW_TILE, width))
        peak = jnp.max(jnp.abs(mixed), axis=1, keepdims=True)
        coded = jnp.round(mixed * jnp.exp2(VALUE_BITS - exponent(peak, PEAK_LEAST)))
        most = 2.0**VALUE_BITS - 1
        coded = jnp.clip(coded, -most, most).astype(jnp.int32)
        peaks = jnp.broadcast_to(peak, (ROW_TILE, width))
        half = per_dest // 2
        for k in range(dests):
            rows = slice(k * per_dest, (k + 1) * per_dest)
            dest = tile * dests + k
            high, low = coded[k * per_dest : k * per_dest + half], coded[k * per_dest + half : rows.stop]
            out_ref[dest, :half] = (high << 16) | (low & 0xFFFF)
            log_line = jnp.sum(jnp.where(diagonal, logs[rows], 0.0), axis=0, keepdims=True)
            peak_line = jnp.sum(jnp.where(diagonal, peaks[rows], 0.0), axis=0, keepdims=True)
            log_power = exponent(jnp.abs(log_line), LEAST)
            lines = jnp.concatenate(
                [
                    jnp.round(log_line * jnp.exp2(LOG_BITS - log_power)),
                    log_power,
                    exponent(peak_line, PEAK_LEAST),
                    jnp.zeros((LOG_ROWS - 3, width), jnp.float32),
                ],
                axis=0,
            )
            out_ref[dest, half:] = lines.astype(jnp.int32)
        ready = pl.ds(tile * dests, dests)
        copies.append(
            pltpu.make_async_copy(
                out_ref.at[ready],
                out_hbm.at[pl.ds(lax.rem(first_place + tile, places) * dests, dests)],
                sems.at[tile],
            )
        )
        copies[-1].start()
    for copy in copies:
        copy.wait()


def prefix_partials(
    rows_q, keys, values, far_keys, far_values, after, per_dest, turn, score_scale
):
    rows, width = rows_q.shape
    length = keys.shape[0]
    step_rows = min(STEP_ROWS, rows)
    dests = step_rows // per_dest
    out_rows = per_dest // 2 + LOG_ROWS
    blocked = {"in_specs": [IN_VMEM] * 5}
    if step_rows < rows:
        blocked["grid"] = (rows // step_rows,)
        blocked["in_specs"] = [pl.BlockSpec((step_rows, width), lambda i: (i, 0))]
        blocked["in_specs"] += [pl.BlockSpec((length, width), lambda i: (0, 0))] * 4
    blocked["in_specs"] += [pl.BlockSpec(memory_space=pl.ANY)]
    return pl.pallas_call(
        functools.partial(
            prefix_kernel, per_dest=per_dest, turn=turn, score_scale=score_scale
        ),
        **blocked,
        out_specs=IN_HBM,
        out_shape=pltpu.HBM((rows // per_dest, out_rows, width), jnp.int32),
        scratch_shapes=[
            pltpu.VMEM((dests, out_rows, width), jnp.int32),
            pltpu.VMEM((2, ROW_TILE, length), jnp.float32),
            pltpu.SemaphoreType.DMA((step_rows // ROW_TILE,)),
        ],
        compiler_params=pltpu.CompilerParams(vmem_limit_bytes=PREFIX_VMEM),
        cost_estimate=pl.CostEstimate(
            flops=8 * rows * length * width,
            bytes_accessed=8 * length * width + 6 * rows * width,
            transcendentals=2 * rows * length,
        ),
        name="prefix_attention",
    )(rows_q, keys, values, far_keys, far_values, after)


def join_kernel(got_ref, suf_ref, suf_log_ref, out_ref, log_ref, *, kv_count):
    count, heads, width = out_ref.shape
    group = heads // kv_count
    per_dest = count * group
    half = per_dest // 2
    parts = got_ref.shape[0] // kv_count
    lane = lax.broadcasted_iota(jnp.int32, (per_dest, width), 1)
    row = lax.broadcasted_iota(jnp.int32, (per_dest, width), 0)
    diagonal = lane == row

    def column(line):
        return jnp.sum(jnp.where(diagonal, line, 0.0), axis=1, keepdims=True)

    lines = [jnp.zeros((1, width), jnp.float32) for _ in range(count)]
    for place in range(kv_count):
        g = kv_count - 1 - place
        heads_of = slice(g * group, (g + 1) * group)
        suf_mixed = jnp.concatenate([suf_ref[r, heads_of] for r in range(count)], axis=0)
        suf_log = jnp.concatenate([suf_log_ref[r, heads_of] for r in range(count)], axis=0)
        logs, scales = [], []
        top = suf_log
        for s in range(parts):
            tail = got_ref[s * kv_count + place, half:].astype(jnp.float32)
            log_line = tail[0:1] * jnp.exp2(tail[1:2] - LOG_BITS)
            logs.append(jnp.broadcast_to(column(log_line), (per_dest, width)))
            scales.append(column(jnp.exp2(tail[2:3] - VALUE_BITS)))
            top = jnp.maximum(top, logs[-1])
        weight = jnp.exp(suf_log - top)
        acc = weight * suf_mixed
        total = weight
        for s in range(parts):
            words = got_ref[s * kv_count + place, :half]
            coded = jnp.concatenate([words >> 16, (words << 16) >> 16], axis=0)
            weight = jnp.exp(logs[s] - top)
            acc = acc + (weight * scales[s]) * coded.astype(jnp.float32)
            total = total + weight
        acc = acc / total
        logged = top + jnp.log(total)
        for r in range(count):
            rows = slice(r * group, (r + 1) * group)
            out_ref[r, heads_of] = acc[rows]
            spot = lane[:group] == row[:group] + g * group
            lines[r] = lines[r] + jnp.sum(jnp.where(spot, logged[rows], 0.0), axis=0, keepdims=True)
    for r in range(count):
        log_ref[r : r + 1] = lines[r][:, :heads]


def join_partials(got, suf_mixed, suf_log, kv_count):
    count, heads, width = suf_mixed.shape
    return pl.pallas_call(
        functools.partial(join_kernel, kv_count=kv_count),
        in_specs=[IN_VMEM] * 3,
        out_specs=[IN_VMEM] * 2,
        out_shape=[
            jax.ShapeDtypeStruct((count, heads, width), jnp.float32),
            jax.ShapeDtypeStruct((count, heads), jnp.float32),
        ],
        compiler_params=pltpu.CompilerParams(vmem_limit_bytes=SMALL_VMEM),
        name="join_partials",
    )(got, suf_mixed, suf_log)


def exchange(pieces, first):
    seq, head, rep = lax.axis_size("seq"), lax.axis_size("head"), lax.axis_size("rep")
    order = [(first - s) % seq for s in range(seq)]
    groups = [
        [(s * head + h) * rep + r for s in order for h in reversed(range(head))]
        for r in range(rep)
    ]
    return lax.all_to_all(
        pieces,
        ("seq", "head", "rep"),
        split_axis=0,
        concat_axis=0,
        axis_index_groups=groups,
        tiled=True,
    )


def per_device(
    queries, prefix_keys, prefix_values, suffix_keys, suffix_values, suffix_lengths, slot_map
):
    count, heads, width = queries.shape
    kv_count = suffix_keys.shape[2]
    per_dest = count * heads // kv_count
    score_scale = 1.0 / math.sqrt(width)
    sent, near_keys, near_values = layout_queries(
        queries, kv_count, lax.axis_size("seq"), (prefix_keys[:, 0, :], prefix_values[:, 0, :])
    )
    seq = lax.axis_size("seq")
    last, middle = seq - 1, seq // 2
    got_q = exchange(sent, last)
    far_keys = lax.ppermute(near_keys, "rep", [(0, 1), (1, 0)])
    far_values = lax.ppermute(near_values, "rep", [(0, 1), (1, 0)])
    earlier = []
    for place in range(count):
        mixed, log = suffix_partials(
            place,
            queries,
            suffix_keys,
            suffix_values,
            suffix_lengths,
            slot_map,
            earlier if place == count - 1 else (),
            score_scale,
        )
        earlier += [mixed, log]
    partials = prefix_partials(
        got_q.reshape(-1, width),
        near_keys,
        near_values,
        far_keys,
        far_values,
        earlier[0],
        per_dest,
        (middle - last) % seq,
        score_scale,
    )
    got = exchange(partials, middle)
    return join_partials(got, mixed, log, kv_count)


def solution(mesh):
    by_request = P(("seq", "head", "rep"))
    by_block = P(("seq", "rep"), "head", None)
    placed = (by_request, by_block, by_block, by_request, by_request, by_request, by_request)
    return jax.shard_map(
        per_device,
        mesh=mesh,
        in_specs=placed,
        out_specs=(by_request, by_request),
        check_vma=False,
    )
```

```python
import functools
import math

import jax
import jax.numpy as jnp
from jax import lax
from jax.experimental import pallas as pl
from jax.experimental.pallas import tpu as pltpu
from jax.sharding import PartitionSpec as P

ROW_TILE = 128
STEP_ROWS = 512
SUF_COPIES = 8
AT_ONCE = 4
LANES = 128
LOG_ROWS = 8
VALUE_BITS = 15
LOG_BITS = 30
LOG2E = math.log2(math.e)
LEAST = 1e-25
PEAK_LEAST = 1e-33
NT = (((1,), (1,)), ((), ()))
PREFIX_VMEM = 14 * 1024 * 1024
SUFFIX_VMEM = 20 * 1024 * 1024
SMALL_VMEM = 8 * 1024 * 1024
IN_VMEM = pl.BlockSpec(memory_space=pltpu.VMEM)
IN_HBM = pl.BlockSpec(memory_space=pltpu.HBM)


def in_hbm(array):
    return pltpu.with_memory_space_constraint(array, pltpu.HBM)


def layout_kernel(*refs, carried):
    q_hbm, carried_refs, refs = refs[0], refs[1 : 1 + carried], refs[1 + carried :]
    sent_hbm, brought_refs = refs[0], refs[1 : 1 + carried]
    buf, in_sems, out_sems, carry_sems = refs[1 + carried :]
    groups, rows, _ = buf.shape
    count = q_hbm.shape[0]
    group = rows // count
    repeats = sent_hbm.shape[0] // groups
    reads = [
        pltpu.make_async_copy(
            q_hbm.at[r, pl.ds(g * group, group)],
            buf.at[groups - 1 - g, pl.ds(r * group, group)],
            in_sems.at[g, r],
        )
        for g in range(groups)
        for r in range(count)
    ]
    carries = [
        pltpu.make_async_copy(source, target, carry_sems.at[i])
        for i, (source, target) in enumerate(zip(carried_refs, brought_refs))
    ]
    for copy in reads + carries:
        copy.start()
    for read in reads:
        read.wait()
    writes = [
        pltpu.make_async_copy(buf, sent_hbm.at[pl.ds(s * groups, groups)], out_sems.at[s])
        for s in range(repeats)
    ]
    for write in writes:
        write.start()
    for copy in writes + carries:
        copy.wait()


def layout_queries(queries, groups, repeats, carried):
    count, heads, width = queries.shape
    rows = count * heads // groups
    return pl.pallas_call(
        functools.partial(layout_kernel, carried=len(carried)),
        in_specs=[IN_HBM] * (1 + len(carried)),
        out_specs=[IN_HBM] + [IN_VMEM] * len(carried),
        out_shape=[pltpu.HBM((repeats * groups, rows, width), queries.dtype)]
        + [pltpu.VMEM(array.shape, array.dtype) for array in carried],
        scratch_shapes=[
            pltpu.VMEM((groups, rows, width), queries.dtype),
            pltpu.SemaphoreType.DMA((groups, count)),
            pltpu.SemaphoreType.DMA((repeats,)),
            pltpu.SemaphoreType.DMA((len(carried),)),
        ],
        compiler_params=pltpu.CompilerParams(vmem_limit_bytes=SMALL_VMEM),
        name="layout_queries",
    )(in_hbm(queries), *map(in_hbm, carried))


def suffix_kernel(*refs, place, kv_count, score_scale):
    slot_hbm, length_hbm, q_hbm, k_hbm, v_hbm = refs[:5]
    refs = refs[5:]
    count, heads, width = q_hbm.shape
    last = place == count - 1
    earlier, refs = (refs[: 2 * place], refs[2 * place :]) if last else ((), refs)
    mixed_ref, log_ref = refs[:2]
    slot_ref, length_ref, q_ref, k_buf, v_buf, score_ref, peak_ref, sum_ref, acc_ref, sems, small_sems = refs[2:]
    rows = k_hbm.shape[1]
    copy_rows = rows // SUF_COPIES
    copies = []
    for which, (source, target) in enumerate(((k_hbm, k_buf), (v_hbm, v_buf))):
        for c in range(SUF_COPIES):
            part = pl.ds(c * copy_rows, copy_rows)
            copies.append(
                pltpu.make_async_copy(source.at[place, part], target.at[part], sems.at[which, c])
            )
    k_copies, v_copies = copies[:SUF_COPIES], copies[SUF_COPIES:]
    small = [
        pltpu.make_async_copy(source, target, small_sems.at[i])
        for i, (source, target) in enumerate(
            [(slot_hbm, slot_ref), (length_hbm, length_ref), (q_hbm, q_ref)]
        )
    ]
    for copy in small + k_copies[:AT_ONCE]:
        copy.start()
    for copy in small:
        copy.wait()

    def request_of(slot):
        found = jnp.int32(0)
        for r in range(1, count):
            found = jnp.where(lax.rem(slot_ref[r], count) == slot, r, found)
        return found

    request = request_of(place)
    limit = length_ref[request] * kv_count

    def live(c):
        return limit > c * copy_rows

    for c in range(AT_ONCE, SUF_COPIES):
        pl.when(live(c))(k_copies[c].start)
    query = q_ref[request]
    lane = lax.broadcasted_iota(jnp.int32, (heads, LANES), 1)
    group = lax.broadcasted_iota(jnp.int32, (heads, LANES), 0) // (heads // kv_count)
    lane = jnp.where((lane % kv_count) == group, lane, rows)
    peak_ref[...] = jnp.full((heads, LANES), -1e30, jnp.float32)
    for c in range(SUF_COPIES):
        if c < AT_ONCE:
            k_copies[c].wait()

        @pl.when(live(c))
        def _(c=c):
            if c >= AT_ONCE:
                k_copies[c].wait()
            v_copies[c].start()
            part = lax.dot_general(
                query, k_buf[c * copy_rows : (c + 1) * copy_rows], NT, preferred_element_type=jnp.float32
            )
            peak = peak_ref[...]
            for begin in range(0, copy_rows, LANES):
                at = c * copy_rows + begin
                tile = jnp.where(lane < limit - at, part[:, begin : begin + LANES], -1e30)
                score_ref[:, at : at + LANES] = tile
                peak = jnp.maximum(peak, tile)
            peak_ref[...] = peak

    row_max = jnp.max(peak_ref[...], axis=1, keepdims=True)
    sum_ref[...] = jnp.zeros((heads, LANES), jnp.float32)
    acc_ref[...] = jnp.zeros((heads, width), jnp.float32)
    for c in range(SUF_COPIES):

        @pl.when(live(c))
        def _(c=c):
            v_copies[c].wait()
            part = slice(c * copy_rows, (c + 1) * copy_rows)
            terms = jnp.exp2((score_ref[:, part] - row_max) * (score_scale * LOG2E))
            sums = sum_ref[...]
            for begin in range(0, copy_rows, LANES):
                sums = sums + terms[:, begin : begin + LANES]
            sum_ref[...] = sums
            acc_ref[...] += jnp.dot(
                terms.astype(jnp.bfloat16), v_buf[part], preferred_element_type=jnp.float32
            )

    sums, acc = sum_ref[...], acc_ref[...]
    total = jnp.sum(sums, axis=1, keepdims=True)
    mixed = acc / total
    log = jnp.broadcast_to(row_max * score_scale + jnp.log(total), (heads, width))
    if not last:
        mixed_ref[...] = mixed
        log_ref[...] = log
        return
    mixed_ref[request] = mixed
    log_ref[request] = log
    for slot in range(place):
        mixed_ref[request_of(slot)] = earlier[2 * slot][...]
        log_ref[request_of(slot)] = earlier[2 * slot + 1][...]


def suffix_partials(place, queries, keys, values, lengths, slots, earlier, score_scale):
    count, heads, width = queries.shape
    kv_count = keys.shape[2]
    rows = keys.shape[1] * kv_count
    result = (count, heads, width) if place == count - 1 else (heads, width)
    operands = (
        slots,
        lengths,
        queries,
        keys.reshape(count, rows, width),
        values.reshape(count, rows, width),
    )
    return pl.pallas_call(
        functools.partial(
            suffix_kernel,
            place=place,
            kv_count=kv_count,
            score_scale=score_scale,
        ),
        in_specs=[IN_HBM] * len(operands) + [IN_VMEM] * len(earlier),
        out_specs=[IN_VMEM] * 2,
        out_shape=[pltpu.VMEM(result, jnp.float32)] * 2,
        scratch_shapes=[
            pltpu.SMEM((count,), jnp.int32),
            pltpu.SMEM((count,), jnp.int32),
            pltpu.VMEM((count, heads, width), queries.dtype),
            pltpu.VMEM((rows, width), keys.dtype),
            pltpu.VMEM((rows, width), values.dtype),
            pltpu.VMEM((heads, rows), jnp.float32),
            pltpu.VMEM((heads, LANES), jnp.float32),
            pltpu.VMEM((heads, LANES), jnp.float32),
            pltpu.VMEM((heads, width), jnp.float32),
            pltpu.SemaphoreType.DMA((2, SUF_COPIES)),
            pltpu.SemaphoreType.DMA((3,)),
        ],
        compiler_params=pltpu.CompilerParams(vmem_limit_bytes=SUFFIX_VMEM),
        cost_estimate=pl.CostEstimate(
            flops=4 * heads * rows * width,
            bytes_accessed=4 * rows * width,
            transcendentals=heads * rows,
        ),
        name=f"suffix_attention_{place}",
    )(*map(in_hbm, operands), *earlier)


def exponent(size, least):
    return jnp.floor(jnp.log2(jnp.maximum(size, least))) + 1.0


def prefix_kernel(
    q_ref, k0_ref, v0_ref, k1_ref, v1_ref, _, out_hbm, out_ref, score_ref, sems, *, per_dest, score_scale
):
    width = q_ref.shape[1]
    tiles = q_ref.shape[0] // ROW_TILE
    dests = ROW_TILE // per_dest
    keys, values = (k0_ref, k1_ref), (v0_ref, v1_ref)
    units = [(tile, block) for tile in range(tiles) for block in range(2)]
    first_dest = 0 if out_hbm.shape == out_ref.shape else pl.program_id(0) * (tiles * dests)
    copies = []
    lane = lax.broadcasted_iota(jnp.int32, (per_dest, width), 1)
    row = lax.broadcasted_iota(jnp.int32, (per_dest, width), 0)
    diagonal = lane == row

    def score(unit, slot):
        tile, block = unit
        score_ref[slot] = lax.dot_general(
            q_ref[tile * ROW_TILE : (tile + 1) * ROW_TILE],
            keys[block][...],
            NT,
            preferred_element_type=jnp.float32,
        )

    score(units[0], 0)
    held = None
    for step, (tile, block) in enumerate(units):
        if step + 1 < len(units):
            score(units[step + 1], (step + 1) % 2)
        scores = score_ref[step % 2]
        row_max = jnp.max(scores, axis=1, keepdims=True)
        terms = jnp.exp2((scores - row_max) * (score_scale * LOG2E))
        total = jnp.sum(terms, axis=1, keepdims=True)
        acc = jnp.dot(
            terms.astype(jnp.bfloat16), values[block][...], preferred_element_type=jnp.float32
        )
        if block == 0:
            held = (row_max, total, acc)
            continue
        max0, total0, acc0 = held
        top = jnp.maximum(max0, row_max)
        weight0 = jnp.exp((max0 - top) * score_scale)
        weight1 = jnp.exp((row_max - top) * score_scale)
        joined = weight0 * total0 + weight1 * total
        mixed = (weight0 * acc0 + weight1 * acc) / joined
        logs = jnp.broadcast_to(top * score_scale + jnp.log(joined), (ROW_TILE, width))
        peak = jnp.max(jnp.abs(mixed), axis=1, keepdims=True)
        coded = jnp.round(mixed * jnp.exp2(VALUE_BITS - exponent(peak, PEAK_LEAST)))
        most = 2.0**VALUE_BITS - 1
        coded = jnp.clip(coded, -most, most).astype(jnp.int32)
        peaks = jnp.broadcast_to(peak, (ROW_TILE, width))
        half = per_dest // 2
        for k in range(dests):
            rows = slice(k * per_dest, (k + 1) * per_dest)
            dest = tile * dests + k
            high, low = coded[k * per_dest : k * per_dest + half], coded[k * per_dest + half : rows.stop]
            out_ref[dest, :half] = (high << 16) | (low & 0xFFFF)
            log_line = jnp.sum(jnp.where(diagonal, logs[rows], 0.0), axis=0, keepdims=True)
            peak_line = jnp.sum(jnp.where(diagonal, peaks[rows], 0.0), axis=0, keepdims=True)
            log_power = exponent(jnp.abs(log_line), LEAST)
            lines = jnp.concatenate(
                [
                    jnp.round(log_line * jnp.exp2(LOG_BITS - log_power)),
                    log_power,
                    exponent(peak_line, PEAK_LEAST),
                    jnp.zeros((LOG_ROWS - 3, width), jnp.float32),
                ],
                axis=0,
            )
            out_ref[dest, half:] = lines.astype(jnp.int32)
        ready = pl.ds(tile * dests, dests)
        copies.append(
            pltpu.make_async_copy(
                out_ref.at[ready],
                out_hbm.at[pl.ds(first_dest + tile * dests, dests)],
                sems.at[tile],
            )
        )
        copies[-1].start()
    for copy in copies:
        copy.wait()


def prefix_partials(
    rows_q, keys, values, far_keys, far_values, after, per_dest, score_scale
):
    rows, width = rows_q.shape
    length = keys.shape[0]
    step_rows = min(STEP_ROWS, rows)
    dests = step_rows // per_dest
    out_rows = per_dest // 2 + LOG_ROWS
    blocked = {"in_specs": [IN_VMEM] * 5}
    if step_rows < rows:
        blocked["grid"] = (rows // step_rows,)
        blocked["in_specs"] = [pl.BlockSpec((step_rows, width), lambda i: (i, 0))]
        blocked["in_specs"] += [pl.BlockSpec((length, width), lambda i: (0, 0))] * 4
    blocked["in_specs"] += [pl.BlockSpec(memory_space=pl.ANY)]
    return pl.pallas_call(
        functools.partial(
            prefix_kernel, per_dest=per_dest, score_scale=score_scale
        ),
        **blocked,
        out_specs=IN_HBM,
        out_shape=pltpu.HBM((rows // per_dest, out_rows, width), jnp.int32),
        scratch_shapes=[
            pltpu.VMEM((dests, out_rows, width), jnp.int32),
            pltpu.VMEM((2, ROW_TILE, length), jnp.float32),
            pltpu.SemaphoreType.DMA((step_rows // ROW_TILE,)),
        ],
        compiler_params=pltpu.CompilerParams(vmem_limit_bytes=PREFIX_VMEM),
        cost_estimate=pl.CostEstimate(
            flops=8 * rows * length * width,
            bytes_accessed=8 * length * width + 6 * rows * width,
            transcendentals=2 * rows * length,
        ),
        name="prefix_attention",
    )(rows_q, keys, values, far_keys, far_values, after)


def join_kernel(got_ref, suf_ref, suf_log_ref, out_ref, log_ref, *, kv_count):
    count, heads, width = out_ref.shape
    group = heads // kv_count
    per_dest = count * group
    half = per_dest // 2
    parts = got_ref.shape[0] // kv_count
    lane = lax.broadcasted_iota(jnp.int32, (per_dest, width), 1)
    row = lax.broadcasted_iota(jnp.int32, (per_dest, width), 0)
    diagonal = lane == row

    def column(line):
        return jnp.sum(jnp.where(diagonal, line, 0.0), axis=1, keepdims=True)

    lines = [jnp.zeros((1, width), jnp.float32) for _ in range(count)]
    for place in range(kv_count):
        g = kv_count - 1 - place
        heads_of = slice(g * group, (g + 1) * group)
        suf_mixed = jnp.concatenate([suf_ref[r, heads_of] for r in range(count)], axis=0)
        suf_log = jnp.concatenate([suf_log_ref[r, heads_of] for r in range(count)], axis=0)
        logs, scales = [], []
        top = suf_log
        for s in range(parts):
            tail = got_ref[s * kv_count + place, half:].astype(jnp.float32)
            log_line = tail[0:1] * jnp.exp2(tail[1:2] - LOG_BITS)
            logs.append(jnp.broadcast_to(column(log_line), (per_dest, width)))
            scales.append(column(jnp.exp2(tail[2:3] - VALUE_BITS)))
            top = jnp.maximum(top, logs[-1])
        weight = jnp.exp(suf_log - top)
        acc = weight * suf_mixed
        total = weight
        for s in range(parts):
            words = got_ref[s * kv_count + place, :half]
            coded = jnp.concatenate([words >> 16, (words << 16) >> 16], axis=0)
            weight = jnp.exp(logs[s] - top)
            acc = acc + (weight * scales[s]) * coded.astype(jnp.float32)
            total = total + weight
        acc = acc / total
        logged = top + jnp.log(total)
        for r in range(count):
            rows = slice(r * group, (r + 1) * group)
            out_ref[r, heads_of] = acc[rows]
            spot = lane[:group] == row[:group] + g * group
            lines[r] = lines[r] + jnp.sum(jnp.where(spot, logged[rows], 0.0), axis=0, keepdims=True)
    for r in range(count):
        log_ref[r : r + 1] = lines[r][:, :heads]


def join_partials(got, suf_mixed, suf_log, kv_count):
    count, heads, width = suf_mixed.shape
    return pl.pallas_call(
        functools.partial(join_kernel, kv_count=kv_count),
        in_specs=[IN_VMEM] * 3,
        out_specs=[IN_VMEM] * 2,
        out_shape=[
            jax.ShapeDtypeStruct((count, heads, width), jnp.float32),
            jax.ShapeDtypeStruct((count, heads), jnp.float32),
        ],
        compiler_params=pltpu.CompilerParams(vmem_limit_bytes=SMALL_VMEM),
        name="join_partials",
    )(got, suf_mixed, suf_log)


def exchange(pieces, first):
    seq, head, rep = lax.axis_size("seq"), lax.axis_size("head"), lax.axis_size("rep")
    order = [(first - s) % seq for s in range(seq)]
    groups = [
        [(s * head + h) * rep + r for s in order for h in reversed(range(head))]
        for r in range(rep)
    ]
    return lax.all_to_all(
        pieces,
        ("seq", "head", "rep"),
        split_axis=0,
        concat_axis=0,
        axis_index_groups=groups,
        tiled=True,
    )


def per_device(
    queries, prefix_keys, prefix_values, suffix_keys, suffix_values, suffix_lengths, slot_map
):
    count, heads, width = queries.shape
    kv_count = suffix_keys.shape[2]
    per_dest = count * heads // kv_count
    score_scale = 1.0 / math.sqrt(width)
    sent, near_keys, near_values = layout_queries(
        queries, kv_count, lax.axis_size("seq"), (prefix_keys[:, 0, :], prefix_values[:, 0, :])
    )
    seq = lax.axis_size("seq")
    middle = seq // 2
    got_q = exchange(sent, middle)
    far_keys = lax.ppermute(near_keys, "rep", [(0, 1), (1, 0)])
    far_values = lax.ppermute(near_values, "rep", [(0, 1), (1, 0)])
    earlier = []
    for place in range(count):
        mixed, log = suffix_partials(
            place,
            queries,
            suffix_keys,
            suffix_values,
            suffix_lengths,
            slot_map,
            earlier if place == count - 1 else (),
            score_scale,
        )
        earlier += [mixed, log]
    partials = prefix_partials(
        got_q.reshape(-1, width),
        near_keys,
        near_values,
        far_keys,
        far_values,
        earlier[0],
        per_dest,
        score_scale,
    )
    got = exchange(partials, middle)
    return join_partials(got, mixed, log, kv_count)


def solution(mesh):
    by_request = P(("seq", "head", "rep"))
    by_block = P(("seq", "rep"), "head", None)
    placed = (by_request, by_block, by_block, by_request, by_request, by_request, by_request)
    return jax.shard_map(
        per_device,
        mesh=mesh,
        in_specs=placed,
        out_specs=(by_request, by_request),
        check_vma=False,
    )
```

```python
import functools
import math

import jax
import jax.numpy as jnp
from jax import lax
from jax.experimental import pallas as pl
from jax.experimental.pallas import tpu as pltpu
from jax.sharding import PartitionSpec as P

ROW_TILE = 128
STEP_ROWS = 512
SUF_COPIES = 4
AT_ONCE = 2
BRING_PARTS = 2
LANES = 128
LOG_ROWS = 8
VALUE_BITS = 15
LOG_BITS = 30
LOG2E = math.log2(math.e)
LEAST = 1e-25
PEAK_LEAST = 1e-33
NT = (((1,), (1,)), ((), ()))
PREFIX_VMEM = 14 * 1024 * 1024
SUFFIX_VMEM = 20 * 1024 * 1024
SMALL_VMEM = 8 * 1024 * 1024
IN_VMEM = pl.BlockSpec(memory_space=pltpu.VMEM)
IN_HBM = pl.BlockSpec(memory_space=pltpu.HBM)


def in_hbm(array):
    return pltpu.with_memory_space_constraint(array, pltpu.HBM)


def layout_kernel(q_hbm, sent_hbm, buf, in_sems, out_sems):
    groups, rows, _ = buf.shape
    count = q_hbm.shape[0]
    group = rows // count
    repeats = sent_hbm.shape[0] // groups
    reads = [
        pltpu.make_async_copy(
            q_hbm.at[r, pl.ds(g * group, group)],
            buf.at[groups - 1 - g, pl.ds(r * group, group)],
            in_sems.at[g, r],
        )
        for g in range(groups)
        for r in range(count)
    ]
    for read in reads:
        read.start()
    for read in reads:
        read.wait()
    writes = [
        pltpu.make_async_copy(buf, sent_hbm.at[pl.ds(s * groups, groups)], out_sems.at[s])
        for s in range(repeats)
    ]
    for write in writes:
        write.start()
    for write in writes:
        write.wait()


def layout_queries(queries, groups, repeats):
    count, heads, width = queries.shape
    rows = count * heads // groups
    return pl.pallas_call(
        layout_kernel,
        in_specs=[IN_HBM],
        out_specs=IN_HBM,
        out_shape=pltpu.HBM((repeats * groups, rows, width), queries.dtype),
        scratch_shapes=[
            pltpu.VMEM((groups, rows, width), queries.dtype),
            pltpu.SemaphoreType.DMA((groups, count)),
            pltpu.SemaphoreType.DMA((repeats,)),
        ],
        compiler_params=pltpu.CompilerParams(vmem_limit_bytes=SMALL_VMEM),
        name="layout_queries",
    )(in_hbm(queries))


def bring_kernel(*refs):
    sources, targets, sems = refs[: len(refs) // 2], refs[len(refs) // 2 : -1], refs[-1]
    parts = sems.shape[1]
    copies = []
    for i, (source, target) in enumerate(zip(sources, targets)):
        rows = source.shape[0] // parts
        for c in range(parts):
            part = pl.ds(c * rows, rows)
            copies.append(pltpu.make_async_copy(source.at[part], target.at[part], sems.at[i, c]))
            copies[-1].start()
    for copy in copies:
        copy.wait()


def bring(*arrays):
    return pl.pallas_call(
        bring_kernel,
        in_specs=[IN_HBM] * len(arrays),
        out_specs=[IN_VMEM] * len(arrays),
        out_shape=[pltpu.VMEM(array.shape, array.dtype) for array in arrays],
        scratch_shapes=[pltpu.SemaphoreType.DMA((len(arrays), BRING_PARTS))],
        compiler_params=pltpu.CompilerParams(vmem_limit_bytes=SMALL_VMEM),
        cost_estimate=pl.CostEstimate(
            flops=0, bytes_accessed=sum(2 * 2 * array.size for array in arrays), transcendentals=0
        ),
        name="bring_prefix",
    )(*map(in_hbm, arrays))


def suffix_kernel(*refs, place, kv_count, score_scale):
    slot_hbm, length_hbm, q_hbm, k_hbm, v_hbm = refs[:5]
    refs = refs[5:]
    count, heads, width = q_hbm.shape
    last = place == count - 1
    earlier, refs = (refs[: 2 * place], refs[2 * place :]) if last else ((), refs)
    mixed_ref, log_ref = refs[:2]
    slot_ref, length_ref, q_ref, k_buf, v_buf, score_ref, peak_ref, sum_ref, acc_ref, sems, small_sems = refs[2:]
    rows = k_hbm.shape[1]
    copy_rows = rows // SUF_COPIES
    copies = []
    for which, (source, target) in enumerate(((k_hbm, k_buf), (v_hbm, v_buf))):
        for c in range(SUF_COPIES):
            part = pl.ds(c * copy_rows, copy_rows)
            copies.append(
                pltpu.make_async_copy(source.at[place, part], target.at[part], sems.at[which, c])
            )
    k_copies, v_copies = copies[:SUF_COPIES], copies[SUF_COPIES:]
    small = [
        pltpu.make_async_copy(source, target, small_sems.at[i])
        for i, (source, target) in enumerate(
            [(slot_hbm, slot_ref), (length_hbm, length_ref), (q_hbm, q_ref)]
        )
    ]
    for copy in small + k_copies[:AT_ONCE]:
        copy.start()
    for copy in small:
        copy.wait()

    def request_of(slot):
        found = jnp.int32(0)
        for r in range(1, count):
            found = jnp.where(lax.rem(slot_ref[r], count) == slot, r, found)
        return found

    request = request_of(place)
    limit = length_ref[request] * kv_count

    def live(c):
        return limit > c * copy_rows

    for c in range(AT_ONCE, SUF_COPIES):
        pl.when(live(c))(k_copies[c].start)
    query = q_ref[request]
    lane = lax.broadcasted_iota(jnp.int32, (heads, LANES), 1)
    group = lax.broadcasted_iota(jnp.int32, (heads, LANES), 0) // (heads // kv_count)
    lane = jnp.where((lane % kv_count) == group, lane, rows)
    peak_ref[...] = jnp.full((heads, LANES), -1e30, jnp.float32)
    for c in range(SUF_COPIES):
        if c < AT_ONCE:
            k_copies[c].wait()

        @pl.when(live(c))
        def _(c=c):
            if c >= AT_ONCE:
                k_copies[c].wait()
            v_copies[c].start()
            part = lax.dot_general(
                query, k_buf[c * copy_rows : (c + 1) * copy_rows], NT, preferred_element_type=jnp.float32
            )
            peak = peak_ref[...]
            for begin in range(0, copy_rows, LANES):
                at = c * copy_rows + begin
                tile = jnp.where(lane < limit - at, part[:, begin : begin + LANES], -1e30)
                score_ref[:, at : at + LANES] = tile
                peak = jnp.maximum(peak, tile)
            peak_ref[...] = peak

    row_max = jnp.max(peak_ref[...], axis=1, keepdims=True)
    sum_ref[...] = jnp.zeros((heads, LANES), jnp.float32)
    acc_ref[...] = jnp.zeros((heads, width), jnp.float32)
    for c in range(SUF_COPIES):

        @pl.when(live(c))
        def _(c=c):
            v_copies[c].wait()
            part = slice(c * copy_rows, (c + 1) * copy_rows)
            terms = jnp.exp2((score_ref[:, part] - row_max) * (score_scale * LOG2E))
            sums = sum_ref[...]
            for begin in range(0, copy_rows, LANES):
                sums = sums + terms[:, begin : begin + LANES]
            sum_ref[...] = sums
            acc_ref[...] += jnp.dot(
                terms.astype(jnp.bfloat16), v_buf[part], preferred_element_type=jnp.float32
            )

    sums, acc = sum_ref[...], acc_ref[...]
    total = jnp.sum(sums, axis=1, keepdims=True)
    mixed = acc / total
    log = jnp.broadcast_to(row_max * score_scale + jnp.log(total), (heads, width))
    if not last:
        mixed_ref[...] = mixed
        log_ref[...] = log
        return
    mixed_ref[request] = mixed
    log_ref[request] = log
    for slot in range(place):
        mixed_ref[request_of(slot)] = earlier[2 * slot][...]
        log_ref[request_of(slot)] = earlier[2 * slot + 1][...]


def suffix_partials(place, queries, keys, values, lengths, slots, earlier, score_scale):
    count, heads, width = queries.shape
    kv_count = keys.shape[2]
    rows = keys.shape[1] * kv_count
    result = (count, heads, width) if place == count - 1 else (heads, width)
    operands = (
        slots,
        lengths,
        queries,
        keys.reshape(count, rows, width),
        values.reshape(count, rows, width),
    )
    return pl.pallas_call(
        functools.partial(
            suffix_kernel,
            place=place,
            kv_count=kv_count,
            score_scale=score_scale,
        ),
        in_specs=[IN_HBM] * len(operands) + [IN_VMEM] * len(earlier),
        out_specs=[IN_VMEM] * 2,
        out_shape=[pltpu.VMEM(result, jnp.float32)] * 2,
        scratch_shapes=[
            pltpu.SMEM((count,), jnp.int32),
            pltpu.SMEM((count,), jnp.int32),
            pltpu.VMEM((count, heads, width), queries.dtype),
            pltpu.VMEM((rows, width), keys.dtype),
            pltpu.VMEM((rows, width), values.dtype),
            pltpu.VMEM((heads, rows), jnp.float32),
            pltpu.VMEM((heads, LANES), jnp.float32),
            pltpu.VMEM((heads, LANES), jnp.float32),
            pltpu.VMEM((heads, width), jnp.float32),
            pltpu.SemaphoreType.DMA((2, SUF_COPIES)),
            pltpu.SemaphoreType.DMA((3,)),
        ],
        compiler_params=pltpu.CompilerParams(vmem_limit_bytes=SUFFIX_VMEM),
        cost_estimate=pl.CostEstimate(
            flops=4 * heads * rows * width,
            bytes_accessed=4 * rows * width,
            transcendentals=heads * rows,
        ),
        name=f"suffix_attention_{place}",
    )(*map(in_hbm, operands), *earlier)


def exponent(size, least):
    return jnp.floor(jnp.log2(jnp.maximum(size, least))) + 1.0


def prefix_kernel(
    q_ref, k0_ref, v0_ref, k1_ref, v1_ref, _, out_hbm, out_ref, score_ref, sems, *, per_dest, score_scale
):
    width = q_ref.shape[1]
    tiles = q_ref.shape[0] // ROW_TILE
    dests = ROW_TILE // per_dest
    keys, values = (k0_ref, k1_ref), (v0_ref, v1_ref)
    units = [(tile, block) for tile in range(tiles) for block in range(2)]
    first_dest = 0 if out_hbm.shape == out_ref.shape else pl.program_id(0) * (tiles * dests)
    copies = []
    lane = lax.broadcasted_iota(jnp.int32, (per_dest, width), 1)
    row = lax.broadcasted_iota(jnp.int32, (per_dest, width), 0)
    diagonal = lane == row

    def score(unit, slot):
        tile, block = unit
        score_ref[slot] = lax.dot_general(
            q_ref[tile * ROW_TILE : (tile + 1) * ROW_TILE],
            keys[block][...],
            NT,
            preferred_element_type=jnp.float32,
        )

    score(units[0], 0)
    held = None
    for step, (tile, block) in enumerate(units):
        if step + 1 < len(units):
            score(units[step + 1], (step + 1) % 2)
        scores = score_ref[step % 2]
        row_max = jnp.max(scores, axis=1, keepdims=True)
        terms = jnp.exp2((scores - row_max) * (score_scale * LOG2E))
        total = jnp.sum(terms, axis=1, keepdims=True)
        acc = jnp.dot(
            terms.astype(jnp.bfloat16), values[block][...], preferred_element_type=jnp.float32
        )
        if block == 0:
            held = (row_max, total, acc)
            continue
        max0, total0, acc0 = held
        top = jnp.maximum(max0, row_max)
        weight0 = jnp.exp((max0 - top) * score_scale)
        weight1 = jnp.exp((row_max - top) * score_scale)
        joined = weight0 * total0 + weight1 * total
        mixed = (weight0 * acc0 + weight1 * acc) / joined
        logs = jnp.broadcast_to(top * score_scale + jnp.log(joined), (ROW_TILE, width))
        peak = jnp.max(jnp.abs(mixed), axis=1, keepdims=True)
        coded = jnp.round(mixed * jnp.exp2(VALUE_BITS - exponent(peak, PEAK_LEAST)))
        most = 2.0**VALUE_BITS - 1
        coded = jnp.clip(coded, -most, most).astype(jnp.int32)
        peaks = jnp.broadcast_to(peak, (ROW_TILE, width))
        half = per_dest // 2
        for k in range(dests):
            rows = slice(k * per_dest, (k + 1) * per_dest)
            dest = tile * dests + k
            high, low = coded[k * per_dest : k * per_dest + half], coded[k * per_dest + half : rows.stop]
            out_ref[dest, :half] = (high << 16) | (low & 0xFFFF)
            log_line = jnp.sum(jnp.where(diagonal, logs[rows], 0.0), axis=0, keepdims=True)
            peak_line = jnp.sum(jnp.where(diagonal, peaks[rows], 0.0), axis=0, keepdims=True)
            log_power = exponent(jnp.abs(log_line), LEAST)
            lines = jnp.concatenate(
                [
                    jnp.round(log_line * jnp.exp2(LOG_BITS - log_power)),
                    log_power,
                    exponent(peak_line, PEAK_LEAST),
                    jnp.zeros((LOG_ROWS - 3, width), jnp.float32),
                ],
                axis=0,
            )
            out_ref[dest, half:] = lines.astype(jnp.int32)
        ready = pl.ds(tile * dests, dests)
        copies.append(
            pltpu.make_async_copy(
                out_ref.at[ready],
                out_hbm.at[pl.ds(first_dest + tile * dests, dests)],
                sems.at[tile],
            )
        )
        copies[-1].start()
    for copy in copies:
        copy.wait()


def prefix_partials(
    rows_q, keys, values, far_keys, far_values, after, per_dest, score_scale
):
    rows, width = rows_q.shape
    length = keys.shape[0]
    step_rows = min(STEP_ROWS, rows)
    dests = step_rows // per_dest
    out_rows = per_dest // 2 + LOG_ROWS
    blocked = {"in_specs": [IN_VMEM] * 5}
    if step_rows < rows:
        blocked["grid"] = (rows // step_rows,)
        blocked["in_specs"] = [pl.BlockSpec((step_rows, width), lambda i: (i, 0))]
        blocked["in_specs"] += [pl.BlockSpec((length, width), lambda i: (0, 0))] * 4
    blocked["in_specs"] += [pl.BlockSpec(memory_space=pl.ANY)]
    return pl.pallas_call(
        functools.partial(
            prefix_kernel, per_dest=per_dest, score_scale=score_scale
        ),
        **blocked,
        out_specs=IN_HBM,
        out_shape=pltpu.HBM((rows // per_dest, out_rows, width), jnp.int32),
        scratch_shapes=[
            pltpu.VMEM((dests, out_rows, width), jnp.int32),
            pltpu.VMEM((2, ROW_TILE, length), jnp.float32),
            pltpu.SemaphoreType.DMA((step_rows // ROW_TILE,)),
        ],
        compiler_params=pltpu.CompilerParams(vmem_limit_bytes=PREFIX_VMEM),
        cost_estimate=pl.CostEstimate(
            flops=8 * rows * length * width,
            bytes_accessed=8 * length * width + 6 * rows * width,
            transcendentals=2 * rows * length,
        ),
        name="prefix_attention",
    )(rows_q, keys, values, far_keys, far_values, after)


def join_kernel(got_ref, suf_ref, suf_log_ref, out_ref, log_ref, *, kv_count):
    count, heads, width = out_ref.shape
    group = heads // kv_count
    per_dest = count * group
    half = per_dest // 2
    parts = got_ref.shape[0] // kv_count
    lane = lax.broadcasted_iota(jnp.int32, (per_dest, width), 1)
    row = lax.broadcasted_iota(jnp.int32, (per_dest, width), 0)
    diagonal = lane == row

    def column(line):
        return jnp.sum(jnp.where(diagonal, line, 0.0), axis=1, keepdims=True)

    lines = [jnp.zeros((1, width), jnp.float32) for _ in range(count)]
    for place in range(kv_count):
        g = kv_count - 1 - place
        heads_of = slice(g * group, (g + 1) * group)
        suf_mixed = jnp.concatenate([suf_ref[r, heads_of] for r in range(count)], axis=0)
        suf_log = jnp.concatenate([suf_log_ref[r, heads_of] for r in range(count)], axis=0)
        logs, scales = [], []
        top = suf_log
        for s in range(parts):
            tail = got_ref[s * kv_count + place, half:].astype(jnp.float32)
            log_line = tail[0:1] * jnp.exp2(tail[1:2] - LOG_BITS)
            logs.append(jnp.broadcast_to(column(log_line), (per_dest, width)))
            scales.append(column(jnp.exp2(tail[2:3] - VALUE_BITS)))
            top = jnp.maximum(top, logs[-1])
        weight = jnp.exp(suf_log - top)
        acc = weight * suf_mixed
        total = weight
        for s in range(parts):
            words = got_ref[s * kv_count + place, :half]
            coded = jnp.concatenate([words >> 16, (words << 16) >> 16], axis=0)
            weight = jnp.exp(logs[s] - top)
            acc = acc + (weight * scales[s]) * coded.astype(jnp.float32)
            total = total + weight
        acc = acc / total
        logged = top + jnp.log(total)
        for r in range(count):
            rows = slice(r * group, (r + 1) * group)
            out_ref[r, heads_of] = acc[rows]
            spot = lane[:group] == row[:group] + g * group
            lines[r] = lines[r] + jnp.sum(jnp.where(spot, logged[rows], 0.0), axis=0, keepdims=True)
    for r in range(count):
        log_ref[r : r + 1] = lines[r][:, :heads]


def join_partials(got, suf_mixed, suf_log, kv_count):
    count, heads, width = suf_mixed.shape
    return pl.pallas_call(
        functools.partial(join_kernel, kv_count=kv_count),
        in_specs=[IN_VMEM] * 3,
        out_specs=[IN_VMEM] * 2,
        out_shape=[
            jax.ShapeDtypeStruct((count, heads, width), jnp.float32),
            jax.ShapeDtypeStruct((count, heads), jnp.float32),
        ],
        compiler_params=pltpu.CompilerParams(vmem_limit_bytes=SMALL_VMEM),
        name="join_partials",
    )(got, suf_mixed, suf_log)


def exchange(pieces, first):
    seq, head, rep = lax.axis_size("seq"), lax.axis_size("head"), lax.axis_size("rep")
    order = [(first - s) % seq for s in range(seq)]
    groups = [
        [(s * head + h) * rep + r for s in order for h in reversed(range(head))]
        for r in range(rep)
    ]
    return lax.all_to_all(
        pieces,
        ("seq", "head", "rep"),
        split_axis=0,
        concat_axis=0,
        axis_index_groups=groups,
        tiled=True,
    )


def per_device(
    queries, prefix_keys, prefix_values, suffix_keys, suffix_values, suffix_lengths, slot_map
):
    count, heads, width = queries.shape
    kv_count = suffix_keys.shape[2]
    per_dest = count * heads // kv_count
    score_scale = 1.0 / math.sqrt(width)
    sent = layout_queries(queries, kv_count, lax.axis_size("seq"))
    seq = lax.axis_size("seq")
    middle = seq // 2
    got_q = exchange(sent, middle)
    near_keys, near_values = bring(prefix_keys[:, 0, :], prefix_values[:, 0, :])
    far_keys = lax.ppermute(near_keys, "rep", [(0, 1), (1, 0)])
    far_values = lax.ppermute(near_values, "rep", [(0, 1), (1, 0)])
    earlier = []
    for place in range(count):
        mixed, log = suffix_partials(
            place,
            queries,
            suffix_keys,
            suffix_values,
            suffix_lengths,
            slot_map,
            earlier if place == count - 1 else (),
            score_scale,
        )
        earlier += [mixed, log]
    partials = prefix_partials(
        got_q.reshape(-1, width),
        near_keys,
        near_values,
        far_keys,
        far_values,
        earlier[0],
        per_dest,
        score_scale,
    )
    got = exchange(partials, middle)
    return join_partials(got, mixed, log, kv_count)


def solution(mesh):
    by_request = P(("seq", "head", "rep"))
    by_block = P(("seq", "rep"), "head", None)
    placed = (by_request, by_block, by_block, by_request, by_request, by_request, by_request)
    return jax.shard_map(
        per_device,
        mesh=mesh,
        in_specs=placed,
        out_specs=(by_request, by_request),
        check_vma=False,
    )
```

```python
import functools
import math

import jax
import jax.numpy as jnp
from jax import lax
from jax.experimental import pallas as pl
from jax.experimental.pallas import tpu as pltpu
from jax.sharding import PartitionSpec as P

ROW_TILE = 128
STEP_ROWS = 512
SUF_COPIES = 4
AT_ONCE = 2
LANES = 128
PIECE = 256
TILE_ROWS = 2
VALUE_BITS = 15
LOG_BITS = 30
LOG2E = math.log2(math.e)
LEAST = 1e-25
PEAK_LEAST = 1e-33
NT = (((1,), (1,)), ((), ()))
PREFIX_VMEM = 14 * 1024 * 1024
SUFFIX_VMEM = 20 * 1024 * 1024
SMALL_VMEM = 8 * 1024 * 1024
IN_VMEM = pl.BlockSpec(memory_space=pltpu.VMEM)
IN_HBM = pl.BlockSpec(memory_space=pltpu.HBM)


def in_hbm(array):
    return pltpu.with_memory_space_constraint(array, pltpu.HBM)


def layout_kernel(q_hbm, sent_hbm, buf, in_sems, out_sems):
    groups = buf.shape[0]
    repeats = sent_hbm.shape[0] // groups
    reads = [
        pltpu.make_async_copy(q_hbm.at[:, g], buf.at[groups - 1 - g], in_sems.at[g])
        for g in range(groups)
    ]
    for read in reads:
        read.start()
    for read in reads:
        read.wait()
    writes = [
        pltpu.make_async_copy(buf, sent_hbm.at[pl.ds(s * groups, groups)], out_sems.at[s])
        for s in range(repeats)
    ]
    for write in writes:
        write.start()
    for write in writes:
        write.wait()


def layout_queries(queries, groups, repeats):
    count, heads, width = queries.shape
    group = heads // groups
    return pl.pallas_call(
        layout_kernel,
        in_specs=[IN_HBM],
        out_specs=IN_HBM,
        out_shape=pltpu.HBM((repeats * groups, count, group, width), queries.dtype),
        scratch_shapes=[
            pltpu.VMEM((groups, count, group, width), queries.dtype),
            pltpu.SemaphoreType.DMA((groups,)),
            pltpu.SemaphoreType.DMA((repeats,)),
        ],
        compiler_params=pltpu.CompilerParams(vmem_limit_bytes=SMALL_VMEM),
        name="layout_queries",
    )(in_hbm(queries.reshape(count, groups, group, width)))


def weigh(scores, weights, part, row_max, factor):
    sums = jnp.zeros((scores.shape[0], LANES), jnp.float32)
    for begin in range(part.start, part.stop, PIECE):
        piece = slice(begin, begin + PIECE)
        terms = jnp.exp2((scores[:, piece] - row_max) * factor)
        weights[:, piece] = terms.astype(jnp.bfloat16)
        for lane in range(0, PIECE, LANES):
            sums = sums + terms[:, lane : lane + LANES]
    return sums


def suffix_kernel(*refs, place, carried, kv_count, score_scale):
    slot_hbm, length_hbm, q_hbm, k_hbm, v_hbm = refs[:5]
    refs = refs[5:]
    count, heads, width = q_hbm.shape
    carried_refs, refs = refs[:carried], refs[carried:]
    last = place == count - 1
    earlier, refs = (refs[: 2 * place], refs[2 * place :]) if last else ((), refs)
    mixed_ref, log_ref = refs[:2]
    brought_refs, refs = refs[2 : 2 + carried], refs[2 + carried :]
    slot_ref, length_ref, q_ref, k_buf, v_buf, score_ref, weight_ref = refs[:7]
    peak_ref, sum_ref, acc_ref, sems, small_sems = refs[7:]
    rows = k_hbm.shape[1]
    copy_rows = rows // SUF_COPIES
    copies = []
    for which, (source, target) in enumerate(((k_hbm, k_buf), (v_hbm, v_buf))):
        for c in range(SUF_COPIES):
            part = pl.ds(c * copy_rows, copy_rows)
            copies.append(
                pltpu.make_async_copy(source.at[place, part], target.at[part], sems.at[which, c])
            )
    k_copies, v_copies = copies[:SUF_COPIES], copies[SUF_COPIES:]
    small = [
        pltpu.make_async_copy(source, target, small_sems.at[i])
        for i, (source, target) in enumerate(
            [(slot_hbm, slot_ref), (length_hbm, length_ref), (q_hbm, q_ref)]
            + list(zip(carried_refs, brought_refs))
        )
    ]
    small, carries = small[:3], small[3:]
    for copy in small + k_copies[:AT_ONCE] + carries:
        copy.start()
    for copy in small:
        copy.wait()

    def request_of(slot):
        found = jnp.int32(0)
        for r in range(1, count):
            found = jnp.where(lax.rem(slot_ref[r], count) == slot, r, found)
        return found

    request = request_of(place)
    limit = length_ref[request] * kv_count

    def live(c):
        return limit > c * copy_rows

    for c in range(AT_ONCE, SUF_COPIES):
        pl.when(live(c))(k_copies[c].start)
    query = q_ref[request]
    lane = lax.broadcasted_iota(jnp.int32, (heads, LANES), 1)
    group = lax.broadcasted_iota(jnp.int32, (heads, LANES), 0) // (heads // kv_count)
    lane = jnp.where((lane % kv_count) == group, lane, rows)
    peak_ref[...] = jnp.full((heads, LANES), -1e30, jnp.float32)
    for c in range(SUF_COPIES):
        if c < AT_ONCE:
            k_copies[c].wait()

        @pl.when(live(c))
        def _(c=c):
            if c >= AT_ONCE:
                k_copies[c].wait()
            v_copies[c].start()
            peak = peak_ref[...]
            for at in range(c * copy_rows, (c + 1) * copy_rows, 2 * PIECE):
                part = lax.dot_general(
                    query, k_buf[at : at + 2 * PIECE], NT, preferred_element_type=jnp.float32
                )
                for begin in range(0, 2 * PIECE, LANES):
                    tile = jnp.where(lane < limit - (at + begin), part[:, begin : begin + LANES], -1e30)
                    score_ref[:, at + begin : at + begin + LANES] = tile
                    peak = jnp.maximum(peak, tile)
            peak_ref[...] = peak

    row_max = jnp.max(peak_ref[...], axis=1, keepdims=True)
    sum_ref[...] = jnp.zeros((heads, LANES), jnp.float32)
    acc_ref[...] = jnp.zeros((heads, width), jnp.float32)
    for c in range(SUF_COPIES):

        @pl.when(live(c))
        def _(c=c):
            v_copies[c].wait()
            part = slice(c * copy_rows, (c + 1) * copy_rows)
            sum_ref[...] += weigh(score_ref, weight_ref, part, row_max, score_scale * LOG2E)
            acc_ref[...] += jnp.dot(
                weight_ref[:, part], v_buf[part], preferred_element_type=jnp.float32
            )

    sums, acc = sum_ref[...], acc_ref[...]
    total = jnp.sum(sums, axis=1, keepdims=True)
    mixed = acc / total
    log = jnp.broadcast_to(row_max * score_scale + jnp.log(total), (heads, width))
    for carry in carries:
        carry.wait()
    if not last:
        mixed_ref[...] = mixed
        log_ref[...] = log
        return
    mixed_ref[request] = mixed
    log_ref[request] = log
    for slot in range(place):
        mixed_ref[request_of(slot)] = earlier[2 * slot][...]
        log_ref[request_of(slot)] = earlier[2 * slot + 1][...]


def suffix_partials(
    place, queries, keys, values, lengths, slots, carried, earlier, score_scale
):
    count, heads, width = queries.shape
    kv_count = keys.shape[2]
    rows = keys.shape[1] * kv_count
    result = (count, heads, width) if place == count - 1 else (heads, width)
    operands = (
        slots,
        lengths,
        queries,
        keys.reshape(count, rows, width),
        values.reshape(count, rows, width),
        *carried,
    )
    return pl.pallas_call(
        functools.partial(
            suffix_kernel,
            place=place,
            carried=len(carried),
            kv_count=kv_count,
            score_scale=score_scale,
        ),
        in_specs=[IN_HBM] * len(operands) + [IN_VMEM] * len(earlier),
        out_specs=[IN_VMEM] * (2 + len(carried)),
        out_shape=[pltpu.VMEM(result, jnp.float32)] * 2
        + [pltpu.VMEM(array.shape, array.dtype) for array in carried],
        scratch_shapes=[
            pltpu.SMEM((count,), jnp.int32),
            pltpu.SMEM((count,), jnp.int32),
            pltpu.VMEM((count, heads, width), queries.dtype),
            pltpu.VMEM((rows, width), keys.dtype),
            pltpu.VMEM((rows, width), values.dtype),
            pltpu.VMEM((heads, rows), jnp.float32),
            pltpu.VMEM((heads, rows), jnp.bfloat16),
            pltpu.VMEM((heads, LANES), jnp.float32),
            pltpu.VMEM((heads, LANES), jnp.float32),
            pltpu.VMEM((heads, width), jnp.float32),
            pltpu.SemaphoreType.DMA((2, SUF_COPIES)),
            pltpu.SemaphoreType.DMA((3 + len(carried),)),
        ],
        compiler_params=pltpu.CompilerParams(vmem_limit_bytes=SUFFIX_VMEM),
        cost_estimate=pl.CostEstimate(
            flops=4 * heads * rows * width,
            bytes_accessed=4 * rows * width,
            transcendentals=heads * rows,
        ),
        name=f"suffix_attention_{place}",
    )(*map(in_hbm, operands), *earlier)


def exponent(size, least):
    return jnp.floor(jnp.log2(jnp.maximum(size, least))) + 1.0


def prefix_kernel(
    q_ref, k0_ref, v0_ref, k1_ref, v1_ref, _, out_hbm, out_ref, score_ref, weight_ref, sems, *, per_dest, score_scale
):
    width = q_ref.shape[1]
    tiles = q_ref.shape[0] // ROW_TILE
    dests = ROW_TILE // per_dest
    keys, values = (k0_ref, k1_ref), (v0_ref, v1_ref)
    units = [(tile, block) for tile in range(tiles) for block in range(2)]
    first_dest = 0 if out_hbm.shape == out_ref.shape else pl.program_id(0) * (tiles * dests)
    copies = []
    lane = lax.broadcasted_iota(jnp.int32, (per_dest, width), 1)
    row = lax.broadcasted_iota(jnp.int32, (per_dest, width), 0)
    diagonal = lane == row

    length = k0_ref.shape[0]

    def score(unit, slot):
        tile, block = unit
        query = q_ref[tile * ROW_TILE : (tile + 1) * ROW_TILE]
        peak = None
        for at in range(0, length, PIECE):
            part = lax.dot_general(
                query, keys[block][at : at + PIECE], NT, preferred_element_type=jnp.float32
            )
            score_ref[slot, :, at : at + PIECE] = part
            for begin in range(0, PIECE, LANES):
                lanes = part[:, begin : begin + LANES]
                peak = lanes if peak is None else jnp.maximum(peak, lanes)
        return jnp.max(peak, axis=1, keepdims=True)

    later_max = score(units[0], 0)
    held = None
    for step, (tile, block) in enumerate(units):
        row_max = later_max
        if step + 1 < len(units):
            later_max = score(units[step + 1], (step + 1) % 2)
        slot = step % 2
        sums = weigh(
            score_ref.at[slot], weight_ref.at[slot], slice(0, length), row_max, score_scale * LOG2E
        )
        total = jnp.sum(sums, axis=1, keepdims=True)
        acc = jnp.dot(weight_ref[slot], values[block][...], preferred_element_type=jnp.float32)
        if block == 0:
            held = (row_max, total, acc)
            continue
        max0, total0, acc0 = held
        top = jnp.maximum(max0, row_max)
        weight0 = jnp.exp((max0 - top) * score_scale)
        weight1 = jnp.exp((row_max - top) * score_scale)
        joined = weight0 * total0 + weight1 * total
        mixed = (weight0 * acc0 + weight1 * acc) / joined
        logs = jnp.broadcast_to(top * score_scale + jnp.log(joined), (ROW_TILE, width))
        peak = jnp.max(jnp.abs(mixed), axis=1, keepdims=True)
        coded = jnp.round(mixed * jnp.exp2(VALUE_BITS - exponent(peak, PEAK_LEAST)))
        most = 2.0**VALUE_BITS - 1
        coded = jnp.clip(coded, -most, most).astype(jnp.int32)
        peaks = jnp.broadcast_to(peak, (ROW_TILE, width))
        half = per_dest // 2
        for k in range(dests):
            rows = slice(k * per_dest, (k + 1) * per_dest)
            dest = tile * dests + k
            high, low = coded[k * per_dest : k * per_dest + half], coded[k * per_dest + half : rows.stop]
            words = (high << 16) | (low & 0xFFFF)
            for j in range(half // TILE_ROWS):
                out_ref[dest, j] = words[j * TILE_ROWS : (j + 1) * TILE_ROWS]
            log_line = jnp.sum(jnp.where(diagonal, logs[rows], 0.0), axis=0, keepdims=True)
            peak_line = jnp.sum(jnp.where(diagonal, peaks[rows], 0.0), axis=0, keepdims=True)
            log_power = exponent(jnp.abs(log_line), LEAST)
            mantissa = jnp.round(log_line * jnp.exp2(LOG_BITS - log_power)).astype(jnp.int32)
            powers = log_power.astype(jnp.int32) << 16
            powers = powers | (exponent(peak_line, PEAK_LEAST).astype(jnp.int32) & 0xFFFF)
            out_ref[dest, half // TILE_ROWS] = jnp.concatenate([mantissa, powers], axis=0)
        ready = pl.ds(tile * dests, dests)
        copies.append(
            pltpu.make_async_copy(
                out_ref.at[ready],
                out_hbm.at[pl.ds(first_dest + tile * dests, dests)],
                sems.at[tile],
            )
        )
        copies[-1].start()
    for copy in copies:
        copy.wait()


def prefix_partials(
    rows_q, keys, values, far_keys, far_values, after, per_dest, score_scale
):
    rows, width = rows_q.shape
    length = keys.shape[0]
    step_rows = min(STEP_ROWS, rows)
    dests = step_rows // per_dest
    out_piece = (per_dest // 2 // TILE_ROWS + 1, TILE_ROWS, width)
    blocked = {"in_specs": [IN_VMEM] * 5}
    if step_rows < rows:
        blocked["grid"] = (rows // step_rows,)
        blocked["in_specs"] = [pl.BlockSpec((step_rows, width), lambda i: (i, 0))]
        blocked["in_specs"] += [pl.BlockSpec((length, width), lambda i: (0, 0))] * 4
    blocked["in_specs"] += [pl.BlockSpec(memory_space=pl.ANY)]
    return pl.pallas_call(
        functools.partial(
            prefix_kernel, per_dest=per_dest, score_scale=score_scale
        ),
        **blocked,
        out_specs=IN_HBM,
        out_shape=pltpu.HBM((rows // per_dest, *out_piece), jnp.int32),
        scratch_shapes=[
            pltpu.VMEM((dests, *out_piece), jnp.int32),
            pltpu.VMEM((2, ROW_TILE, length), jnp.float32),
            pltpu.VMEM((2, ROW_TILE, length), jnp.bfloat16),
            pltpu.SemaphoreType.DMA((step_rows // ROW_TILE,)),
        ],
        compiler_params=pltpu.CompilerParams(vmem_limit_bytes=PREFIX_VMEM),
        cost_estimate=pl.CostEstimate(
            flops=8 * rows * length * width,
            bytes_accessed=8 * length * width + 6 * rows * width,
            transcendentals=2 * rows * length,
        ),
        name="prefix_attention",
    )(rows_q, keys, values, far_keys, far_values, after)


def join_kernel(got_ref, suf_ref, suf_log_ref, out_ref, log_ref, *, kv_count):
    count, heads, width = out_ref.shape
    group = heads // kv_count
    per_dest = count * group
    half = per_dest // 2
    parts = got_ref.shape[0] // kv_count
    lane = lax.broadcasted_iota(jnp.int32, (per_dest, width), 1)
    row = lax.broadcasted_iota(jnp.int32, (per_dest, width), 0)
    diagonal = lane == row

    def column(line):
        return jnp.sum(jnp.where(diagonal, line, 0.0), axis=1, keepdims=True)

    lines = [jnp.zeros((1, width), jnp.float32) for _ in range(count)]
    for place in range(kv_count):
        g = kv_count - 1 - place
        heads_of = slice(g * group, (g + 1) * group)
        suf_mixed = jnp.concatenate([suf_ref[r, heads_of] for r in range(count)], axis=0)
        suf_log = jnp.concatenate([suf_log_ref[r, heads_of] for r in range(count)], axis=0)
        logs, scales = [], []
        top = suf_log
        for s in range(parts):
            tail = got_ref[s * kv_count + place, half // TILE_ROWS]
            mantissa, powers = tail[0:1], tail[1:2]
            log_power = (powers >> 16).astype(jnp.float32)
            peak_power = ((powers << 16) >> 16).astype(jnp.float32)
            log_line = mantissa.astype(jnp.float32) * jnp.exp2(log_power - LOG_BITS)
            logs.append(jnp.broadcast_to(column(log_line), (per_dest, width)))
            scales.append(column(jnp.exp2(peak_power - VALUE_BITS)))
            top = jnp.maximum(top, logs[-1])
        weight = jnp.exp(suf_log - top)
        acc = weight * suf_mixed
        total = weight
        for s in range(parts):
            words = jnp.concatenate(
                [got_ref[s * kv_count + place, j] for j in range(half // TILE_ROWS)], axis=0
            )
            coded = jnp.concatenate([words >> 16, (words << 16) >> 16], axis=0)
            weight = jnp.exp(logs[s] - top)
            acc = acc + (weight * scales[s]) * coded.astype(jnp.float32)
            total = total + weight
        acc = acc / total
        logged = top + jnp.log(total)
        for r in range(count):
            rows = slice(r * group, (r + 1) * group)
            out_ref[r, heads_of] = acc[rows]
            spot = lane[:group] == row[:group] + g * group
            lines[r] = lines[r] + jnp.sum(jnp.where(spot, logged[rows], 0.0), axis=0, keepdims=True)
    for r in range(count):
        log_ref[r : r + 1] = lines[r][:, :heads]


def join_partials(got, suf_mixed, suf_log, kv_count):
    count, heads, width = suf_mixed.shape
    return pl.pallas_call(
        functools.partial(join_kernel, kv_count=kv_count),
        in_specs=[IN_VMEM] * 3,
        out_specs=[IN_VMEM] * 2,
        out_shape=[
            jax.ShapeDtypeStruct((count, heads, width), jnp.float32),
            jax.ShapeDtypeStruct((count, heads), jnp.float32),
        ],
        compiler_params=pltpu.CompilerParams(vmem_limit_bytes=SMALL_VMEM),
        name="join_partials",
    )(got, suf_mixed, suf_log)


def exchange(pieces, first):
    seq, head, rep = lax.axis_size("seq"), lax.axis_size("head"), lax.axis_size("rep")
    order = [(first - s) % seq for s in range(seq)]
    groups = [
        [(s * head + h) * rep + r for s in order for h in reversed(range(head))]
        for r in range(rep)
    ]
    return lax.all_to_all(
        pieces,
        ("seq", "head", "rep"),
        split_axis=0,
        concat_axis=0,
        axis_index_groups=groups,
        tiled=True,
    )


def per_device(
    queries, prefix_keys, prefix_values, suffix_keys, suffix_values, suffix_lengths, slot_map
):
    count, heads, width = queries.shape
    kv_count = suffix_keys.shape[2]
    per_dest = count * heads // kv_count
    score_scale = 1.0 / math.sqrt(width)
    sent = layout_queries(queries, kv_count, lax.axis_size("seq"))
    seq = lax.axis_size("seq")
    middle = seq // 2
    got_q = exchange(sent, middle)
    keys = prefix_keys[:, 0, :]
    values = prefix_values[:, 0, :]
    far_keys = lax.ppermute(keys, "rep", [(0, 1), (1, 0)])
    far_values = lax.ppermute(values, "rep", [(0, 1), (1, 0)])
    earlier = []
    for place in range(count):
        mixed, log, *brought = suffix_partials(
            place,
            queries,
            suffix_keys,
            suffix_values,
            suffix_lengths,
            slot_map,
            (keys, values) if place == 0 else (),
            earlier if place == count - 1 else (),
            score_scale,
        )
        earlier += [mixed, log]
        if brought:
            near_keys, near_values = brought
    partials = prefix_partials(
        got_q.reshape(-1, width),
        near_keys,
        near_values,
        far_keys,
        far_values,
        earlier[0],
        per_dest,
        score_scale,
    )
    got = exchange(partials, middle)
    return join_partials(got, mixed, log, kv_count)


def solution(mesh):
    by_request = P(("seq", "head", "rep"))
    by_block = P(("seq", "rep"), "head", None)
    placed = (by_request, by_block, by_block, by_request, by_request, by_request, by_request)
    return jax.shard_map(
        per_device,
        mesh=mesh,
        in_specs=placed,
        out_specs=(by_request, by_request),
        check_vma=False,
    )
```

```python
import functools
import math

import jax
import jax.numpy as jnp
from jax import lax
from jax.experimental import pallas as pl
from jax.experimental.pallas import tpu as pltpu
from jax.sharding import PartitionSpec as P

ROW_TILE = 128
STEP_ROWS = 512
SUF_COPIES = 4
AT_ONCE = 2
LANES = 128
PIECE = 256
TILE_ROWS = 2
VALUE_BITS = 15
LOG_BITS = 30
LOG2E = math.log2(math.e)
LEAST = 1e-25
PEAK_LEAST = 1e-33
NT = (((1,), (1,)), ((), ()))
PREFIX_VMEM = 14 * 1024 * 1024
SUFFIX_VMEM = 20 * 1024 * 1024
SMALL_VMEM = 8 * 1024 * 1024
IN_VMEM = pl.BlockSpec(memory_space=pltpu.VMEM)
IN_HBM = pl.BlockSpec(memory_space=pltpu.HBM)


def in_hbm(array):
    return pltpu.with_memory_space_constraint(array, pltpu.HBM)


def layout_kernel(q_hbm, sent_ref, in_sems):
    groups = q_hbm.shape[1]
    repeats = sent_ref.shape[0] // groups
    reads = [
        pltpu.make_async_copy(q_hbm.at[:, g], sent_ref.at[groups - 1 - g], in_sems.at[g])
        for g in range(groups)
    ]
    for read in reads:
        read.start()
    for read in reads:
        read.wait()
    for s in range(1, repeats):
        sent_ref[s * groups : (s + 1) * groups] = sent_ref[:groups]


def layout_queries(queries, groups, repeats):
    count, heads, width = queries.shape
    group = heads // groups
    return pl.pallas_call(
        layout_kernel,
        in_specs=[IN_HBM],
        out_specs=IN_VMEM,
        out_shape=pltpu.VMEM((repeats * groups, count, group, width), queries.dtype),
        scratch_shapes=[pltpu.SemaphoreType.DMA((groups,))],
        compiler_params=pltpu.CompilerParams(vmem_limit_bytes=SMALL_VMEM),
        name="layout_queries",
    )(in_hbm(queries.reshape(count, groups, group, width)))


def weigh(scores, weights, part, row_max, factor):
    sums = jnp.zeros((scores.shape[0], LANES), jnp.float32)
    for begin in range(part.start, part.stop, PIECE):
        piece = slice(begin, begin + PIECE)
        terms = jnp.exp2((scores[:, piece] - row_max) * factor)
        weights[:, piece] = terms.astype(jnp.bfloat16)
        for lane in range(0, PIECE, LANES):
            sums = sums + terms[:, lane : lane + LANES]
    return sums


def suffix_kernel(*refs, place, carried, kv_count, score_scale):
    slot_hbm, length_hbm, q_hbm, k_hbm, v_hbm = refs[:5]
    refs = refs[5:]
    count, heads, width = q_hbm.shape
    carried_refs, refs = refs[:carried], refs[carried:]
    last = place == count - 1
    earlier, refs = (refs[: 2 * place], refs[2 * place :]) if last else ((), refs)
    mixed_ref, log_ref = refs[:2]
    brought_refs, refs = refs[2 : 2 + carried], refs[2 + carried :]
    slot_ref, length_ref, q_ref, k_buf, v_buf, score_ref, weight_ref = refs[:7]
    peak_ref, sum_ref, acc_ref, sems, small_sems = refs[7:]
    rows = k_hbm.shape[1]
    copy_rows = rows // SUF_COPIES
    copies = []
    for which, (source, target) in enumerate(((k_hbm, k_buf), (v_hbm, v_buf))):
        for c in range(SUF_COPIES):
            part = pl.ds(c * copy_rows, copy_rows)
            copies.append(
                pltpu.make_async_copy(source.at[place, part], target.at[part], sems.at[which, c])
            )
    k_copies, v_copies = copies[:SUF_COPIES], copies[SUF_COPIES:]
    small = [
        pltpu.make_async_copy(source, target, small_sems.at[i])
        for i, (source, target) in enumerate(
            [(slot_hbm, slot_ref), (length_hbm, length_ref), (q_hbm, q_ref)]
            + list(zip(carried_refs, brought_refs))
        )
    ]
    small, carries = small[:3], small[3:]
    for copy in small + k_copies[:AT_ONCE] + carries:
        copy.start()
    for copy in small:
        copy.wait()

    def request_of(slot):
        found = jnp.int32(0)
        for r in range(1, count):
            found = jnp.where(lax.rem(slot_ref[r], count) == slot, r, found)
        return found

    request = request_of(place)
    limit = length_ref[request] * kv_count

    def live(c):
        return limit > c * copy_rows

    for c in range(AT_ONCE, SUF_COPIES):
        pl.when(live(c))(k_copies[c].start)
    query = q_ref[request]
    lane = lax.broadcasted_iota(jnp.int32, (heads, LANES), 1)
    group = lax.broadcasted_iota(jnp.int32, (heads, LANES), 0) // (heads // kv_count)
    lane = jnp.where((lane % kv_count) == group, lane, rows)
    peak_ref[...] = jnp.full((heads, LANES), -1e30, jnp.float32)
    for c in range(SUF_COPIES):
        if c < AT_ONCE:
            k_copies[c].wait()

        @pl.when(live(c))
        def _(c=c):
            if c >= AT_ONCE:
                k_copies[c].wait()
            v_copies[c].start()
            peak = peak_ref[...]
            for at in range(c * copy_rows, (c + 1) * copy_rows, 2 * PIECE):
                part = lax.dot_general(
                    query, k_buf[at : at + 2 * PIECE], NT, preferred_element_type=jnp.float32
                )
                for begin in range(0, 2 * PIECE, LANES):
                    tile = jnp.where(lane < limit - (at + begin), part[:, begin : begin + LANES], -1e30)
                    score_ref[:, at + begin : at + begin + LANES] = tile
                    peak = jnp.maximum(peak, tile)
            peak_ref[...] = peak

    row_max = jnp.max(peak_ref[...], axis=1, keepdims=True)
    sum_ref[...] = jnp.zeros((heads, LANES), jnp.float32)
    acc_ref[...] = jnp.zeros((heads, width), jnp.float32)
    for c in range(SUF_COPIES):

        @pl.when(live(c))
        def _(c=c):
            v_copies[c].wait()
            part = slice(c * copy_rows, (c + 1) * copy_rows)
            sum_ref[...] += weigh(score_ref, weight_ref, part, row_max, score_scale * LOG2E)
            acc_ref[...] += jnp.dot(
                weight_ref[:, part], v_buf[part], preferred_element_type=jnp.float32
            )

    sums, acc = sum_ref[...], acc_ref[...]
    total = jnp.sum(sums, axis=1, keepdims=True)
    mixed = acc / total
    log = jnp.broadcast_to(row_max * score_scale + jnp.log(total), (heads, width))
    for carry in carries:
        carry.wait()
    if not last:
        mixed_ref[...] = mixed
        log_ref[...] = log
        return
    mixed_ref[request] = mixed
    log_ref[request] = log
    for slot in range(place):
        mixed_ref[request_of(slot)] = earlier[2 * slot][...]
        log_ref[request_of(slot)] = earlier[2 * slot + 1][...]


def suffix_partials(
    place, queries, keys, values, lengths, slots, carried, earlier, score_scale
):
    count, heads, width = queries.shape
    kv_count = keys.shape[2]
    rows = keys.shape[1] * kv_count
    result = (count, heads, width) if place == count - 1 else (heads, width)
    operands = (
        slots,
        lengths,
        queries,
        keys.reshape(count, rows, width),
        values.reshape(count, rows, width),
        *carried,
    )
    return pl.pallas_call(
        functools.partial(
            suffix_kernel,
            place=place,
            carried=len(carried),
            kv_count=kv_count,
            score_scale=score_scale,
        ),
        in_specs=[IN_HBM] * len(operands) + [IN_VMEM] * len(earlier),
        out_specs=[IN_VMEM] * (2 + len(carried)),
        out_shape=[pltpu.VMEM(result, jnp.float32)] * 2
        + [pltpu.VMEM(array.shape, array.dtype) for array in carried],
        scratch_shapes=[
            pltpu.SMEM((count,), jnp.int32),
            pltpu.SMEM((count,), jnp.int32),
            pltpu.VMEM((count, heads, width), queries.dtype),
            pltpu.VMEM((rows, width), keys.dtype),
            pltpu.VMEM((rows, width), values.dtype),
            pltpu.VMEM((heads, rows), jnp.float32),
            pltpu.VMEM((heads, rows), jnp.bfloat16),
            pltpu.VMEM((heads, LANES), jnp.float32),
            pltpu.VMEM((heads, LANES), jnp.float32),
            pltpu.VMEM((heads, width), jnp.float32),
            pltpu.SemaphoreType.DMA((2, SUF_COPIES)),
            pltpu.SemaphoreType.DMA((3 + len(carried),)),
        ],
        compiler_params=pltpu.CompilerParams(vmem_limit_bytes=SUFFIX_VMEM),
        cost_estimate=pl.CostEstimate(
            flops=4 * heads * rows * width,
            bytes_accessed=4 * rows * width,
            transcendentals=heads * rows,
        ),
        name=f"suffix_attention_{place}",
    )(*map(in_hbm, operands), *earlier)


def exponent(size, least):
    return jnp.floor(jnp.log2(jnp.maximum(size, least))) + 1.0


def prefix_kernel(
    q_ref, k0_ref, v0_ref, k1_ref, v1_ref, _, out_ref, score_ref, weight_ref, *, per_dest, score_scale
):
    width = q_ref.shape[1]
    tiles = q_ref.shape[0] // ROW_TILE
    dests = ROW_TILE // per_dest
    keys, values = (k0_ref, k1_ref), (v0_ref, v1_ref)
    units = [(tile, block) for tile in range(tiles) for block in range(2)]
    steps = out_ref.shape[0] // (tiles * dests)
    first_dest = 0 if steps == 1 else pl.program_id(0) * (tiles * dests)
    lane = lax.broadcasted_iota(jnp.int32, (per_dest, width), 1)
    row = lax.broadcasted_iota(jnp.int32, (per_dest, width), 0)
    diagonal = lane == row

    length = k0_ref.shape[0]

    def score(unit, slot):
        tile, block = unit
        query = q_ref[tile * ROW_TILE : (tile + 1) * ROW_TILE]
        peak = None
        for at in range(0, length, PIECE):
            part = lax.dot_general(
                query, keys[block][at : at + PIECE], NT, preferred_element_type=jnp.float32
            )
            score_ref[slot, :, at : at + PIECE] = part
            for begin in range(0, PIECE, LANES):
                lanes = part[:, begin : begin + LANES]
                peak = lanes if peak is None else jnp.maximum(peak, lanes)
        return jnp.max(peak, axis=1, keepdims=True)

    later_max = score(units[0], 0)
    held = None
    for step, (tile, block) in enumerate(units):
        row_max = later_max
        if step + 1 < len(units):
            later_max = score(units[step + 1], (step + 1) % 2)
        slot = step % 2
        sums = weigh(
            score_ref.at[slot], weight_ref.at[slot], slice(0, length), row_max, score_scale * LOG2E
        )
        total = jnp.sum(sums, axis=1, keepdims=True)
        acc = jnp.dot(weight_ref[slot], values[block][...], preferred_element_type=jnp.float32)
        if block == 0:
            held = (row_max, total, acc)
            continue
        max0, total0, acc0 = held
        top = jnp.maximum(max0, row_max)
        weight0 = jnp.exp((max0 - top) * score_scale)
        weight1 = jnp.exp((row_max - top) * score_scale)
        joined = weight0 * total0 + weight1 * total
        mixed = (weight0 * acc0 + weight1 * acc) / joined
        logs = jnp.broadcast_to(top * score_scale + jnp.log(joined), (ROW_TILE, width))
        peak = jnp.max(jnp.abs(mixed), axis=1, keepdims=True)
        coded = jnp.round(mixed * jnp.exp2(VALUE_BITS - exponent(peak, PEAK_LEAST)))
        most = 2.0**VALUE_BITS - 1
        coded = jnp.clip(coded, -most, most).astype(jnp.int32)
        peaks = jnp.broadcast_to(peak, (ROW_TILE, width))
        half = per_dest // 2
        for k in range(dests):
            rows = slice(k * per_dest, (k + 1) * per_dest)
            dest = first_dest + tile * dests + k
            high, low = coded[k * per_dest : k * per_dest + half], coded[k * per_dest + half : rows.stop]
            words = (high << 16) | (low & 0xFFFF)
            for j in range(half // TILE_ROWS):
                out_ref[dest, j] = words[j * TILE_ROWS : (j + 1) * TILE_ROWS]
            log_line = jnp.sum(jnp.where(diagonal, logs[rows], 0.0), axis=0, keepdims=True)
            peak_line = jnp.sum(jnp.where(diagonal, peaks[rows], 0.0), axis=0, keepdims=True)
            log_power = exponent(jnp.abs(log_line), LEAST)
            mantissa = jnp.round(log_line * jnp.exp2(LOG_BITS - log_power)).astype(jnp.int32)
            powers = log_power.astype(jnp.int32) << 16
            powers = powers | (exponent(peak_line, PEAK_LEAST).astype(jnp.int32) & 0xFFFF)
            out_ref[dest, half // TILE_ROWS] = jnp.concatenate([mantissa, powers], axis=0)


def prefix_partials(
    rows_q, keys, values, far_keys, far_values, after, per_dest, score_scale
):
    rows, width = rows_q.shape
    length = keys.shape[0]
    step_rows = min(STEP_ROWS, rows)
    out_piece = (per_dest // 2 // TILE_ROWS + 1, TILE_ROWS, width)
    blocked = {"in_specs": [IN_VMEM] * 5}
    if step_rows < rows:
        blocked["grid"] = (rows // step_rows,)
        blocked["in_specs"] = [pl.BlockSpec((step_rows, width), lambda i: (i, 0))]
        blocked["in_specs"] += [pl.BlockSpec((length, width), lambda i: (0, 0))] * 4
    blocked["in_specs"] += [pl.BlockSpec(memory_space=pl.ANY)]
    return pl.pallas_call(
        functools.partial(
            prefix_kernel, per_dest=per_dest, score_scale=score_scale
        ),
        **blocked,
        out_specs=IN_VMEM,
        out_shape=pltpu.VMEM((rows // per_dest, *out_piece), jnp.int32),
        scratch_shapes=[
            pltpu.VMEM((2, ROW_TILE, length), jnp.float32),
            pltpu.VMEM((2, ROW_TILE, length), jnp.bfloat16),
        ],
        compiler_params=pltpu.CompilerParams(vmem_limit_bytes=PREFIX_VMEM),
        cost_estimate=pl.CostEstimate(
            flops=8 * rows * length * width,
            bytes_accessed=8 * length * width + 6 * rows * width,
            transcendentals=2 * rows * length,
        ),
        name="prefix_attention",
    )(rows_q, keys, values, far_keys, far_values, after)


def join_kernel(got_ref, suf_ref, suf_log_ref, out_ref, log_ref, *, kv_count):
    count, heads, width = out_ref.shape
    group = heads // kv_count
    per_dest = count * group
    half = per_dest // 2
    parts = got_ref.shape[0] // kv_count
    lane = lax.broadcasted_iota(jnp.int32, (per_dest, width), 1)
    row = lax.broadcasted_iota(jnp.int32, (per_dest, width), 0)
    diagonal = lane == row

    def column(line):
        return jnp.sum(jnp.where(diagonal, line, 0.0), axis=1, keepdims=True)

    lines = [jnp.zeros((1, width), jnp.float32) for _ in range(count)]
    for place in range(kv_count):
        g = kv_count - 1 - place
        heads_of = slice(g * group, (g + 1) * group)
        suf_mixed = jnp.concatenate([suf_ref[r, heads_of] for r in range(count)], axis=0)
        suf_log = jnp.concatenate([suf_log_ref[r, heads_of] for r in range(count)], axis=0)
        logs, scales = [], []
        top = suf_log
        for s in range(parts):
            tail = got_ref[s * kv_count + place, half // TILE_ROWS]
            mantissa, powers = tail[0:1], tail[1:2]
            log_power = (powers >> 16).astype(jnp.float32)
            peak_power = ((powers << 16) >> 16).astype(jnp.float32)
            log_line = mantissa.astype(jnp.float32) * jnp.exp2(log_power - LOG_BITS)
            logs.append(jnp.broadcast_to(column(log_line), (per_dest, width)))
            scales.append(column(jnp.exp2(peak_power - VALUE_BITS)))
            top = jnp.maximum(top, logs[-1])
        weight = jnp.exp(suf_log - top)
        acc = weight * suf_mixed
        total = weight
        for s in range(parts):
            words = jnp.concatenate(
                [got_ref[s * kv_count + place, j] for j in range(half // TILE_ROWS)], axis=0
            )
            coded = jnp.concatenate([words >> 16, (words << 16) >> 16], axis=0)
            weight = jnp.exp(logs[s] - top)
            acc = acc + (weight * scales[s]) * coded.astype(jnp.float32)
            total = total + weight
        acc = acc / total
        logged = top + jnp.log(total)
        for r in range(count):
            rows = slice(r * group, (r + 1) * group)
            out_ref[r, heads_of] = acc[rows]
            spot = lane[:group] == row[:group] + g * group
            lines[r] = lines[r] + jnp.sum(jnp.where(spot, logged[rows], 0.0), axis=0, keepdims=True)
    for r in range(count):
        log_ref[r : r + 1] = lines[r][:, :heads]


def join_partials(got, suf_mixed, suf_log, kv_count):
    count, heads, width = suf_mixed.shape
    return pl.pallas_call(
        functools.partial(join_kernel, kv_count=kv_count),
        in_specs=[IN_VMEM] * 3,
        out_specs=[IN_VMEM] * 2,
        out_shape=[
            jax.ShapeDtypeStruct((count, heads, width), jnp.float32),
            jax.ShapeDtypeStruct((count, heads), jnp.float32),
        ],
        compiler_params=pltpu.CompilerParams(vmem_limit_bytes=SMALL_VMEM),
        name="join_partials",
    )(got, suf_mixed, suf_log)


def exchange(pieces, first):
    seq, head, rep = lax.axis_size("seq"), lax.axis_size("head"), lax.axis_size("rep")
    order = [(first - s) % seq for s in range(seq)]
    groups = [
        [(s * head + h) * rep + r for s in order for h in reversed(range(head))]
        for r in range(rep)
    ]
    return lax.all_to_all(
        pieces,
        ("seq", "head", "rep"),
        split_axis=0,
        concat_axis=0,
        axis_index_groups=groups,
        tiled=True,
    )


def per_device(
    queries, prefix_keys, prefix_values, suffix_keys, suffix_values, suffix_lengths, slot_map
):
    count, heads, width = queries.shape
    kv_count = suffix_keys.shape[2]
    per_dest = count * heads // kv_count
    score_scale = 1.0 / math.sqrt(width)
    sent = layout_queries(queries, kv_count, lax.axis_size("seq"))
    seq = lax.axis_size("seq")
    middle = seq // 2
    got_q = exchange(sent, middle)
    keys = prefix_keys[:, 0, :]
    values = prefix_values[:, 0, :]
    far_keys = lax.ppermute(keys, "rep", [(0, 1), (1, 0)])
    far_values = lax.ppermute(values, "rep", [(0, 1), (1, 0)])
    earlier = []
    for place in range(count):
        mixed, log, *brought = suffix_partials(
            place,
            queries,
            suffix_keys,
            suffix_values,
            suffix_lengths,
            slot_map,
            (keys, values) if place == 0 else (),
            earlier if place == count - 1 else (),
            score_scale,
        )
        earlier += [mixed, log]
        if brought:
            near_keys, near_values = brought
    partials = prefix_partials(
        got_q.reshape(-1, width),
        near_keys,
        near_values,
        far_keys,
        far_values,
        earlier[0],
        per_dest,
        score_scale,
    )
    got = exchange(partials, middle)
    return join_partials(got, mixed, log, kv_count)


def solution(mesh):
    by_request = P(("seq", "head", "rep"))
    by_block = P(("seq", "rep"), "head", None)
    placed = (by_request, by_block, by_block, by_request, by_request, by_request, by_request)
    return jax.shard_map(
        per_device,
        mesh=mesh,
        in_specs=placed,
        out_specs=(by_request, by_request),
        check_vma=False,
    )
```

```python
import functools
import math

import jax
import jax.numpy as jnp
from jax import lax
from jax.experimental import pallas as pl
from jax.experimental.pallas import tpu as pltpu
from jax.sharding import PartitionSpec as P

ROW_TILE = 128
STEP_ROWS = 512
SUF_COPIES = 4
AT_ONCE = 2
LANES = 128
PIECE = 256
TILE_ROWS = 2
VALUE_BITS = 15
LOG_BITS = 30
LOG2E = math.log2(math.e)
LEAST = 1e-25
PEAK_LEAST = 1e-33
NT = (((1,), (1,)), ((), ()))
PREFIX_VMEM = 14 * 1024 * 1024
SUFFIX_VMEM = 20 * 1024 * 1024
SMALL_VMEM = 8 * 1024 * 1024
IN_VMEM = pl.BlockSpec(memory_space=pltpu.VMEM)
IN_HBM = pl.BlockSpec(memory_space=pltpu.HBM)


def in_hbm(array):
    return pltpu.with_memory_space_constraint(array, pltpu.HBM)


def layout_kernel(q_hbm, sent_hbm, buf, in_sems, out_sems):
    groups = buf.shape[0]
    repeats = sent_hbm.shape[0] // groups
    reads = [
        pltpu.make_async_copy(q_hbm.at[:, g], buf.at[groups - 1 - g], in_sems.at[g])
        for g in range(groups)
    ]
    for read in reads:
        read.start()
    for read in reads:
        read.wait()
    writes = [
        pltpu.make_async_copy(buf, sent_hbm.at[pl.ds(s * groups, groups)], out_sems.at[s])
        for s in range(repeats)
    ]
    for write in writes:
        write.start()
    for write in writes:
        write.wait()


def layout_queries(queries, groups, repeats):
    count, heads, width = queries.shape
    group = heads // groups
    return pl.pallas_call(
        layout_kernel,
        in_specs=[IN_HBM],
        out_specs=IN_HBM,
        out_shape=pltpu.HBM((repeats * groups, count, group, width), queries.dtype),
        scratch_shapes=[
            pltpu.VMEM((groups, count, group, width), queries.dtype),
            pltpu.SemaphoreType.DMA((groups,)),
            pltpu.SemaphoreType.DMA((repeats,)),
        ],
        compiler_params=pltpu.CompilerParams(vmem_limit_bytes=SMALL_VMEM),
        name="layout_queries",
    )(in_hbm(queries.reshape(count, groups, group, width)))


def weigh(scores, weights, part, row_max, factor):
    sums = jnp.zeros((scores.shape[0], LANES), jnp.float32)
    for begin in range(part.start, part.stop, PIECE):
        piece = slice(begin, begin + PIECE)
        terms = jnp.exp2((scores[:, piece] - row_max) * factor)
        weights[:, piece] = terms.astype(jnp.bfloat16)
        for lane in range(0, PIECE, LANES):
            sums = sums + terms[:, lane : lane + LANES]
    return sums


def suffix_kernel(*refs, place, carried, kv_count, score_scale):
    slot_hbm, length_hbm, q_hbm, k_hbm, v_hbm = refs[:5]
    refs = refs[5:]
    count, heads, width = q_hbm.shape
    carried_refs, refs = refs[:carried], refs[carried:]
    last = place == count - 1
    earlier, refs = (refs[: 2 * place], refs[2 * place :]) if last else ((), refs)
    mixed_ref, log_ref = refs[:2]
    brought_refs, refs = refs[2 : 2 + carried], refs[2 + carried :]
    slot_ref, length_ref, q_ref, k_buf, v_buf, score_ref, weight_ref = refs[:7]
    peak_ref, sum_ref, acc_ref, sems, small_sems = refs[7:]
    rows = k_hbm.shape[1]
    copy_rows = rows // SUF_COPIES
    copies = []
    for which, (source, target) in enumerate(((k_hbm, k_buf), (v_hbm, v_buf))):
        for c in range(SUF_COPIES):
            part = pl.ds(c * copy_rows, copy_rows)
            copies.append(
                pltpu.make_async_copy(source.at[place, part], target.at[part], sems.at[which, c])
            )
    k_copies, v_copies = copies[:SUF_COPIES], copies[SUF_COPIES:]
    small = [
        pltpu.make_async_copy(source, target, small_sems.at[i])
        for i, (source, target) in enumerate(
            [(slot_hbm, slot_ref), (length_hbm, length_ref), (q_hbm, q_ref)]
            + list(zip(carried_refs, brought_refs))
        )
    ]
    small, carries = small[:3], small[3:]
    for copy in small + k_copies[:AT_ONCE] + carries:
        copy.start()
    for copy in small:
        copy.wait()

    def request_of(slot):
        found = jnp.int32(0)
        for r in range(1, count):
            found = jnp.where(lax.rem(slot_ref[r], count) == slot, r, found)
        return found

    request = request_of(place)
    limit = length_ref[request] * kv_count

    def live(c):
        return limit > c * copy_rows

    for c in range(AT_ONCE, SUF_COPIES):
        pl.when(live(c))(k_copies[c].start)
    query = q_ref[request]
    lane = lax.broadcasted_iota(jnp.int32, (heads, LANES), 1)
    group = lax.broadcasted_iota(jnp.int32, (heads, LANES), 0) // (heads // kv_count)
    lane = jnp.where((lane % kv_count) == group, lane, rows)
    peak_ref[...] = jnp.full((heads, LANES), -1e30, jnp.float32)
    for c in range(SUF_COPIES):
        if c < AT_ONCE:
            k_copies[c].wait()

        @pl.when(live(c))
        def _(c=c):
            if c >= AT_ONCE:
                k_copies[c].wait()
            v_copies[c].start()
            peak = peak_ref[...]
            for at in range(c * copy_rows, (c + 1) * copy_rows, 2 * PIECE):
                part = lax.dot_general(
                    query, k_buf[at : at + 2 * PIECE], NT, preferred_element_type=jnp.float32
                )
                for begin in range(0, 2 * PIECE, LANES):
                    tile = jnp.where(lane < limit - (at + begin), part[:, begin : begin + LANES], -1e30)
                    score_ref[:, at + begin : at + begin + LANES] = tile
                    peak = jnp.maximum(peak, tile)
            peak_ref[...] = peak

    row_max = jnp.max(peak_ref[...], axis=1, keepdims=True)
    sum_ref[...] = jnp.zeros((heads, LANES), jnp.float32)
    acc_ref[...] = jnp.zeros((heads, width), jnp.float32)
    for c in range(SUF_COPIES):

        @pl.when(live(c))
        def _(c=c):
            v_copies[c].wait()
            part = slice(c * copy_rows, (c + 1) * copy_rows)
            sum_ref[...] += weigh(score_ref, weight_ref, part, row_max, score_scale * LOG2E)
            acc_ref[...] += jnp.dot(
                weight_ref[:, part], v_buf[part], preferred_element_type=jnp.float32
            )

    sums, acc = sum_ref[...], acc_ref[...]
    total = jnp.sum(sums, axis=1, keepdims=True)
    mixed = acc / total
    log = jnp.broadcast_to(row_max * score_scale + jnp.log(total), (heads, width))
    for carry in carries:
        carry.wait()
    if not last:
        mixed_ref[...] = mixed
        log_ref[...] = log
        return
    mixed_ref[request] = mixed
    log_ref[request] = log
    for slot in range(place):
        mixed_ref[request_of(slot)] = earlier[2 * slot][...]
        log_ref[request_of(slot)] = earlier[2 * slot + 1][...]


def suffix_partials(
    place, queries, keys, values, lengths, slots, carried, earlier, score_scale
):
    count, heads, width = queries.shape
    kv_count = keys.shape[2]
    rows = keys.shape[1] * kv_count
    result = (count, heads, width) if place == count - 1 else (heads, width)
    operands = (
        slots,
        lengths,
        queries,
        keys.reshape(count, rows, width),
        values.reshape(count, rows, width),
        *carried,
    )
    return pl.pallas_call(
        functools.partial(
            suffix_kernel,
            place=place,
            carried=len(carried),
            kv_count=kv_count,
            score_scale=score_scale,
        ),
        in_specs=[IN_HBM] * len(operands) + [IN_VMEM] * len(earlier),
        out_specs=[IN_VMEM] * (2 + len(carried)),
        out_shape=[pltpu.VMEM(result, jnp.float32)] * 2
        + [pltpu.VMEM(array.shape, array.dtype) for array in carried],
        scratch_shapes=[
            pltpu.SMEM((count,), jnp.int32),
            pltpu.SMEM((count,), jnp.int32),
            pltpu.VMEM((count, heads, width), queries.dtype),
            pltpu.VMEM((rows, width), keys.dtype),
            pltpu.VMEM((rows, width), values.dtype),
            pltpu.VMEM((heads, rows), jnp.float32),
            pltpu.VMEM((heads, rows), jnp.bfloat16),
            pltpu.VMEM((heads, LANES), jnp.float32),
            pltpu.VMEM((heads, LANES), jnp.float32),
            pltpu.VMEM((heads, width), jnp.float32),
            pltpu.SemaphoreType.DMA((2, SUF_COPIES)),
            pltpu.SemaphoreType.DMA((3 + len(carried),)),
        ],
        compiler_params=pltpu.CompilerParams(vmem_limit_bytes=SUFFIX_VMEM),
        cost_estimate=pl.CostEstimate(
            flops=4 * heads * rows * width,
            bytes_accessed=4 * rows * width,
            transcendentals=heads * rows,
        ),
        name=f"suffix_attention_{place}",
    )(*map(in_hbm, operands), *earlier)


def exponent(size, least):
    return jnp.floor(jnp.log2(jnp.maximum(size, least))) + 1.0


def prefix_kernel(
    q_ref, k0_ref, v0_ref, k1_ref, v1_ref, _, out_hbm, out_ref, score_ref, weight_ref, sems, *, per_dest, score_scale
):
    width = q_ref.shape[1]
    tiles = q_ref.shape[0] // ROW_TILE
    dests = ROW_TILE // per_dest
    keys, values = (k0_ref, k1_ref), (v0_ref, v1_ref)
    units = [(tile, block) for tile in range(tiles) for block in range(2)]
    first_dest = 0 if out_hbm.shape == out_ref.shape else pl.program_id(0) * (tiles * dests)
    copies = []
    lane = lax.broadcasted_iota(jnp.int32, (per_dest, width), 1)
    row = lax.broadcasted_iota(jnp.int32, (per_dest, width), 0)
    diagonal = lane == row

    length = k0_ref.shape[0]

    def score(unit, slot):
        tile, block = unit
        query = q_ref[tile * ROW_TILE : (tile + 1) * ROW_TILE]
        peak = None
        for at in range(0, length, PIECE):
            part = lax.dot_general(
                query, keys[block][at : at + PIECE], NT, preferred_element_type=jnp.float32
            )
            score_ref[slot, :, at : at + PIECE] = part
            for begin in range(0, PIECE, LANES):
                lanes = part[:, begin : begin + LANES]
                peak = lanes if peak is None else jnp.maximum(peak, lanes)
        return jnp.max(peak, axis=1, keepdims=True)

    later_max = score(units[0], 0)
    held = None
    for step, (tile, block) in enumerate(units):
        row_max = later_max
        if step + 1 < len(units):
            later_max = score(units[step + 1], (step + 1) % 2)
        slot = step % 2
        sums = weigh(
            score_ref.at[slot], weight_ref.at[slot], slice(0, length), row_max, score_scale * LOG2E
        )
        total = jnp.sum(sums, axis=1, keepdims=True)
        acc = jnp.dot(weight_ref[slot], values[block][...], preferred_element_type=jnp.float32)
        if block == 0:
            held = (row_max, total, acc)
            continue
        max0, total0, acc0 = held
        top = jnp.maximum(max0, row_max)
        weight0 = jnp.exp((max0 - top) * score_scale)
        weight1 = jnp.exp((row_max - top) * score_scale)
        joined = weight0 * total0 + weight1 * total
        mixed = (weight0 * acc0 + weight1 * acc) / joined
        logs = jnp.broadcast_to(top * score_scale + jnp.log(joined), (ROW_TILE, width))
        peak = jnp.max(jnp.abs(mixed), axis=1, keepdims=True)
        coded = jnp.round(mixed * jnp.exp2(VALUE_BITS - exponent(peak, PEAK_LEAST)))
        most = 2.0**VALUE_BITS - 1
        coded = jnp.clip(coded, -most, most).astype(jnp.int32)
        peaks = jnp.broadcast_to(peak, (ROW_TILE, width))
        half = per_dest // 2
        for k in range(dests):
            rows = slice(k * per_dest, (k + 1) * per_dest)
            dest = tile * dests + k
            high, low = coded[k * per_dest : k * per_dest + half], coded[k * per_dest + half : rows.stop]
            words = (high << 16) | (low & 0xFFFF)
            for j in range(half // TILE_ROWS):
                out_ref[dest, j] = words[j * TILE_ROWS : (j + 1) * TILE_ROWS]
            log_line = jnp.sum(jnp.where(diagonal, logs[rows], 0.0), axis=0, keepdims=True)
            peak_line = jnp.sum(jnp.where(diagonal, peaks[rows], 0.0), axis=0, keepdims=True)
            log_power = exponent(jnp.abs(log_line), LEAST)
            mantissa = jnp.round(log_line * jnp.exp2(LOG_BITS - log_power)).astype(jnp.int32)
            powers = log_power.astype(jnp.int32) << 16
            powers = powers | (exponent(peak_line, PEAK_LEAST).astype(jnp.int32) & 0xFFFF)
            out_ref[dest, half // TILE_ROWS] = jnp.concatenate([mantissa, powers], axis=0)
        ready = pl.ds(tile * dests, dests)
        copies.append(
            pltpu.make_async_copy(
                out_ref.at[ready],
                out_hbm.at[pl.ds(first_dest + tile * dests, dests)],
                sems.at[tile],
            )
        )
        copies[-1].start()
    for copy in copies:
        copy.wait()


def prefix_partials(
    rows_q, keys, values, far_keys, far_values, after, per_dest, score_scale
):
    rows, width = rows_q.shape
    length = keys.shape[0]
    step_rows = min(STEP_ROWS, rows)
    dests = step_rows // per_dest
    out_piece = (per_dest // 2 // TILE_ROWS + 1, TILE_ROWS, width)
    blocked = {"in_specs": [IN_VMEM] * 5}
    if step_rows < rows:
        blocked["grid"] = (rows // step_rows,)
        blocked["in_specs"] = [pl.BlockSpec((step_rows, width), lambda i: (i, 0))]
        blocked["in_specs"] += [pl.BlockSpec((length, width), lambda i: (0, 0))] * 4
    blocked["in_specs"] += [pl.BlockSpec(memory_space=pl.ANY)]
    return pl.pallas_call(
        functools.partial(
            prefix_kernel, per_dest=per_dest, score_scale=score_scale
        ),
        **blocked,
        out_specs=IN_HBM,
        out_shape=pltpu.HBM((rows // per_dest, *out_piece), jnp.int32),
        scratch_shapes=[
            pltpu.VMEM((dests, *out_piece), jnp.int32),
            pltpu.VMEM((2, ROW_TILE, length), jnp.float32),
            pltpu.VMEM((2, ROW_TILE, length), jnp.bfloat16),
            pltpu.SemaphoreType.DMA((step_rows // ROW_TILE,)),
        ],
        compiler_params=pltpu.CompilerParams(vmem_limit_bytes=PREFIX_VMEM),
        cost_estimate=pl.CostEstimate(
            flops=8 * rows * length * width,
            bytes_accessed=8 * length * width + 6 * rows * width,
            transcendentals=2 * rows * length,
        ),
        name="prefix_attention",
    )(rows_q, keys, values, far_keys, far_values, after)


def join_kernel(got_ref, suf_ref, suf_log_ref, out_ref, log_ref, *, kv_count):
    count, heads, width = out_ref.shape
    group = heads // kv_count
    per_dest = count * group
    half = per_dest // 2
    parts = got_ref.shape[0] // kv_count
    lane = lax.broadcasted_iota(jnp.int32, (per_dest, width), 1)
    row = lax.broadcasted_iota(jnp.int32, (per_dest, width), 0)
    diagonal = lane == row

    def column(line):
        return jnp.sum(jnp.where(diagonal, line, 0.0), axis=1, keepdims=True)

    lines = [jnp.zeros((1, width), jnp.float32) for _ in range(count)]
    for place in range(kv_count):
        g = kv_count - 1 - place
        heads_of = slice(g * group, (g + 1) * group)
        suf_mixed = jnp.concatenate([suf_ref[r, heads_of] for r in range(count)], axis=0)
        suf_log = jnp.concatenate([suf_log_ref[r, heads_of] for r in range(count)], axis=0)
        logs, scales = [], []
        top = suf_log
        for s in range(parts):
            tail = got_ref[s * kv_count + place, half // TILE_ROWS]
            mantissa, powers = tail[0:1], tail[1:2]
            log_power = (powers >> 16).astype(jnp.float32)
            peak_power = ((powers << 16) >> 16).astype(jnp.float32)
            log_line = mantissa.astype(jnp.float32) * jnp.exp2(log_power - LOG_BITS)
            logs.append(jnp.broadcast_to(column(log_line), (per_dest, width)))
            scales.append(column(jnp.exp2(peak_power - VALUE_BITS)))
            top = jnp.maximum(top, logs[-1])
        weight = jnp.exp(suf_log - top)
        acc = weight * suf_mixed
        total = weight
        for s in range(parts):
            words = jnp.concatenate(
                [got_ref[s * kv_count + place, j] for j in range(half // TILE_ROWS)], axis=0
            )
            coded = jnp.concatenate([words >> 16, (words << 16) >> 16], axis=0)
            weight = jnp.exp(logs[s] - top)
            acc = acc + (weight * scales[s]) * coded.astype(jnp.float32)
            total = total + weight
        acc = acc / total
        logged = top + jnp.log(total)
        for r in range(count):
            rows = slice(r * group, (r + 1) * group)
            out_ref[r, heads_of] = acc[rows]
            spot = lane[:group] == row[:group] + g * group
            lines[r] = lines[r] + jnp.sum(jnp.where(spot, logged[rows], 0.0), axis=0, keepdims=True)
    for r in range(count):
        log_ref[r : r + 1] = lines[r][:, :heads]


def join_partials(got, suf_mixed, suf_log, kv_count):
    count, heads, width = suf_mixed.shape
    return pl.pallas_call(
        functools.partial(join_kernel, kv_count=kv_count),
        in_specs=[IN_VMEM] * 3,
        out_specs=[IN_VMEM] * 2,
        out_shape=[
            jax.ShapeDtypeStruct((count, heads, width), jnp.float32),
            jax.ShapeDtypeStruct((count, heads), jnp.float32),
        ],
        compiler_params=pltpu.CompilerParams(vmem_limit_bytes=SMALL_VMEM),
        name="join_partials",
    )(got, suf_mixed, suf_log)


def exchange(pieces, first):
    seq, head, rep = lax.axis_size("seq"), lax.axis_size("head"), lax.axis_size("rep")
    order = [(first - s) % seq for s in range(seq)]
    groups = [
        [(s * head + h) * rep + r for s in order for h in reversed(range(head))]
        for r in range(rep)
    ]
    return lax.all_to_all(
        pieces,
        ("seq", "head", "rep"),
        split_axis=0,
        concat_axis=0,
        axis_index_groups=groups,
        tiled=True,
    )


def per_device(
    queries, prefix_keys, prefix_values, suffix_keys, suffix_values, suffix_lengths, slot_map
):
    count, heads, width = queries.shape
    kv_count = suffix_keys.shape[2]
    per_dest = count * heads // kv_count
    score_scale = 1.0 / math.sqrt(width)
    sent = layout_queries(queries, kv_count, lax.axis_size("seq"))
    seq = lax.axis_size("seq")
    middle = (seq - 1) // 2
    got_q = exchange(sent, middle)
    keys = prefix_keys[:, 0, :]
    values = prefix_values[:, 0, :]
    far_keys = lax.ppermute(keys, "rep", [(0, 1), (1, 0)])
    far_values = lax.ppermute(values, "rep", [(0, 1), (1, 0)])
    earlier = []
    for place in range(count):
        mixed, log, *brought = suffix_partials(
            place,
            queries,
            suffix_keys,
            suffix_values,
            suffix_lengths,
            slot_map,
            (keys, values) if place == 0 else (),
            earlier if place == count - 1 else (),
            score_scale,
        )
        earlier += [mixed, log]
        if brought:
            near_keys, near_values = brought
    partials = prefix_partials(
        got_q.reshape(-1, width),
        near_keys,
        near_values,
        far_keys,
        far_values,
        earlier[0],
        per_dest,
        score_scale,
    )
    got = exchange(partials, middle)
    return join_partials(got, mixed, log, kv_count)


def solution(mesh):
    by_request = P(("seq", "head", "rep"))
    by_block = P(("seq", "rep"), "head", None)
    placed = (by_request, by_block, by_block, by_request, by_request, by_request, by_request)
    return jax.shard_map(
        per_device,
        mesh=mesh,
        in_specs=placed,
        out_specs=(by_request, by_request),
        check_vma=False,
    )
```

```python
import functools
import math

import jax
import jax.numpy as jnp
from jax import lax
from jax.experimental import pallas as pl
from jax.experimental.pallas import tpu as pltpu
from jax.sharding import PartitionSpec as P

ROW_TILE = 128
STEP_ROWS = 512
SUF_COPIES = 4
AT_ONCE = 2
LANES = 128
PIECE = 256
TILE_ROWS = 2
VALUE_BITS = 15
LOG_BITS = 30
LOG2E = math.log2(math.e)
LEAST = 1e-25
PEAK_LEAST = 1e-33
NT = (((1,), (1,)), ((), ()))
PREFIX_VMEM = 14 * 1024 * 1024
SUFFIX_VMEM = 20 * 1024 * 1024
SMALL_VMEM = 8 * 1024 * 1024
IN_VMEM = pl.BlockSpec(memory_space=pltpu.VMEM)
IN_HBM = pl.BlockSpec(memory_space=pltpu.HBM)


def in_hbm(array):
    return pltpu.with_memory_space_constraint(array, pltpu.HBM)


def layout_kernel(q_hbm, sent_hbm, buf, in_sems, out_sems):
    groups = buf.shape[0]
    repeats = sent_hbm.shape[0] // groups
    reads = [
        pltpu.make_async_copy(q_hbm.at[:, g], buf.at[groups - 1 - g], in_sems.at[g])
        for g in range(groups)
    ]
    for read in reads:
        read.start()
    for read in reads:
        read.wait()
    writes = [
        pltpu.make_async_copy(buf, sent_hbm.at[pl.ds(s * groups, groups)], out_sems.at[s])
        for s in range(repeats)
    ]
    for write in writes:
        write.start()
    for write in writes:
        write.wait()


def layout_queries(queries, groups, repeats):
    count, heads, width = queries.shape
    group = heads // groups
    return pl.pallas_call(
        layout_kernel,
        in_specs=[IN_HBM],
        out_specs=IN_HBM,
        out_shape=pltpu.HBM((repeats * groups, count, group, width), queries.dtype),
        scratch_shapes=[
            pltpu.VMEM((groups, count, group, width), queries.dtype),
            pltpu.SemaphoreType.DMA((groups,)),
            pltpu.SemaphoreType.DMA((repeats,)),
        ],
        compiler_params=pltpu.CompilerParams(vmem_limit_bytes=SMALL_VMEM),
        name="layout_queries",
    )(in_hbm(queries.reshape(count, groups, group, width)))


def weigh(scores, weights, part, row_max, factor):
    sums = jnp.zeros((scores.shape[0], LANES), jnp.float32)
    for begin in range(part.start, part.stop, PIECE):
        piece = slice(begin, begin + PIECE)
        terms = jnp.exp2((scores[:, piece] - row_max) * factor)
        weights[:, piece] = terms.astype(jnp.bfloat16)
        for lane in range(0, PIECE, LANES):
            sums = sums + terms[:, lane : lane + LANES]
    return sums


def suffix_kernel(*refs, place, carried, kv_count, score_scale):
    slot_hbm, length_hbm, q_hbm, k_hbm, v_hbm = refs[:5]
    refs = refs[5:]
    count, heads, width = q_hbm.shape
    carried_refs, refs = refs[:carried], refs[carried:]
    last = place == count - 1
    earlier, refs = (refs[: 2 * place], refs[2 * place :]) if last else ((), refs)
    mixed_ref, log_ref = refs[:2]
    brought_refs, refs = refs[2 : 2 + carried], refs[2 + carried :]
    slot_ref, length_ref, q_ref, k_buf, v_buf, score_ref, weight_ref = refs[:7]
    peak_ref, sum_ref, acc_ref, sems, small_sems = refs[7:]
    rows = k_hbm.shape[1]
    copy_rows = rows // SUF_COPIES
    copies = []
    for which, (source, target) in enumerate(((k_hbm, k_buf), (v_hbm, v_buf))):
        for c in range(SUF_COPIES):
            part = pl.ds(c * copy_rows, copy_rows)
            copies.append(
                pltpu.make_async_copy(source.at[place, part], target.at[part], sems.at[which, c])
            )
    k_copies, v_copies = copies[:SUF_COPIES], copies[SUF_COPIES:]
    small = [
        pltpu.make_async_copy(source, target, small_sems.at[i])
        for i, (source, target) in enumerate(
            [(slot_hbm, slot_ref), (length_hbm, length_ref), (q_hbm, q_ref)]
            + list(zip(carried_refs, brought_refs))
        )
    ]
    small, carries = small[:3], small[3:]
    for copy in small + k_copies[:AT_ONCE] + carries:
        copy.start()
    for copy in small:
        copy.wait()

    def request_of(slot):
        found = jnp.int32(0)
        for r in range(1, count):
            found = jnp.where(lax.rem(slot_ref[r], count) == slot, r, found)
        return found

    request = request_of(place)
    limit = length_ref[request] * kv_count

    def live(c):
        return limit > c * copy_rows

    for c in range(AT_ONCE, SUF_COPIES):
        pl.when(live(c))(k_copies[c].start)
    query = q_ref[request]
    lane = lax.broadcasted_iota(jnp.int32, (heads, LANES), 1)
    group = lax.broadcasted_iota(jnp.int32, (heads, LANES), 0) // (heads // kv_count)
    lane = jnp.where((lane % kv_count) == group, lane, rows)
    peak_ref[...] = jnp.full((heads, LANES), -1e30, jnp.float32)
    for c in range(SUF_COPIES):
        if c < AT_ONCE:
            k_copies[c].wait()

        @pl.when(live(c))
        def _(c=c):
            if c >= AT_ONCE:
                k_copies[c].wait()
            v_copies[c].start()
            peak = peak_ref[...]
            for at in range(c * copy_rows, (c + 1) * copy_rows, 2 * PIECE):
                part = lax.dot_general(
                    query, k_buf[at : at + 2 * PIECE], NT, preferred_element_type=jnp.float32
                )
                for begin in range(0, 2 * PIECE, LANES):
                    tile = jnp.where(lane < limit - (at + begin), part[:, begin : begin + LANES], -1e30)
                    score_ref[:, at + begin : at + begin + LANES] = tile
                    peak = jnp.maximum(peak, tile)
            peak_ref[...] = peak

    row_max = jnp.max(peak_ref[...], axis=1, keepdims=True)
    sum_ref[...] = jnp.zeros((heads, LANES), jnp.float32)
    acc_ref[...] = jnp.zeros((heads, width), jnp.float32)
    for c in range(SUF_COPIES):

        @pl.when(live(c))
        def _(c=c):
            v_copies[c].wait()
            part = slice(c * copy_rows, (c + 1) * copy_rows)
            sum_ref[...] += weigh(score_ref, weight_ref, part, row_max, score_scale * LOG2E)
            acc_ref[...] += jnp.dot(
                weight_ref[:, part], v_buf[part], preferred_element_type=jnp.float32
            )

    sums, acc = sum_ref[...], acc_ref[...]
    total = jnp.sum(sums, axis=1, keepdims=True)
    mixed = acc / total
    log = jnp.broadcast_to(row_max * score_scale + jnp.log(total), (heads, width))
    for carry in carries:
        carry.wait()
    if not last:
        mixed_ref[...] = mixed
        log_ref[...] = log
        return
    mixed_ref[request] = mixed
    log_ref[request] = log
    for slot in range(place):
        mixed_ref[request_of(slot)] = earlier[2 * slot][...]
        log_ref[request_of(slot)] = earlier[2 * slot + 1][...]


def suffix_partials(
    place, queries, keys, values, lengths, slots, carried, earlier, score_scale
):
    count, heads, width = queries.shape
    kv_count = keys.shape[2]
    rows = keys.shape[1] * kv_count
    result = (count, heads, width) if place == count - 1 else (heads, width)
    operands = (
        slots,
        lengths,
        queries,
        keys.reshape(count, rows, width),
        values.reshape(count, rows, width),
        *carried,
    )
    return pl.pallas_call(
        functools.partial(
            suffix_kernel,
            place=place,
            carried=len(carried),
            kv_count=kv_count,
            score_scale=score_scale,
        ),
        in_specs=[IN_HBM] * len(operands) + [IN_VMEM] * len(earlier),
        out_specs=[IN_VMEM] * (2 + len(carried)),
        out_shape=[pltpu.VMEM(result, jnp.float32)] * 2
        + [pltpu.VMEM(array.shape, array.dtype) for array in carried],
        scratch_shapes=[
            pltpu.SMEM((count,), jnp.int32),
            pltpu.SMEM((count,), jnp.int32),
            pltpu.VMEM((count, heads, width), queries.dtype),
            pltpu.VMEM((rows, width), keys.dtype),
            pltpu.VMEM((rows, width), values.dtype),
            pltpu.VMEM((heads, rows), jnp.float32),
            pltpu.VMEM((heads, rows), jnp.bfloat16),
            pltpu.VMEM((heads, LANES), jnp.float32),
            pltpu.VMEM((heads, LANES), jnp.float32),
            pltpu.VMEM((heads, width), jnp.float32),
            pltpu.SemaphoreType.DMA((2, SUF_COPIES)),
            pltpu.SemaphoreType.DMA((3 + len(carried),)),
        ],
        compiler_params=pltpu.CompilerParams(vmem_limit_bytes=SUFFIX_VMEM),
        cost_estimate=pl.CostEstimate(
            flops=4 * heads * rows * width,
            bytes_accessed=4 * rows * width,
            transcendentals=heads * rows,
        ),
        name=f"suffix_attention_{place}",
    )(*map(in_hbm, operands), *earlier)


def exponent(size, least):
    return jnp.floor(jnp.log2(jnp.maximum(size, least))) + 1.0


def prefix_kernel(
    q_ref, k0_ref, v0_ref, k1_ref, v1_ref, _, out_hbm, out_ref, score_ref, weight_ref, sems, *, per_dest, turn, score_scale
):
    width = q_ref.shape[1]
    tiles = q_ref.shape[0] // ROW_TILE
    dests = ROW_TILE // per_dest
    keys, values = (k0_ref, k1_ref), (v0_ref, v1_ref)
    units = [(tile, block) for tile in range(tiles) for block in range(2)]
    places = out_hbm.shape[0] // dests
    first_place = turn + (0 if out_hbm.shape == out_ref.shape else pl.program_id(0) * tiles)
    copies = []
    lane = lax.broadcasted_iota(jnp.int32, (per_dest, width), 1)
    row = lax.broadcasted_iota(jnp.int32, (per_dest, width), 0)
    diagonal = lane == row

    length = k0_ref.shape[0]

    def score(unit, slot):
        tile, block = unit
        query = q_ref[tile * ROW_TILE : (tile + 1) * ROW_TILE]
        peak = None
        for at in range(0, length, PIECE):
            part = lax.dot_general(
                query, keys[block][at : at + PIECE], NT, preferred_element_type=jnp.float32
            )
            score_ref[slot, :, at : at + PIECE] = part
            for begin in range(0, PIECE, LANES):
                lanes = part[:, begin : begin + LANES]
                peak = lanes if peak is None else jnp.maximum(peak, lanes)
        return jnp.max(peak, axis=1, keepdims=True)

    later_max = score(units[0], 0)
    held = None
    for step, (tile, block) in enumerate(units):
        row_max = later_max
        if step + 1 < len(units):
            later_max = score(units[step + 1], (step + 1) % 2)
        slot = step % 2
        sums = weigh(
            score_ref.at[slot], weight_ref.at[slot], slice(0, length), row_max, score_scale * LOG2E
        )
        total = jnp.sum(sums, axis=1, keepdims=True)
        acc = jnp.dot(weight_ref[slot], values[block][...], preferred_element_type=jnp.float32)
        if block == 0:
            held = (row_max, total, acc)
            continue
        max0, total0, acc0 = held
        top = jnp.maximum(max0, row_max)
        weight0 = jnp.exp((max0 - top) * score_scale)
        weight1 = jnp.exp((row_max - top) * score_scale)
        joined = weight0 * total0 + weight1 * total
        mixed = (weight0 * acc0 + weight1 * acc) / joined
        logs = jnp.broadcast_to(top * score_scale + jnp.log(joined), (ROW_TILE, width))
        peak = jnp.max(jnp.abs(mixed), axis=1, keepdims=True)
        coded = jnp.round(mixed * jnp.exp2(VALUE_BITS - exponent(peak, PEAK_LEAST)))
        most = 2.0**VALUE_BITS - 1
        coded = jnp.clip(coded, -most, most).astype(jnp.int32)
        peaks = jnp.broadcast_to(peak, (ROW_TILE, width))
        half = per_dest // 2
        for k in range(dests):
            rows = slice(k * per_dest, (k + 1) * per_dest)
            dest = tile * dests + k
            high, low = coded[k * per_dest : k * per_dest + half], coded[k * per_dest + half : rows.stop]
            words = (high << 16) | (low & 0xFFFF)
            for j in range(half // TILE_ROWS):
                out_ref[dest, j] = words[j * TILE_ROWS : (j + 1) * TILE_ROWS]
            log_line = jnp.sum(jnp.where(diagonal, logs[rows], 0.0), axis=0, keepdims=True)
            peak_line = jnp.sum(jnp.where(diagonal, peaks[rows], 0.0), axis=0, keepdims=True)
            log_power = exponent(jnp.abs(log_line), LEAST)
            mantissa = jnp.round(log_line * jnp.exp2(LOG_BITS - log_power)).astype(jnp.int32)
            powers = log_power.astype(jnp.int32) << 16
            powers = powers | (exponent(peak_line, PEAK_LEAST).astype(jnp.int32) & 0xFFFF)
            out_ref[dest, half // TILE_ROWS] = jnp.concatenate([mantissa, powers], axis=0)
        ready = pl.ds(tile * dests, dests)
        copies.append(
            pltpu.make_async_copy(
                out_ref.at[ready],
                out_hbm.at[pl.ds(lax.rem(first_place + tile, places) * dests, dests)],
                sems.at[tile],
            )
        )
        copies[-1].start()
    for copy in copies:
        copy.wait()


def prefix_partials(
    rows_q, keys, values, far_keys, far_values, after, per_dest, turn, score_scale
):
    rows, width = rows_q.shape
    length = keys.shape[0]
    step_rows = min(STEP_ROWS, rows)
    dests = step_rows // per_dest
    out_piece = (per_dest // 2 // TILE_ROWS + 1, TILE_ROWS, width)
    blocked = {"in_specs": [IN_VMEM] * 5}
    if step_rows < rows:
        blocked["grid"] = (rows // step_rows,)
        blocked["in_specs"] = [pl.BlockSpec((step_rows, width), lambda i: (i, 0))]
        blocked["in_specs"] += [pl.BlockSpec((length, width), lambda i: (0, 0))] * 4
    blocked["in_specs"] += [pl.BlockSpec(memory_space=pl.ANY)]
    return pl.pallas_call(
        functools.partial(
            prefix_kernel, per_dest=per_dest, turn=turn, score_scale=score_scale
        ),
        **blocked,
        out_specs=IN_HBM,
        out_shape=pltpu.HBM((rows // per_dest, *out_piece), jnp.int32),
        scratch_shapes=[
            pltpu.VMEM((dests, *out_piece), jnp.int32),
            pltpu.VMEM((2, ROW_TILE, length), jnp.float32),
            pltpu.VMEM((2, ROW_TILE, length), jnp.bfloat16),
            pltpu.SemaphoreType.DMA((step_rows // ROW_TILE,)),
        ],
        compiler_params=pltpu.CompilerParams(vmem_limit_bytes=PREFIX_VMEM),
        cost_estimate=pl.CostEstimate(
            flops=8 * rows * length * width,
            bytes_accessed=8 * length * width + 6 * rows * width,
            transcendentals=2 * rows * length,
        ),
        name="prefix_attention",
    )(rows_q, keys, values, far_keys, far_values, after)


def join_kernel(got_ref, suf_ref, suf_log_ref, out_ref, log_ref, *, kv_count):
    count, heads, width = out_ref.shape
    group = heads // kv_count
    per_dest = count * group
    half = per_dest // 2
    parts = got_ref.shape[0] // kv_count
    lane = lax.broadcasted_iota(jnp.int32, (per_dest, width), 1)
    row = lax.broadcasted_iota(jnp.int32, (per_dest, width), 0)
    diagonal = lane == row

    def column(line):
        return jnp.sum(jnp.where(diagonal, line, 0.0), axis=1, keepdims=True)

    lines = [jnp.zeros((1, width), jnp.float32) for _ in range(count)]
    for place in range(kv_count):
        g = kv_count - 1 - place
        heads_of = slice(g * group, (g + 1) * group)
        suf_mixed = jnp.concatenate([suf_ref[r, heads_of] for r in range(count)], axis=0)
        suf_log = jnp.concatenate([suf_log_ref[r, heads_of] for r in range(count)], axis=0)
        logs, scales = [], []
        top = suf_log
        for s in range(parts):
            tail = got_ref[s * kv_count + place, half // TILE_ROWS]
            mantissa, powers = tail[0:1], tail[1:2]
            log_power = (powers >> 16).astype(jnp.float32)
            peak_power = ((powers << 16) >> 16).astype(jnp.float32)
            log_line = mantissa.astype(jnp.float32) * jnp.exp2(log_power - LOG_BITS)
            logs.append(jnp.broadcast_to(column(log_line), (per_dest, width)))
            scales.append(column(jnp.exp2(peak_power - VALUE_BITS)))
            top = jnp.maximum(top, logs[-1])
        weight = jnp.exp(suf_log - top)
        acc = weight * suf_mixed
        total = weight
        for s in range(parts):
            words = jnp.concatenate(
                [got_ref[s * kv_count + place, j] for j in range(half // TILE_ROWS)], axis=0
            )
            coded = jnp.concatenate([words >> 16, (words << 16) >> 16], axis=0)
            weight = jnp.exp(logs[s] - top)
            acc = acc + (weight * scales[s]) * coded.astype(jnp.float32)
            total = total + weight
        acc = acc / total
        logged = top + jnp.log(total)
        for r in range(count):
            rows = slice(r * group, (r + 1) * group)
            out_ref[r, heads_of] = acc[rows]
            spot = lane[:group] == row[:group] + g * group
            lines[r] = lines[r] + jnp.sum(jnp.where(spot, logged[rows], 0.0), axis=0, keepdims=True)
    for r in range(count):
        log_ref[r : r + 1] = lines[r][:, :heads]


def join_partials(got, suf_mixed, suf_log, kv_count):
    count, heads, width = suf_mixed.shape
    return pl.pallas_call(
        functools.partial(join_kernel, kv_count=kv_count),
        in_specs=[IN_VMEM] * 3,
        out_specs=[IN_VMEM] * 2,
        out_shape=[
            jax.ShapeDtypeStruct((count, heads, width), jnp.float32),
            jax.ShapeDtypeStruct((count, heads), jnp.float32),
        ],
        compiler_params=pltpu.CompilerParams(vmem_limit_bytes=SMALL_VMEM),
        name="join_partials",
    )(got, suf_mixed, suf_log)


def exchange(pieces, first):
    seq, head, rep = lax.axis_size("seq"), lax.axis_size("head"), lax.axis_size("rep")
    order = [(first - s) % seq for s in range(seq)]
    groups = [
        [(s * head + h) * rep + r for s in order for h in reversed(range(head))]
        for r in range(rep)
    ]
    return lax.all_to_all(
        pieces,
        ("seq", "head", "rep"),
        split_axis=0,
        concat_axis=0,
        axis_index_groups=groups,
        tiled=True,
    )


def per_device(
    queries, prefix_keys, prefix_values, suffix_keys, suffix_values, suffix_lengths, slot_map
):
    count, heads, width = queries.shape
    kv_count = suffix_keys.shape[2]
    per_dest = count * heads // kv_count
    score_scale = 1.0 / math.sqrt(width)
    sent = layout_queries(queries, kv_count, lax.axis_size("seq"))
    seq = lax.axis_size("seq")
    out_first, back_first = (seq - 1) // 2, seq // 2
    got_q = exchange(sent, out_first)
    keys = prefix_keys[:, 0, :]
    values = prefix_values[:, 0, :]
    far_keys = lax.ppermute(keys, "rep", [(0, 1), (1, 0)])
    far_values = lax.ppermute(values, "rep", [(0, 1), (1, 0)])
    earlier = []
    for place in range(count):
        mixed, log, *brought = suffix_partials(
            place,
            queries,
            suffix_keys,
            suffix_values,
            suffix_lengths,
            slot_map,
            (keys, values) if place == 0 else (),
            earlier if place == count - 1 else (),
            score_scale,
        )
        earlier += [mixed, log]
        if brought:
            near_keys, near_values = brought
    partials = prefix_partials(
        got_q.reshape(-1, width),
        near_keys,
        near_values,
        far_keys,
        far_values,
        earlier[0],
        per_dest,
        (back_first - out_first) % seq,
        score_scale,
    )
    got = exchange(partials, back_first)
    return join_partials(got, mixed, log, kv_count)


def solution(mesh):
    by_request = P(("seq", "head", "rep"))
    by_block = P(("seq", "rep"), "head", None)
    placed = (by_request, by_block, by_block, by_request, by_request, by_request, by_request)
    return jax.shard_map(
        per_device,
        mesh=mesh,
        in_specs=placed,
        out_specs=(by_request, by_request),
        check_vma=False,
    )
```

```python
import functools
import math

import jax
import jax.numpy as jnp
from jax import lax
from jax.experimental import pallas as pl
from jax.experimental.pallas import tpu as pltpu
from jax.sharding import PartitionSpec as P

ROW_TILE = 128
STEP_ROWS = 512
SUF_COPIES = 4
AT_ONCE = 2
LANES = 128
PIECE = 256
TILE_ROWS = 2
VALUE_BITS = 15
LOG_BITS = 30
LOG2E = math.log2(math.e)
LEAST = 1e-25
PEAK_LEAST = 1e-33
NT = (((1,), (1,)), ((), ()))
PREFIX_VMEM = 14 * 1024 * 1024
SUFFIX_VMEM = 20 * 1024 * 1024
SMALL_VMEM = 8 * 1024 * 1024
IN_VMEM = pl.BlockSpec(memory_space=pltpu.VMEM)
IN_HBM = pl.BlockSpec(memory_space=pltpu.HBM)


def in_hbm(array):
    return pltpu.with_memory_space_constraint(array, pltpu.HBM)


def layout_kernel(q_hbm, sent_hbm, buf, in_sems, out_sems):
    groups = buf.shape[0]
    repeats = sent_hbm.shape[0] // groups
    reads = [
        pltpu.make_async_copy(q_hbm.at[:, g], buf.at[groups - 1 - g], in_sems.at[g])
        for g in range(groups)
    ]
    for read in reads:
        read.start()
    for read in reads:
        read.wait()
    writes = [
        pltpu.make_async_copy(buf, sent_hbm.at[pl.ds(s * groups, groups)], out_sems.at[s])
        for s in range(repeats)
    ]
    for write in writes:
        write.start()
    for write in writes:
        write.wait()


def layout_queries(queries, groups, repeats):
    count, heads, width = queries.shape
    group = heads // groups
    return pl.pallas_call(
        layout_kernel,
        in_specs=[IN_HBM],
        out_specs=IN_HBM,
        out_shape=pltpu.HBM((repeats * groups, count, group, width), queries.dtype),
        scratch_shapes=[
            pltpu.VMEM((groups, count, group, width), queries.dtype),
            pltpu.SemaphoreType.DMA((groups,)),
            pltpu.SemaphoreType.DMA((repeats,)),
        ],
        compiler_params=pltpu.CompilerParams(vmem_limit_bytes=SMALL_VMEM),
        name="layout_queries",
    )(in_hbm(queries.reshape(count, groups, group, width)))


def weigh(scores, weights, part, row_max, factor):
    sums = jnp.zeros((scores.shape[0], LANES), jnp.float32)
    for begin in range(part.start, part.stop, PIECE):
        piece = slice(begin, begin + PIECE)
        terms = jnp.exp2((scores[:, piece] - row_max) * factor)
        weights[:, piece] = terms.astype(jnp.bfloat16)
        for lane in range(0, PIECE, LANES):
            sums = sums + terms[:, lane : lane + LANES]
    return sums


def suffix_kernel(*refs, place, carried, kv_count, score_scale):
    slot_hbm, length_hbm, q_hbm, k_hbm, v_hbm = refs[:5]
    refs = refs[5:]
    count, heads, width = q_hbm.shape
    carried_refs, refs = refs[:carried], refs[carried:]
    last = place == count - 1
    earlier, refs = (refs[: 2 * place], refs[2 * place :]) if last else ((), refs)
    mixed_ref, log_ref = refs[:2]
    brought_refs, refs = refs[2 : 2 + carried], refs[2 + carried :]
    slot_ref, length_ref, q_ref, k_buf, v_buf, score_ref, weight_ref = refs[:7]
    peak_ref, sum_ref, acc_ref, sems, small_sems = refs[7:]
    rows = k_hbm.shape[1]
    copy_rows = rows // SUF_COPIES
    copies = []
    for which, (source, target) in enumerate(((k_hbm, k_buf), (v_hbm, v_buf))):
        for c in range(SUF_COPIES):
            part = pl.ds(c * copy_rows, copy_rows)
            copies.append(
                pltpu.make_async_copy(source.at[place, part], target.at[part], sems.at[which, c])
            )
    k_copies, v_copies = copies[:SUF_COPIES], copies[SUF_COPIES:]
    small = [
        pltpu.make_async_copy(source, target, small_sems.at[i])
        for i, (source, target) in enumerate(
            [(slot_hbm, slot_ref), (length_hbm, length_ref), (q_hbm, q_ref)]
            + list(zip(carried_refs, brought_refs))
        )
    ]
    small, carries = small[:3], small[3:]
    for copy in small + k_copies[:AT_ONCE] + carries:
        copy.start()
    for copy in small:
        copy.wait()

    def request_of(slot):
        found = jnp.int32(0)
        for r in range(1, count):
            found = jnp.where(lax.rem(slot_ref[r], count) == slot, r, found)
        return found

    request = request_of(place)
    limit = length_ref[request] * kv_count

    def live(c):
        return limit > c * copy_rows

    for c in range(AT_ONCE, SUF_COPIES):
        pl.when(live(c))(k_copies[c].start)
    query = q_ref[request]
    lane = lax.broadcasted_iota(jnp.int32, (heads, LANES), 1)
    group = lax.broadcasted_iota(jnp.int32, (heads, LANES), 0) // (heads // kv_count)
    lane = jnp.where((lane % kv_count) == group, lane, rows)
    peak_ref[...] = jnp.full((heads, LANES), -1e30, jnp.float32)
    for c in range(SUF_COPIES):
        if c < AT_ONCE:
            k_copies[c].wait()

        @pl.when(live(c))
        def _(c=c):
            if c >= AT_ONCE:
                k_copies[c].wait()
            v_copies[c].start()
            peak = peak_ref[...]
            for at in range(c * copy_rows, (c + 1) * copy_rows, 2 * PIECE):
                part = lax.dot_general(
                    query, k_buf[at : at + 2 * PIECE], NT, preferred_element_type=jnp.float32
                )
                for begin in range(0, 2 * PIECE, LANES):
                    tile = jnp.where(lane < limit - (at + begin), part[:, begin : begin + LANES], -1e30)
                    score_ref[:, at + begin : at + begin + LANES] = tile
                    peak = jnp.maximum(peak, tile)
            peak_ref[...] = peak

    row_max = jnp.max(peak_ref[...], axis=1, keepdims=True)
    sum_ref[...] = jnp.zeros((heads, LANES), jnp.float32)
    acc_ref[...] = jnp.zeros((heads, width), jnp.float32)
    for c in range(SUF_COPIES):

        @pl.when(live(c))
        def _(c=c):
            v_copies[c].wait()
            part = slice(c * copy_rows, (c + 1) * copy_rows)
            sum_ref[...] += weigh(score_ref, weight_ref, part, row_max, score_scale * LOG2E)
            acc_ref[...] += jnp.dot(
                weight_ref[:, part], v_buf[part], preferred_element_type=jnp.float32
            )

    sums, acc = sum_ref[...], acc_ref[...]
    total = jnp.sum(sums, axis=1, keepdims=True)
    mixed = acc / total
    log = jnp.broadcast_to(row_max * score_scale + jnp.log(total), (heads, width))
    for carry in carries:
        carry.wait()
    if not last:
        mixed_ref[...] = mixed
        log_ref[...] = log
        return
    mixed_ref[request] = mixed
    log_ref[request] = log
    for slot in range(place):
        mixed_ref[request_of(slot)] = earlier[2 * slot][...]
        log_ref[request_of(slot)] = earlier[2 * slot + 1][...]


def suffix_partials(
    place, queries, keys, values, lengths, slots, carried, earlier, score_scale
):
    count, heads, width = queries.shape
    kv_count = keys.shape[2]
    rows = keys.shape[1] * kv_count
    result = (count, heads, width) if place == count - 1 else (heads, width)
    operands = (
        slots,
        lengths,
        queries,
        keys.reshape(count, rows, width),
        values.reshape(count, rows, width),
        *carried,
    )
    return pl.pallas_call(
        functools.partial(
            suffix_kernel,
            place=place,
            carried=len(carried),
            kv_count=kv_count,
            score_scale=score_scale,
        ),
        in_specs=[IN_HBM] * len(operands) + [IN_VMEM] * len(earlier),
        out_specs=[IN_VMEM] * (2 + len(carried)),
        out_shape=[pltpu.VMEM(result, jnp.float32)] * 2
        + [pltpu.VMEM(array.shape, array.dtype) for array in carried],
        scratch_shapes=[
            pltpu.SMEM((count,), jnp.int32),
            pltpu.SMEM((count,), jnp.int32),
            pltpu.VMEM((count, heads, width), queries.dtype),
            pltpu.VMEM((rows, width), keys.dtype),
            pltpu.VMEM((rows, width), values.dtype),
            pltpu.VMEM((heads, rows), jnp.float32),
            pltpu.VMEM((heads, rows), jnp.bfloat16),
            pltpu.VMEM((heads, LANES), jnp.float32),
            pltpu.VMEM((heads, LANES), jnp.float32),
            pltpu.VMEM((heads, width), jnp.float32),
            pltpu.SemaphoreType.DMA((2, SUF_COPIES)),
            pltpu.SemaphoreType.DMA((3 + len(carried),)),
        ],
        compiler_params=pltpu.CompilerParams(vmem_limit_bytes=SUFFIX_VMEM),
        cost_estimate=pl.CostEstimate(
            flops=4 * heads * rows * width,
            bytes_accessed=4 * rows * width,
            transcendentals=heads * rows,
        ),
        name=f"suffix_attention_{place}",
    )(*map(in_hbm, operands), *earlier)


def exponent(size, least):
    return jnp.floor(jnp.log2(jnp.maximum(size, least))) + 1.0


def prefix_kernel(
    q_ref, k0_ref, v0_ref, k1_ref, v1_ref, _, out_hbm, out_ref, score_ref, weight_ref, sems, *, per_dest, turn, score_scale
):
    width = q_ref.shape[1]
    tiles = q_ref.shape[0] // ROW_TILE
    dests = ROW_TILE // per_dest
    keys, values = (k0_ref, k1_ref), (v0_ref, v1_ref)
    units = [(tile, block) for tile in range(tiles) for block in range(2)]
    places = out_hbm.shape[0] // dests
    first_place = turn + (0 if out_hbm.shape == out_ref.shape else pl.program_id(0) * tiles)
    copies = []
    lane = lax.broadcasted_iota(jnp.int32, (per_dest, width), 1)
    row = lax.broadcasted_iota(jnp.int32, (per_dest, width), 0)
    diagonal = lane == row

    length = k0_ref.shape[0]

    def score(unit, slot):
        tile, block = unit
        query = q_ref[tile * ROW_TILE : (tile + 1) * ROW_TILE]
        peak = None
        for at in range(0, length, PIECE):
            part = lax.dot_general(
                query, keys[block][at : at + PIECE], NT, preferred_element_type=jnp.float32
            )
            score_ref[slot, :, at : at + PIECE] = part
            for begin in range(0, PIECE, LANES):
                lanes = part[:, begin : begin + LANES]
                peak = lanes if peak is None else jnp.maximum(peak, lanes)
        return jnp.max(peak, axis=1, keepdims=True)

    held = []

    def finish(step, row_max, sums):
        tile, block = units[step]
        total = jnp.sum(sums, axis=1, keepdims=True)
        acc = jnp.dot(weight_ref[step % 2], values[block][...], preferred_element_type=jnp.float32)
        if block == 0:
            held.append((row_max, total, acc))
            return
        max0, total0, acc0 = held.pop()
        top = jnp.maximum(max0, row_max)
        weight0 = jnp.exp((max0 - top) * score_scale)
        weight1 = jnp.exp((row_max - top) * score_scale)
        joined = weight0 * total0 + weight1 * total
        mixed = (weight0 * acc0 + weight1 * acc) / joined
        logs = jnp.broadcast_to(top * score_scale + jnp.log(joined), (ROW_TILE, width))
        peak = jnp.max(jnp.abs(mixed), axis=1, keepdims=True)
        coded = jnp.round(mixed * jnp.exp2(VALUE_BITS - exponent(peak, PEAK_LEAST)))
        most = 2.0**VALUE_BITS - 1
        coded = jnp.clip(coded, -most, most).astype(jnp.int32)
        peaks = jnp.broadcast_to(peak, (ROW_TILE, width))
        half = per_dest // 2
        for k in range(dests):
            rows = slice(k * per_dest, (k + 1) * per_dest)
            dest = tile * dests + k
            high, low = coded[k * per_dest : k * per_dest + half], coded[k * per_dest + half : rows.stop]
            words = (high << 16) | (low & 0xFFFF)
            for j in range(half // TILE_ROWS):
                out_ref[dest, j] = words[j * TILE_ROWS : (j + 1) * TILE_ROWS]
            log_line = jnp.sum(jnp.where(diagonal, logs[rows], 0.0), axis=0, keepdims=True)
            peak_line = jnp.sum(jnp.where(diagonal, peaks[rows], 0.0), axis=0, keepdims=True)
            log_power = exponent(jnp.abs(log_line), LEAST)
            mantissa = jnp.round(log_line * jnp.exp2(LOG_BITS - log_power)).astype(jnp.int32)
            powers = log_power.astype(jnp.int32) << 16
            powers = powers | (exponent(peak_line, PEAK_LEAST).astype(jnp.int32) & 0xFFFF)
            out_ref[dest, half // TILE_ROWS] = jnp.concatenate([mantissa, powers], axis=0)
        ready = pl.ds(tile * dests, dests)
        copies.append(
            pltpu.make_async_copy(
                out_ref.at[ready],
                out_hbm.at[pl.ds(lax.rem(first_place + tile, places) * dests, dests)],
                sems.at[tile],
            )
        )
        copies[-1].start()
    later_max = score(units[0], 0)
    pending = None
    for step in range(len(units)):
        row_max, slot = later_max, step % 2
        if step + 1 < len(units):
            later_max = score(units[step + 1], (step + 1) % 2)
        if pending is not None:
            finish(*pending)
        sums = weigh(
            score_ref.at[slot], weight_ref.at[slot], slice(0, length), row_max, score_scale * LOG2E
        )
        pending = (step, row_max, sums)
    finish(*pending)
    for copy in copies:
        copy.wait()


def prefix_partials(
    rows_q, keys, values, far_keys, far_values, after, per_dest, turn, score_scale
):
    rows, width = rows_q.shape
    length = keys.shape[0]
    step_rows = min(STEP_ROWS, rows)
    dests = step_rows // per_dest
    out_piece = (per_dest // 2 // TILE_ROWS + 1, TILE_ROWS, width)
    blocked = {"in_specs": [IN_VMEM] * 5}
    if step_rows < rows:
        blocked["grid"] = (rows // step_rows,)
        blocked["in_specs"] = [pl.BlockSpec((step_rows, width), lambda i: (i, 0))]
        blocked["in_specs"] += [pl.BlockSpec((length, width), lambda i: (0, 0))] * 4
    blocked["in_specs"] += [pl.BlockSpec(memory_space=pl.ANY)]
    return pl.pallas_call(
        functools.partial(
            prefix_kernel, per_dest=per_dest, turn=turn, score_scale=score_scale
        ),
        **blocked,
        out_specs=IN_HBM,
        out_shape=pltpu.HBM((rows // per_dest, *out_piece), jnp.int32),
        scratch_shapes=[
            pltpu.VMEM((dests, *out_piece), jnp.int32),
            pltpu.VMEM((2, ROW_TILE, length), jnp.float32),
            pltpu.VMEM((2, ROW_TILE, length), jnp.bfloat16),
            pltpu.SemaphoreType.DMA((step_rows // ROW_TILE,)),
        ],
        compiler_params=pltpu.CompilerParams(vmem_limit_bytes=PREFIX_VMEM),
        cost_estimate=pl.CostEstimate(
            flops=8 * rows * length * width,
            bytes_accessed=8 * length * width + 6 * rows * width,
            transcendentals=2 * rows * length,
        ),
        name="prefix_attention",
    )(rows_q, keys, values, far_keys, far_values, after)


def join_kernel(got_ref, suf_ref, suf_log_ref, out_ref, log_ref, *, kv_count):
    count, heads, width = out_ref.shape
    group = heads // kv_count
    per_dest = count * group
    half = per_dest // 2
    parts = got_ref.shape[0] // kv_count
    lane = lax.broadcasted_iota(jnp.int32, (per_dest, width), 1)
    row = lax.broadcasted_iota(jnp.int32, (per_dest, width), 0)
    diagonal = lane == row

    def column(line):
        return jnp.sum(jnp.where(diagonal, line, 0.0), axis=1, keepdims=True)

    lines = [jnp.zeros((1, width), jnp.float32) for _ in range(count)]
    for place in range(kv_count):
        g = kv_count - 1 - place
        heads_of = slice(g * group, (g + 1) * group)
        suf_mixed = jnp.concatenate([suf_ref[r, heads_of] for r in range(count)], axis=0)
        suf_log = jnp.concatenate([suf_log_ref[r, heads_of] for r in range(count)], axis=0)
        logs, scales = [], []
        top = suf_log
        for s in range(parts):
            tail = got_ref[s * kv_count + place, half // TILE_ROWS]
            mantissa, powers = tail[0:1], tail[1:2]
            log_power = (powers >> 16).astype(jnp.float32)
            peak_power = ((powers << 16) >> 16).astype(jnp.float32)
            log_line = mantissa.astype(jnp.float32) * jnp.exp2(log_power - LOG_BITS)
            logs.append(jnp.broadcast_to(column(log_line), (per_dest, width)))
            scales.append(column(jnp.exp2(peak_power - VALUE_BITS)))
            top = jnp.maximum(top, logs[-1])
        weight = jnp.exp(suf_log - top)
        acc = weight * suf_mixed
        total = weight
        for s in range(parts):
            words = jnp.concatenate(
                [got_ref[s * kv_count + place, j] for j in range(half // TILE_ROWS)], axis=0
            )
            coded = jnp.concatenate([words >> 16, (words << 16) >> 16], axis=0)
            weight = jnp.exp(logs[s] - top)
            acc = acc + (weight * scales[s]) * coded.astype(jnp.float32)
            total = total + weight
        acc = acc / total
        logged = top + jnp.log(total)
        for r in range(count):
            rows = slice(r * group, (r + 1) * group)
            out_ref[r, heads_of] = acc[rows]
            spot = lane[:group] == row[:group] + g * group
            lines[r] = lines[r] + jnp.sum(jnp.where(spot, logged[rows], 0.0), axis=0, keepdims=True)
    for r in range(count):
        log_ref[r : r + 1] = lines[r][:, :heads]


def join_partials(got, suf_mixed, suf_log, kv_count):
    count, heads, width = suf_mixed.shape
    return pl.pallas_call(
        functools.partial(join_kernel, kv_count=kv_count),
        in_specs=[IN_VMEM] * 3,
        out_specs=[IN_VMEM] * 2,
        out_shape=[
            jax.ShapeDtypeStruct((count, heads, width), jnp.float32),
            jax.ShapeDtypeStruct((count, heads), jnp.float32),
        ],
        compiler_params=pltpu.CompilerParams(vmem_limit_bytes=SMALL_VMEM),
        name="join_partials",
    )(got, suf_mixed, suf_log)


def exchange(pieces, first):
    seq, head, rep = lax.axis_size("seq"), lax.axis_size("head"), lax.axis_size("rep")
    order = [(first - s) % seq for s in range(seq)]
    groups = [
        [(s * head + h) * rep + r for s in order for h in reversed(range(head))]
        for r in range(rep)
    ]
    return lax.all_to_all(
        pieces,
        ("seq", "head", "rep"),
        split_axis=0,
        concat_axis=0,
        axis_index_groups=groups,
        tiled=True,
    )


def per_device(
    queries, prefix_keys, prefix_values, suffix_keys, suffix_values, suffix_lengths, slot_map
):
    count, heads, width = queries.shape
    kv_count = suffix_keys.shape[2]
    per_dest = count * heads // kv_count
    score_scale = 1.0 / math.sqrt(width)
    sent = layout_queries(queries, kv_count, lax.axis_size("seq"))
    seq = lax.axis_size("seq")
    out_first, back_first = (seq - 1) // 2, seq // 2
    got_q = exchange(sent, out_first)
    keys = prefix_keys[:, 0, :]
    values = prefix_values[:, 0, :]
    far_keys = lax.ppermute(keys, "rep", [(0, 1), (1, 0)])
    far_values = lax.ppermute(values, "rep", [(0, 1), (1, 0)])
    earlier = []
    for place in range(count):
        mixed, log, *brought = suffix_partials(
            place,
            queries,
            suffix_keys,
            suffix_values,
            suffix_lengths,
            slot_map,
            (keys, values) if place == 0 else (),
            earlier if place == count - 1 else (),
            score_scale,
        )
        earlier += [mixed, log]
        if brought:
            near_keys, near_values = brought
    partials = prefix_partials(
        got_q.reshape(-1, width),
        near_keys,
        near_values,
        far_keys,
        far_values,
        earlier[0],
        per_dest,
        (back_first - out_first) % seq,
        score_scale,
    )
    got = exchange(partials, back_first)
    return join_partials(got, mixed, log, kv_count)


def solution(mesh):
    by_request = P(("seq", "head", "rep"))
    by_block = P(("seq", "rep"), "head", None)
    placed = (by_request, by_block, by_block, by_request, by_request, by_request, by_request)
    return jax.shard_map(
        per_device,
        mesh=mesh,
        in_specs=placed,
        out_specs=(by_request, by_request),
        check_vma=False,
    )
```

```python
import functools
import math

import jax
import jax.numpy as jnp
from jax import lax
from jax.experimental import pallas as pl
from jax.experimental.pallas import tpu as pltpu
from jax.sharding import PartitionSpec as P

ROW_TILE = 128
STEP_ROWS = 512
SUF_COPIES = 4
AT_ONCE = 2
LANES = 128
PIECE = 256
TILE_ROWS = 2
VALUE_BITS = 15
LOG_BITS = 30
LOG2E = math.log2(math.e)
LEAST = 1e-25
PEAK_LEAST = 1e-33
NT = (((1,), (1,)), ((), ()))
PREFIX_VMEM = 20 * 1024 * 1024
SUFFIX_VMEM = 20 * 1024 * 1024
SMALL_VMEM = 8 * 1024 * 1024
IN_VMEM = pl.BlockSpec(memory_space=pltpu.VMEM)
IN_HBM = pl.BlockSpec(memory_space=pltpu.HBM)


def in_hbm(array):
    return pltpu.with_memory_space_constraint(array, pltpu.HBM)


def layout_kernel(q_hbm, sent_hbm, buf, in_sems, out_sems):
    groups = buf.shape[0]
    repeats = sent_hbm.shape[0] // groups
    reads = [
        pltpu.make_async_copy(q_hbm.at[:, g], buf.at[groups - 1 - g], in_sems.at[g])
        for g in range(groups)
    ]
    for read in reads:
        read.start()
    for read in reads:
        read.wait()
    writes = [
        pltpu.make_async_copy(buf, sent_hbm.at[pl.ds(s * groups, groups)], out_sems.at[s])
        for s in range(repeats)
    ]
    for write in writes:
        write.start()
    for write in writes:
        write.wait()


def layout_queries(queries, groups, repeats):
    count, heads, width = queries.shape
    group = heads // groups
    return pl.pallas_call(
        layout_kernel,
        in_specs=[IN_HBM],
        out_specs=IN_HBM,
        out_shape=pltpu.HBM((repeats * groups, count, group, width), queries.dtype),
        scratch_shapes=[
            pltpu.VMEM((groups, count, group, width), queries.dtype),
            pltpu.SemaphoreType.DMA((groups,)),
            pltpu.SemaphoreType.DMA((repeats,)),
        ],
        compiler_params=pltpu.CompilerParams(vmem_limit_bytes=SMALL_VMEM),
        name="layout_queries",
    )(in_hbm(queries.reshape(count, groups, group, width)))


def weigh(scores, weights, part, row_max, factor):
    sums = jnp.zeros((scores.shape[0], LANES), jnp.float32)
    for begin in range(part.start, part.stop, PIECE):
        piece = slice(begin, begin + PIECE)
        terms = jnp.exp2((scores[:, piece] - row_max) * factor)
        weights[:, piece] = terms.astype(jnp.bfloat16)
        for lane in range(0, PIECE, LANES):
            sums = sums + terms[:, lane : lane + LANES]
    return sums


def suffix_kernel(*refs, place, carried, kv_count, score_scale):
    slot_hbm, length_hbm, q_hbm, k_hbm, v_hbm = refs[:5]
    refs = refs[5:]
    count, heads, width = q_hbm.shape
    carried_refs, refs = refs[:carried], refs[carried:]
    last = place == count - 1
    earlier, refs = (refs[: 2 * place], refs[2 * place :]) if last else ((), refs)
    mixed_ref, log_ref = refs[:2]
    brought_refs, refs = refs[2 : 2 + carried], refs[2 + carried :]
    slot_ref, length_ref, q_ref, k_buf, v_buf, score_ref, weight_ref = refs[:7]
    peak_ref, sum_ref, acc_ref, sems, small_sems = refs[7:]
    rows = k_hbm.shape[1]
    copy_rows = rows // SUF_COPIES
    copies = []
    for which, (source, target) in enumerate(((k_hbm, k_buf), (v_hbm, v_buf))):
        for c in range(SUF_COPIES):
            part = pl.ds(c * copy_rows, copy_rows)
            copies.append(
                pltpu.make_async_copy(source.at[place, part], target.at[part], sems.at[which, c])
            )
    k_copies, v_copies = copies[:SUF_COPIES], copies[SUF_COPIES:]
    small = [
        pltpu.make_async_copy(source, target, small_sems.at[i])
        for i, (source, target) in enumerate(
            [(slot_hbm, slot_ref), (length_hbm, length_ref), (q_hbm, q_ref)]
            + list(zip(carried_refs, brought_refs))
        )
    ]
    small, carries = small[:3], small[3:]
    for copy in small + k_copies[:AT_ONCE] + carries:
        copy.start()
    for copy in small:
        copy.wait()

    def request_of(slot):
        found = jnp.int32(0)
        for r in range(1, count):
            found = jnp.where(lax.rem(slot_ref[r], count) == slot, r, found)
        return found

    request = request_of(place)
    limit = length_ref[request] * kv_count

    def live(c):
        return limit > c * copy_rows

    for c in range(AT_ONCE, SUF_COPIES):
        pl.when(live(c))(k_copies[c].start)
    query = q_ref[request]
    lane = lax.broadcasted_iota(jnp.int32, (heads, LANES), 1)
    group = lax.broadcasted_iota(jnp.int32, (heads, LANES), 0) // (heads // kv_count)
    lane = jnp.where((lane % kv_count) == group, lane, rows)
    peak_ref[...] = jnp.full((heads, LANES), -1e30, jnp.float32)
    for c in range(SUF_COPIES):
        if c < AT_ONCE:
            k_copies[c].wait()

        @pl.when(live(c))
        def _(c=c):
            if c >= AT_ONCE:
                k_copies[c].wait()
            v_copies[c].start()
            peak = peak_ref[...]
            for at in range(c * copy_rows, (c + 1) * copy_rows, 2 * PIECE):
                part = lax.dot_general(
                    query, k_buf[at : at + 2 * PIECE], NT, preferred_element_type=jnp.float32
                )
                for begin in range(0, 2 * PIECE, LANES):
                    tile = jnp.where(lane < limit - (at + begin), part[:, begin : begin + LANES], -1e30)
                    score_ref[:, at + begin : at + begin + LANES] = tile
                    peak = jnp.maximum(peak, tile)
            peak_ref[...] = peak

    row_max = jnp.max(peak_ref[...], axis=1, keepdims=True)
    sum_ref[...] = jnp.zeros((heads, LANES), jnp.float32)
    acc_ref[...] = jnp.zeros((heads, width), jnp.float32)
    for c in range(SUF_COPIES):

        @pl.when(live(c))
        def _(c=c):
            v_copies[c].wait()
            part = slice(c * copy_rows, (c + 1) * copy_rows)
            sum_ref[...] += weigh(score_ref, weight_ref, part, row_max, score_scale * LOG2E)
            acc_ref[...] += jnp.dot(
                weight_ref[:, part], v_buf[part], preferred_element_type=jnp.float32
            )

    sums, acc = sum_ref[...], acc_ref[...]
    total = jnp.sum(sums, axis=1, keepdims=True)
    mixed = acc / total
    log = jnp.broadcast_to(row_max * score_scale + jnp.log(total), (heads, width))
    for carry in carries:
        carry.wait()
    if not last:
        mixed_ref[...] = mixed
        log_ref[...] = log
        return
    mixed_ref[request] = mixed
    log_ref[request] = log
    for slot in range(place):
        mixed_ref[request_of(slot)] = earlier[2 * slot][...]
        log_ref[request_of(slot)] = earlier[2 * slot + 1][...]


def suffix_partials(
    place, queries, keys, values, lengths, slots, carried, earlier, score_scale
):
    count, heads, width = queries.shape
    kv_count = keys.shape[2]
    rows = keys.shape[1] * kv_count
    result = (count, heads, width) if place == count - 1 else (heads, width)
    operands = (
        slots,
        lengths,
        queries,
        keys.reshape(count, rows, width),
        values.reshape(count, rows, width),
        *carried,
    )
    return pl.pallas_call(
        functools.partial(
            suffix_kernel,
            place=place,
            carried=len(carried),
            kv_count=kv_count,
            score_scale=score_scale,
        ),
        in_specs=[IN_HBM] * len(operands) + [IN_VMEM] * len(earlier),
        out_specs=[IN_VMEM] * (2 + len(carried)),
        out_shape=[pltpu.VMEM(result, jnp.float32)] * 2
        + [pltpu.VMEM(array.shape, array.dtype) for array in carried],
        scratch_shapes=[
            pltpu.SMEM((count,), jnp.int32),
            pltpu.SMEM((count,), jnp.int32),
            pltpu.VMEM((count, heads, width), queries.dtype),
            pltpu.VMEM((rows, width), keys.dtype),
            pltpu.VMEM((rows, width), values.dtype),
            pltpu.VMEM((heads, rows), jnp.float32),
            pltpu.VMEM((heads, rows), jnp.bfloat16),
            pltpu.VMEM((heads, LANES), jnp.float32),
            pltpu.VMEM((heads, LANES), jnp.float32),
            pltpu.VMEM((heads, width), jnp.float32),
            pltpu.SemaphoreType.DMA((2, SUF_COPIES)),
            pltpu.SemaphoreType.DMA((3 + len(carried),)),
        ],
        compiler_params=pltpu.CompilerParams(vmem_limit_bytes=SUFFIX_VMEM),
        cost_estimate=pl.CostEstimate(
            flops=4 * heads * rows * width,
            bytes_accessed=4 * rows * width,
            transcendentals=heads * rows,
        ),
        name=f"suffix_attention_{place}",
    )(*map(in_hbm, operands), *earlier)


def exponent(size, least):
    return jnp.floor(jnp.log2(jnp.maximum(size, least))) + 1.0


def prefix_kernel(
    q_ref, k0_ref, v0_ref, k1_ref, v1_ref, _, out_hbm, out_ref, score_ref, weight_ref, sems, *, per_dest, turn, score_scale
):
    width = q_ref.shape[1]
    tiles = q_ref.shape[0] // ROW_TILE
    dests = ROW_TILE // per_dest
    keys, values = (k0_ref, k1_ref), (v0_ref, v1_ref)
    inner = tiles - 2
    spans = [(0, 1), (1, inner), (tiles - 1, 1)] if inner == 2 else [(t, 1) for t in range(tiles)]
    units = [(first, wide, block) for first, wide in spans for block in range(2)]
    places = out_hbm.shape[0] // dests
    first_place = turn + (0 if out_hbm.shape == out_ref.shape else pl.program_id(0) * tiles)
    copies = []
    lane = lax.broadcasted_iota(jnp.int32, (per_dest, width), 1)
    row = lax.broadcasted_iota(jnp.int32, (per_dest, width), 0)
    diagonal = lane == row

    length = k0_ref.shape[0]

    def score(unit, slot):
        first, wide, block = unit
        query = q_ref[first * ROW_TILE : (first + wide) * ROW_TILE]
        peak = None
        for at in range(0, length, PIECE):
            part = lax.dot_general(
                query, keys[block][at : at + PIECE], NT, preferred_element_type=jnp.float32
            )
            score_ref[slot, : wide * ROW_TILE, at : at + PIECE] = part
            for begin in range(0, PIECE, LANES):
                lanes = part[:, begin : begin + LANES]
                peak = lanes if peak is None else jnp.maximum(peak, lanes)
        return jnp.max(peak, axis=1, keepdims=True)

    held = []

    def finish(step, row_max, sums):
        first, wide, block = units[step]
        row_count = wide * ROW_TILE
        total = jnp.sum(sums, axis=1, keepdims=True)
        acc = jnp.dot(
            weight_ref[step % 2, :row_count], values[block][...], preferred_element_type=jnp.float32
        )
        if block == 0:
            held.append((row_max, total, acc))
            return
        max0, total0, acc0 = held.pop()
        top = jnp.maximum(max0, row_max)
        weight0 = jnp.exp((max0 - top) * score_scale)
        weight1 = jnp.exp((row_max - top) * score_scale)
        joined = weight0 * total0 + weight1 * total
        mixed = (weight0 * acc0 + weight1 * acc) / joined
        logs = jnp.broadcast_to(top * score_scale + jnp.log(joined), (row_count, width))
        peak = jnp.max(jnp.abs(mixed), axis=1, keepdims=True)
        coded = jnp.round(mixed * jnp.exp2(VALUE_BITS - exponent(peak, PEAK_LEAST)))
        most = 2.0**VALUE_BITS - 1
        coded = jnp.clip(coded, -most, most).astype(jnp.int32)
        peaks = jnp.broadcast_to(peak, (row_count, width))
        half = per_dest // 2
        for k in range(wide * dests):
            rows = slice(k * per_dest, (k + 1) * per_dest)
            dest = first * dests + k
            high, low = coded[k * per_dest : k * per_dest + half], coded[k * per_dest + half : rows.stop]
            words = (high << 16) | (low & 0xFFFF)
            for j in range(half // TILE_ROWS):
                out_ref[dest, j] = words[j * TILE_ROWS : (j + 1) * TILE_ROWS]
            log_line = jnp.sum(jnp.where(diagonal, logs[rows], 0.0), axis=0, keepdims=True)
            peak_line = jnp.sum(jnp.where(diagonal, peaks[rows], 0.0), axis=0, keepdims=True)
            log_power = exponent(jnp.abs(log_line), LEAST)
            mantissa = jnp.round(log_line * jnp.exp2(LOG_BITS - log_power)).astype(jnp.int32)
            powers = log_power.astype(jnp.int32) << 16
            powers = powers | (exponent(peak_line, PEAK_LEAST).astype(jnp.int32) & 0xFFFF)
            out_ref[dest, half // TILE_ROWS] = jnp.concatenate([mantissa, powers], axis=0)
        for tile in range(first, first + wide):
            copies.append(
                pltpu.make_async_copy(
                    out_ref.at[pl.ds(tile * dests, dests)],
                    out_hbm.at[pl.ds(lax.rem(first_place + tile, places) * dests, dests)],
                    sems.at[tile],
                )
            )
            copies[-1].start()

    later_max = score(units[0], 0)
    pending = None
    for step in range(len(units)):
        row_max, slot = later_max, step % 2
        if step + 1 < len(units):
            later_max = score(units[step + 1], (step + 1) % 2)
        if pending is not None:
            finish(*pending)
        sums = weigh(
            score_ref.at[slot, pl.ds(0, row_max.shape[0])],
            weight_ref.at[slot, pl.ds(0, row_max.shape[0])],
            slice(0, length),
            row_max,
            score_scale * LOG2E,
        )
        pending = (step, row_max, sums)
    finish(*pending)
    for copy in copies:
        copy.wait()


def prefix_partials(
    rows_q, keys, values, far_keys, far_values, after, per_dest, turn, score_scale
):
    rows, width = rows_q.shape
    length = keys.shape[0]
    step_rows = min(STEP_ROWS, rows)
    dests = step_rows // per_dest
    out_piece = (per_dest // 2 // TILE_ROWS + 1, TILE_ROWS, width)
    blocked = {"in_specs": [IN_VMEM] * 5}
    if step_rows < rows:
        blocked["grid"] = (rows // step_rows,)
        blocked["in_specs"] = [pl.BlockSpec((step_rows, width), lambda i: (i, 0))]
        blocked["in_specs"] += [pl.BlockSpec((length, width), lambda i: (0, 0))] * 4
    blocked["in_specs"] += [pl.BlockSpec(memory_space=pl.ANY)]
    return pl.pallas_call(
        functools.partial(
            prefix_kernel, per_dest=per_dest, turn=turn, score_scale=score_scale
        ),
        **blocked,
        out_specs=IN_HBM,
        out_shape=pltpu.HBM((rows // per_dest, *out_piece), jnp.int32),
        scratch_shapes=[
            pltpu.VMEM((dests, *out_piece), jnp.int32),
            pltpu.VMEM((2, 2 * ROW_TILE, length), jnp.float32),
            pltpu.VMEM((2, 2 * ROW_TILE, length), jnp.bfloat16),
            pltpu.SemaphoreType.DMA((step_rows // ROW_TILE,)),
        ],
        compiler_params=pltpu.CompilerParams(vmem_limit_bytes=PREFIX_VMEM),
        cost_estimate=pl.CostEstimate(
            flops=8 * rows * length * width,
            bytes_accessed=8 * length * width + 6 * rows * width,
            transcendentals=2 * rows * length,
        ),
        name="prefix_attention",
    )(rows_q, keys, values, far_keys, far_values, after)


def join_kernel(got_ref, suf_ref, suf_log_ref, out_ref, log_ref, *, kv_count):
    count, heads, width = out_ref.shape
    group = heads // kv_count
    per_dest = count * group
    half = per_dest // 2
    parts = got_ref.shape[0] // kv_count
    lane = lax.broadcasted_iota(jnp.int32, (per_dest, width), 1)
    row = lax.broadcasted_iota(jnp.int32, (per_dest, width), 0)
    diagonal = lane == row

    def column(line):
        return jnp.sum(jnp.where(diagonal, line, 0.0), axis=1, keepdims=True)

    lines = [jnp.zeros((1, width), jnp.float32) for _ in range(count)]
    for place in range(kv_count):
        g = kv_count - 1 - place
        heads_of = slice(g * group, (g + 1) * group)
        suf_mixed = jnp.concatenate([suf_ref[r, heads_of] for r in range(count)], axis=0)
        suf_log = jnp.concatenate([suf_log_ref[r, heads_of] for r in range(count)], axis=0)
        logs, scales = [], []
        top = suf_log
        for s in range(parts):
            tail = got_ref[s * kv_count + place, half // TILE_ROWS]
            mantissa, powers = tail[0:1], tail[1:2]
            log_power = (powers >> 16).astype(jnp.float32)
            peak_power = ((powers << 16) >> 16).astype(jnp.float32)
            log_line = mantissa.astype(jnp.float32) * jnp.exp2(log_power - LOG_BITS)
            logs.append(jnp.broadcast_to(column(log_line), (per_dest, width)))
            scales.append(column(jnp.exp2(peak_power - VALUE_BITS)))
            top = jnp.maximum(top, logs[-1])
        weight = jnp.exp(suf_log - top)
        acc = weight * suf_mixed
        total = weight
        for s in range(parts):
            words = jnp.concatenate(
                [got_ref[s * kv_count + place, j] for j in range(half // TILE_ROWS)], axis=0
            )
            coded = jnp.concatenate([words >> 16, (words << 16) >> 16], axis=0)
            weight = jnp.exp(logs[s] - top)
            acc = acc + (weight * scales[s]) * coded.astype(jnp.float32)
            total = total + weight
        acc = acc / total
        logged = top + jnp.log(total)
        for r in range(count):
            rows = slice(r * group, (r + 1) * group)
            out_ref[r, heads_of] = acc[rows]
            spot = lane[:group] == row[:group] + g * group
            lines[r] = lines[r] + jnp.sum(jnp.where(spot, logged[rows], 0.0), axis=0, keepdims=True)
    for r in range(count):
        log_ref[r : r + 1] = lines[r][:, :heads]


def join_partials(got, suf_mixed, suf_log, kv_count):
    count, heads, width = suf_mixed.shape
    return pl.pallas_call(
        functools.partial(join_kernel, kv_count=kv_count),
        in_specs=[IN_VMEM] * 3,
        out_specs=[IN_VMEM] * 2,
        out_shape=[
            jax.ShapeDtypeStruct((count, heads, width), jnp.float32),
            jax.ShapeDtypeStruct((count, heads), jnp.float32),
        ],
        compiler_params=pltpu.CompilerParams(vmem_limit_bytes=SMALL_VMEM),
        name="join_partials",
    )(got, suf_mixed, suf_log)


def exchange(pieces, first):
    seq, head, rep = lax.axis_size("seq"), lax.axis_size("head"), lax.axis_size("rep")
    order = [(first - s) % seq for s in range(seq)]
    groups = [
        [(s * head + h) * rep + r for s in order for h in reversed(range(head))]
        for r in range(rep)
    ]
    return lax.all_to_all(
        pieces,
        ("seq", "head", "rep"),
        split_axis=0,
        concat_axis=0,
        axis_index_groups=groups,
        tiled=True,
    )


def per_device(
    queries, prefix_keys, prefix_values, suffix_keys, suffix_values, suffix_lengths, slot_map
):
    count, heads, width = queries.shape
    kv_count = suffix_keys.shape[2]
    per_dest = count * heads // kv_count
    score_scale = 1.0 / math.sqrt(width)
    sent = layout_queries(queries, kv_count, lax.axis_size("seq"))
    seq = lax.axis_size("seq")
    out_first, back_first = (seq - 1) // 2, seq // 2
    got_q = exchange(sent, out_first)
    keys = prefix_keys[:, 0, :]
    values = prefix_values[:, 0, :]
    far_keys = lax.ppermute(keys, "rep", [(0, 1), (1, 0)])
    far_values = lax.ppermute(values, "rep", [(0, 1), (1, 0)])
    earlier = []
    for place in range(count):
        mixed, log, *brought = suffix_partials(
            place,
            queries,
            suffix_keys,
            suffix_values,
            suffix_lengths,
            slot_map,
            (keys, values) if place == 0 else (),
            earlier if place == count - 1 else (),
            score_scale,
        )
        earlier += [mixed, log]
        if brought:
            near_keys, near_values = brought
    partials = prefix_partials(
        got_q.reshape(-1, width),
        near_keys,
        near_values,
        far_keys,
        far_values,
        earlier[0],
        per_dest,
        (back_first - out_first) % seq,
        score_scale,
    )
    got = exchange(partials, back_first)
    return join_partials(got, mixed, log, kv_count)


def solution(mesh):
    by_request = P(("seq", "head", "rep"))
    by_block = P(("seq", "rep"), "head", None)
    placed = (by_request, by_block, by_block, by_request, by_request, by_request, by_request)
    return jax.shard_map(
        per_device,
        mesh=mesh,
        in_specs=placed,
        out_specs=(by_request, by_request),
        check_vma=False,
    )
```

```python
import functools
import math

import jax
import jax.numpy as jnp
from jax import lax
from jax.experimental import pallas as pl
from jax.experimental.pallas import tpu as pltpu
from jax.sharding import PartitionSpec as P

ROW_TILE = 128
STEP_ROWS = 512
SUF_COPIES = 4
AT_ONCE = 4
LANES = 128
PIECE = 256
TILE_ROWS = 2
VALUE_BITS = 15
LOG_BITS = 30
LOG2E = math.log2(math.e)
LEAST = 1e-25
PEAK_LEAST = 1e-33
NT = (((1,), (1,)), ((), ()))
PREFIX_VMEM = 14 * 1024 * 1024
SUFFIX_VMEM = 20 * 1024 * 1024
SMALL_VMEM = 8 * 1024 * 1024
IN_VMEM = pl.BlockSpec(memory_space=pltpu.VMEM)
IN_HBM = pl.BlockSpec(memory_space=pltpu.HBM)


def in_hbm(array):
    return pltpu.with_memory_space_constraint(array, pltpu.HBM)


def layout_kernel(q_hbm, sent_hbm, buf, in_sems, out_sems):
    groups = buf.shape[0]
    repeats = sent_hbm.shape[0] // groups
    reads = [
        pltpu.make_async_copy(q_hbm.at[:, g], buf.at[groups - 1 - g], in_sems.at[g])
        for g in range(groups)
    ]
    for read in reads:
        read.start()
    for read in reads:
        read.wait()
    writes = [
        pltpu.make_async_copy(buf, sent_hbm.at[pl.ds(s * groups, groups)], out_sems.at[s])
        for s in range(repeats)
    ]
    for write in writes:
        write.start()
    for write in writes:
        write.wait()


def layout_queries(queries, groups, repeats):
    count, heads, width = queries.shape
    group = heads // groups
    return pl.pallas_call(
        layout_kernel,
        in_specs=[IN_HBM],
        out_specs=IN_HBM,
        out_shape=pltpu.HBM((repeats * groups, count, group, width), queries.dtype),
        scratch_shapes=[
            pltpu.VMEM((groups, count, group, width), queries.dtype),
            pltpu.SemaphoreType.DMA((groups,)),
            pltpu.SemaphoreType.DMA((repeats,)),
        ],
        compiler_params=pltpu.CompilerParams(vmem_limit_bytes=SMALL_VMEM),
        name="layout_queries",
    )(in_hbm(queries.reshape(count, groups, group, width)))


def weigh(scores, weights, part, row_max, factor):
    sums = jnp.zeros((scores.shape[0], LANES), jnp.float32)
    for begin in range(part.start, part.stop, PIECE):
        piece = slice(begin, begin + PIECE)
        terms = jnp.exp2((scores[:, piece] - row_max) * factor)
        weights[:, piece] = terms.astype(jnp.bfloat16)
        for lane in range(0, PIECE, LANES):
            sums = sums + terms[:, lane : lane + LANES]
    return sums


def suffix_kernel(*refs, place, carried, kv_count, score_scale):
    slot_hbm, length_hbm, q_hbm, k_hbm, v_hbm = refs[:5]
    refs = refs[5:]
    count, heads, width = q_hbm.shape
    carried_refs, refs = refs[:carried], refs[carried:]
    last = place == count - 1
    earlier, refs = (refs[: 2 * place], refs[2 * place :]) if last else ((), refs)
    mixed_ref, log_ref = refs[:2]
    brought_refs, refs = refs[2 : 2 + carried], refs[2 + carried :]
    slot_ref, length_ref, q_ref, k_buf, v_buf, score_ref, weight_ref = refs[:7]
    peak_ref, sum_ref, acc_ref, sems, small_sems = refs[7:]
    rows = k_hbm.shape[1]
    copy_rows = rows // SUF_COPIES
    copies = []
    for which, (source, target) in enumerate(((k_hbm, k_buf), (v_hbm, v_buf))):
        for c in range(SUF_COPIES):
            part = pl.ds(c * copy_rows, copy_rows)
            copies.append(
                pltpu.make_async_copy(source.at[place, part], target.at[part], sems.at[which, c])
            )
    k_copies, v_copies = copies[:SUF_COPIES], copies[SUF_COPIES:]
    small = [
        pltpu.make_async_copy(source, target, small_sems.at[i])
        for i, (source, target) in enumerate(
            [(slot_hbm, slot_ref), (length_hbm, length_ref), (q_hbm, q_ref)]
            + list(zip(carried_refs, brought_refs))
        )
    ]
    small, carries = small[:3], small[3:]
    for copy in small + k_copies[:AT_ONCE] + v_copies[:1] + carries:
        copy.start()
    for copy in small:
        copy.wait()

    def request_of(slot):
        found = jnp.int32(0)
        for r in range(1, count):
            found = jnp.where(lax.rem(slot_ref[r], count) == slot, r, found)
        return found

    request = request_of(place)
    limit = length_ref[request] * kv_count

    def live(c):
        return limit > c * copy_rows

    for c in range(AT_ONCE, SUF_COPIES):
        pl.when(live(c))(k_copies[c].start)
    query = q_ref[request]
    lane = lax.broadcasted_iota(jnp.int32, (heads, LANES), 1)
    group = lax.broadcasted_iota(jnp.int32, (heads, LANES), 0) // (heads // kv_count)
    lane = jnp.where((lane % kv_count) == group, lane, rows)
    peak_ref[...] = jnp.full((heads, LANES), -1e30, jnp.float32)
    for c in range(SUF_COPIES):
        if c < AT_ONCE:
            k_copies[c].wait()

        @pl.when(live(c))
        def _(c=c):
            if c >= AT_ONCE:
                k_copies[c].wait()
            if c > 0:
                v_copies[c].start()
            peak = peak_ref[...]
            for at in range(c * copy_rows, (c + 1) * copy_rows, 2 * PIECE):
                part = lax.dot_general(
                    query, k_buf[at : at + 2 * PIECE], NT, preferred_element_type=jnp.float32
                )
                for begin in range(0, 2 * PIECE, LANES):
                    tile = jnp.where(lane < limit - (at + begin), part[:, begin : begin + LANES], -1e30)
                    score_ref[:, at + begin : at + begin + LANES] = tile
                    peak = jnp.maximum(peak, tile)
            peak_ref[...] = peak

    row_max = jnp.max(peak_ref[...], axis=1, keepdims=True)
    sum_ref[...] = jnp.zeros((heads, LANES), jnp.float32)
    acc_ref[...] = jnp.zeros((heads, width), jnp.float32)
    for c in range(SUF_COPIES):

        @pl.when(live(c))
        def _(c=c):
            v_copies[c].wait()
            part = slice(c * copy_rows, (c + 1) * copy_rows)
            sum_ref[...] += weigh(score_ref, weight_ref, part, row_max, score_scale * LOG2E)
            acc_ref[...] += jnp.dot(
                weight_ref[:, part], v_buf[part], preferred_element_type=jnp.float32
            )

    sums, acc = sum_ref[...], acc_ref[...]
    total = jnp.sum(sums, axis=1, keepdims=True)
    mixed = acc / total
    log = jnp.broadcast_to(row_max * score_scale + jnp.log(total), (heads, width))
    for carry in carries:
        carry.wait()
    if not last:
        mixed_ref[...] = mixed
        log_ref[...] = log
        return
    mixed_ref[request] = mixed
    log_ref[request] = log
    for slot in range(place):
        mixed_ref[request_of(slot)] = earlier[2 * slot][...]
        log_ref[request_of(slot)] = earlier[2 * slot + 1][...]


def suffix_partials(
    place, queries, keys, values, lengths, slots, carried, earlier, score_scale
):
    count, heads, width = queries.shape
    kv_count = keys.shape[2]
    rows = keys.shape[1] * kv_count
    result = (count, heads, width) if place == count - 1 else (heads, width)
    operands = (
        slots,
        lengths,
        queries,
        keys.reshape(count, rows, width),
        values.reshape(count, rows, width),
        *carried,
    )
    return pl.pallas_call(
        functools.partial(
            suffix_kernel,
            place=place,
            carried=len(carried),
            kv_count=kv_count,
            score_scale=score_scale,
        ),
        in_specs=[IN_HBM] * len(operands) + [IN_VMEM] * len(earlier),
        out_specs=[IN_VMEM] * (2 + len(carried)),
        out_shape=[pltpu.VMEM(result, jnp.float32)] * 2
        + [pltpu.VMEM(array.shape, array.dtype) for array in carried],
        scratch_shapes=[
            pltpu.SMEM((count,), jnp.int32),
            pltpu.SMEM((count,), jnp.int32),
            pltpu.VMEM((count, heads, width), queries.dtype),
            pltpu.VMEM((rows, width), keys.dtype),
            pltpu.VMEM((rows, width), values.dtype),
            pltpu.VMEM((heads, rows), jnp.float32),
            pltpu.VMEM((heads, rows), jnp.bfloat16),
            pltpu.VMEM((heads, LANES), jnp.float32),
            pltpu.VMEM((heads, LANES), jnp.float32),
            pltpu.VMEM((heads, width), jnp.float32),
            pltpu.SemaphoreType.DMA((2, SUF_COPIES)),
            pltpu.SemaphoreType.DMA((3 + len(carried),)),
        ],
        compiler_params=pltpu.CompilerParams(vmem_limit_bytes=SUFFIX_VMEM),
        cost_estimate=pl.CostEstimate(
            flops=4 * heads * rows * width,
            bytes_accessed=4 * rows * width,
            transcendentals=heads * rows,
        ),
        name=f"suffix_attention_{place}",
    )(*map(in_hbm, operands), *earlier)


def exponent(size, least):
    return jnp.floor(jnp.log2(jnp.maximum(size, least))) + 1.0


def prefix_kernel(
    q_ref, k0_ref, v0_ref, k1_ref, v1_ref, _, out_hbm, out_ref, score_ref, weight_ref, sems, *, per_dest, turn, score_scale
):
    width = q_ref.shape[1]
    tiles = q_ref.shape[0] // ROW_TILE
    dests = ROW_TILE // per_dest
    keys, values = (k0_ref, k1_ref), (v0_ref, v1_ref)
    units = [(tile, block) for tile in range(tiles) for block in range(2)]
    places = out_hbm.shape[0] // dests
    first_place = turn + (0 if out_hbm.shape == out_ref.shape else pl.program_id(0) * tiles)
    copies = []
    lane = lax.broadcasted_iota(jnp.int32, (per_dest, width), 1)
    row = lax.broadcasted_iota(jnp.int32, (per_dest, width), 0)
    diagonal = lane == row

    length = k0_ref.shape[0]

    def score(unit, slot):
        tile, block = unit
        query = q_ref[tile * ROW_TILE : (tile + 1) * ROW_TILE]
        peak = None
        for at in range(0, length, PIECE):
            part = lax.dot_general(
                query, keys[block][at : at + PIECE], NT, preferred_element_type=jnp.float32
            )
            score_ref[slot, :, at : at + PIECE] = part
            for begin in range(0, PIECE, LANES):
                lanes = part[:, begin : begin + LANES]
                peak = lanes if peak is None else jnp.maximum(peak, lanes)
        return jnp.max(peak, axis=1, keepdims=True)

    held = []

    def finish(step, row_max, sums):
        tile, block = units[step]
        total = jnp.sum(sums, axis=1, keepdims=True)
        acc = jnp.dot(weight_ref[step % 2], values[block][...], preferred_element_type=jnp.float32)
        if block == 0:
            held.append((row_max, total, acc))
            return
        max0, total0, acc0 = held.pop()
        top = jnp.maximum(max0, row_max)
        weight0 = jnp.exp((max0 - top) * score_scale)
        weight1 = jnp.exp((row_max - top) * score_scale)
        joined = weight0 * total0 + weight1 * total
        mixed = (weight0 * acc0 + weight1 * acc) / joined
        logs = jnp.broadcast_to(top * score_scale + jnp.log(joined), (ROW_TILE, width))
        peak = jnp.max(jnp.abs(mixed), axis=1, keepdims=True)
        coded = jnp.round(mixed * jnp.exp2(VALUE_BITS - exponent(peak, PEAK_LEAST)))
        most = 2.0**VALUE_BITS - 1
        coded = jnp.clip(coded, -most, most).astype(jnp.int32)
        peaks = jnp.broadcast_to(peak, (ROW_TILE, width))
        half = per_dest // 2
        for k in range(dests):
            rows = slice(k * per_dest, (k + 1) * per_dest)
            dest = tile * dests + k
            high, low = coded[k * per_dest : k * per_dest + half], coded[k * per_dest + half : rows.stop]
            words = (high << 16) | (low & 0xFFFF)
            for j in range(half // TILE_ROWS):
                out_ref[dest, j] = words[j * TILE_ROWS : (j + 1) * TILE_ROWS]
            log_line = jnp.sum(jnp.where(diagonal, logs[rows], 0.0), axis=0, keepdims=True)
            peak_line = jnp.sum(jnp.where(diagonal, peaks[rows], 0.0), axis=0, keepdims=True)
            log_power = exponent(jnp.abs(log_line), LEAST)
            mantissa = jnp.round(log_line * jnp.exp2(LOG_BITS - log_power)).astype(jnp.int32)
            powers = log_power.astype(jnp.int32) << 16
            powers = powers | (exponent(peak_line, PEAK_LEAST).astype(jnp.int32) & 0xFFFF)
            out_ref[dest, half // TILE_ROWS] = jnp.concatenate([mantissa, powers], axis=0)
        ready = pl.ds(tile * dests, dests)
        copies.append(
            pltpu.make_async_copy(
                out_ref.at[ready],
                out_hbm.at[pl.ds(lax.rem(first_place + tile, places) * dests, dests)],
                sems.at[tile],
            )
        )
        copies[-1].start()
    later_max = score(units[0], 0)
    pending = None
    for step in range(len(units)):
        row_max, slot = later_max, step % 2
        if step + 1 < len(units):
            later_max = score(units[step + 1], (step + 1) % 2)
        if pending is not None:
            finish(*pending)
        sums = weigh(
            score_ref.at[slot], weight_ref.at[slot], slice(0, length), row_max, score_scale * LOG2E
        )
        pending = (step, row_max, sums)
    finish(*pending)
    for copy in copies:
        copy.wait()


def prefix_partials(
    rows_q, keys, values, far_keys, far_values, after, per_dest, turn, score_scale
):
    rows, width = rows_q.shape
    length = keys.shape[0]
    step_rows = min(STEP_ROWS, rows)
    dests = step_rows // per_dest
    out_piece = (per_dest // 2 // TILE_ROWS + 1, TILE_ROWS, width)
    blocked = {"in_specs": [IN_VMEM] * 5}
    if step_rows < rows:
        blocked["grid"] = (rows // step_rows,)
        blocked["in_specs"] = [pl.BlockSpec((step_rows, width), lambda i: (i, 0))]
        blocked["in_specs"] += [pl.BlockSpec((length, width), lambda i: (0, 0))] * 4
    blocked["in_specs"] += [pl.BlockSpec(memory_space=pl.ANY)]
    return pl.pallas_call(
        functools.partial(
            prefix_kernel, per_dest=per_dest, turn=turn, score_scale=score_scale
        ),
        **blocked,
        out_specs=IN_HBM,
        out_shape=pltpu.HBM((rows // per_dest, *out_piece), jnp.int32),
        scratch_shapes=[
            pltpu.VMEM((dests, *out_piece), jnp.int32),
            pltpu.VMEM((2, ROW_TILE, length), jnp.float32),
            pltpu.VMEM((2, ROW_TILE, length), jnp.bfloat16),
            pltpu.SemaphoreType.DMA((step_rows // ROW_TILE,)),
        ],
        compiler_params=pltpu.CompilerParams(vmem_limit_bytes=PREFIX_VMEM),
        cost_estimate=pl.CostEstimate(
            flops=8 * rows * length * width,
            bytes_accessed=8 * length * width + 6 * rows * width,
            transcendentals=2 * rows * length,
        ),
        name="prefix_attention",
    )(rows_q, keys, values, far_keys, far_values, after)


def join_kernel(got_ref, suf_ref, suf_log_ref, out_ref, log_ref, *, kv_count):
    count, heads, width = out_ref.shape
    group = heads // kv_count
    per_dest = count * group
    half = per_dest // 2
    parts = got_ref.shape[0] // kv_count
    lane = lax.broadcasted_iota(jnp.int32, (per_dest, width), 1)
    row = lax.broadcasted_iota(jnp.int32, (per_dest, width), 0)
    diagonal = lane == row

    def column(line):
        return jnp.sum(jnp.where(diagonal, line, 0.0), axis=1, keepdims=True)

    lines = [jnp.zeros((1, width), jnp.float32) for _ in range(count)]
    for place in range(kv_count):
        g = kv_count - 1 - place
        heads_of = slice(g * group, (g + 1) * group)
        suf_mixed = jnp.concatenate([suf_ref[r, heads_of] for r in range(count)], axis=0)
        suf_log = jnp.concatenate([suf_log_ref[r, heads_of] for r in range(count)], axis=0)
        logs, scales = [], []
        top = suf_log
        for s in range(parts):
            tail = got_ref[s * kv_count + place, half // TILE_ROWS]
            mantissa, powers = tail[0:1], tail[1:2]
            log_power = (powers >> 16).astype(jnp.float32)
            peak_power = ((powers << 16) >> 16).astype(jnp.float32)
            log_line = mantissa.astype(jnp.float32) * jnp.exp2(log_power - LOG_BITS)
            logs.append(jnp.broadcast_to(column(log_line), (per_dest, width)))
            scales.append(column(jnp.exp2(peak_power - VALUE_BITS)))
            top = jnp.maximum(top, logs[-1])
        weight = jnp.exp(suf_log - top)
        acc = weight * suf_mixed
        total = weight
        for s in range(parts):
            words = jnp.concatenate(
                [got_ref[s * kv_count + place, j] for j in range(half // TILE_ROWS)], axis=0
            )
            coded = jnp.concatenate([words >> 16, (words << 16) >> 16], axis=0)
            weight = jnp.exp(logs[s] - top)
            acc = acc + (weight * scales[s]) * coded.astype(jnp.float32)
            total = total + weight
        acc = acc / total
        logged = top + jnp.log(total)
        for r in range(count):
            rows = slice(r * group, (r + 1) * group)
            out_ref[r, heads_of] = acc[rows]
            spot = lane[:group] == row[:group] + g * group
            lines[r] = lines[r] + jnp.sum(jnp.where(spot, logged[rows], 0.0), axis=0, keepdims=True)
    for r in range(count):
        log_ref[r : r + 1] = lines[r][:, :heads]


def join_partials(got, suf_mixed, suf_log, kv_count):
    count, heads, width = suf_mixed.shape
    return pl.pallas_call(
        functools.partial(join_kernel, kv_count=kv_count),
        in_specs=[IN_VMEM] * 3,
        out_specs=[IN_VMEM] * 2,
        out_shape=[
            jax.ShapeDtypeStruct((count, heads, width), jnp.float32),
            jax.ShapeDtypeStruct((count, heads), jnp.float32),
        ],
        compiler_params=pltpu.CompilerParams(vmem_limit_bytes=SMALL_VMEM),
        name="join_partials",
    )(got, suf_mixed, suf_log)


def exchange(pieces, first):
    seq, head, rep = lax.axis_size("seq"), lax.axis_size("head"), lax.axis_size("rep")
    order = [(first - s) % seq for s in range(seq)]
    groups = [
        [(s * head + h) * rep + r for s in order for h in reversed(range(head))]
        for r in range(rep)
    ]
    return lax.all_to_all(
        pieces,
        ("seq", "head", "rep"),
        split_axis=0,
        concat_axis=0,
        axis_index_groups=groups,
        tiled=True,
    )


def per_device(
    queries, prefix_keys, prefix_values, suffix_keys, suffix_values, suffix_lengths, slot_map
):
    count, heads, width = queries.shape
    kv_count = suffix_keys.shape[2]
    per_dest = count * heads // kv_count
    score_scale = 1.0 / math.sqrt(width)
    sent = layout_queries(queries, kv_count, lax.axis_size("seq"))
    seq = lax.axis_size("seq")
    out_first, back_first = (seq - 1) // 2, seq // 2
    got_q = exchange(sent, out_first)
    keys = prefix_keys[:, 0, :]
    values = prefix_values[:, 0, :]
    far_keys = lax.ppermute(keys, "rep", [(0, 1), (1, 0)])
    far_values = lax.ppermute(values, "rep", [(0, 1), (1, 0)])
    earlier = []
    for place in range(count):
        mixed, log, *brought = suffix_partials(
            place,
            queries,
            suffix_keys,
            suffix_values,
            suffix_lengths,
            slot_map,
            (keys, values) if place == 0 else (),
            earlier if place == count - 1 else (),
            score_scale,
        )
        earlier += [mixed, log]
        if brought:
            near_keys, near_values = brought
    partials = prefix_partials(
        got_q.reshape(-1, width),
        near_keys,
        near_values,
        far_keys,
        far_values,
        earlier[0],
        per_dest,
        (back_first - out_first) % seq,
        score_scale,
    )
    got = exchange(partials, back_first)
    return join_partials(got, mixed, log, kv_count)


def solution(mesh):
    by_request = P(("seq", "head", "rep"))
    by_block = P(("seq", "rep"), "head", None)
    placed = (by_request, by_block, by_block, by_request, by_request, by_request, by_request)
    return jax.shard_map(
        per_device,
        mesh=mesh,
        in_specs=placed,
        out_specs=(by_request, by_request),
        check_vma=False,
    )
```
